32 devices in a mesh: seq: 16 (over z, y, core), tp: 2 (over x).
Axes of the slice: x: 2, y: 2, z: 4, core: 2. Of those that a mesh axis runs over, the one named last changes fastest.
Arguments:
- frames_in: bfloat16 [1536, 8192], P('tp', 'seq'), may hold values from -30 to 30
- norm_gain: float32 [1536], P('tp'), may hold values from 0.5 to 2
- value_weight: bfloat16 [1536, 1536], P('tp'), may hold values from -0.15625 to 0.15625
- gate_weight: bfloat16 [1536, 1536], P('tp'), may hold values from -0.15625 to 0.15625
- depth_kernel: float32 [1536, 32], P('tp'), may hold values from -6 to 6
- conv_gain: float32 [1536], P('tp'), may hold values from 0.5 to 2
- out_weight: bfloat16 [1536, 1536], P('tp'), may hold values from -0.15625 to 0.15625
- cotangent: bfloat16 [1536, 8192], P('tp', 'seq'), may hold values from -15 to 15
Outputs:
- block_out: bfloat16 [1536, 8192], P('tp', 'seq')
- input_grad: bfloat16 [1536, 8192], P('tp', 'seq')
- grad_norm_gain: float32 [1536], P('tp')
- grad_value: bfloat16 [1536, 1536], P('tp')
- grad_gate: bfloat16 [1536, 1536], P('tp')
- grad_kernel: float32 [1536, 32], P('tp')
- grad_conv_gain: float32 [1536], P('tp')
- grad_out: bfloat16 [1536, 1536], P('tp')
The draws below stay inside these ranges and needn't reach their ends.
All inputs are finite; a program needn't handle non-finite values.
Results may differ from the reference program's by a relative error of at most 0.027.
Values may be sent and summed in bfloat16 or wider, within the bound.
No kernel may reach another device: no remote copies, remote signals or barrier semaphores. Data moves between devices by JAX's collectives and lax.ppermute only.
A program may use at most 64 MiB of HBM per device.

```python
import math
import jax
import jax.numpy as jnp
from jax import lax

D = 1536
KERNEL = 32
FRAMES = 8192
N_TP = 2


def spread_draw(key, rows, cols, base):
    k_noise, k_rows, k_cols = jax.random.split(key, 3)
    place = jnp.arange(cols, dtype=jnp.float32) / max(cols - 1, 1)
    row_scale = jnp.exp(jax.random.uniform(k_rows, (rows, 1), jnp.float32, jnp.log(0.3), jnp.log(3.0)))
    jitter = jnp.exp(jax.random.uniform(k_cols, (1, cols), jnp.float32, -0.35, 0.35))
    ramp = jnp.exp(jnp.log(3.0) * (place - 0.5))
    noise = jnp.clip(jax.random.normal(k_noise, (rows, cols), jnp.float32), -4.0, 4.0)
    return base * noise * row_scale * ramp[None, :] * jitter


def draw_frames_in(key, part):
    return spread_draw(jax.random.fold_in(key, 11), FRAMES, D, 1.0).T.astype(jnp.bfloat16)


def draw_depth_kernel(key, part):
    return spread_draw(jax.random.fold_in(key, 12), KERNEL, D, KERNEL ** (-0.5)).T.astype(jnp.float32)


def draw_cotangent(key, part):
    return spread_draw(jax.random.fold_in(key, 13), FRAMES, D, 0.5).T.astype(jnp.bfloat16)


def block_scale(stream_key, shape, shards, least, top_value):
    loudness, own = 1.0, jax.random.fold_in(stream_key, 6)
    for position, parts in shards:
        heights = jnp.exp(jax.random.uniform(jax.random.fold_in(own, position), (parts,), jnp.float32, least / len(shards), top_value / len(shards)))
        loudness = loudness * jnp.repeat(heights, shape[position] // parts).reshape([-1 if axis == position else 1 for axis in range(len(shape))])
    return loudness


def scatter_about(own_key, dims, scale, bound, shards=(), kind=jnp.bfloat16):
    factor_of = block_scale(own_key, dims, shards, -0.22, 0.18) if shards else 1.0
    values = jax.random.normal(own_key, dims, jnp.float32) * scale * factor_of
    return jnp.minimum(jnp.maximum(values, -bound), bound).astype(kind)


def setup_inputs(seed: int = 0) -> dict:
    keys = jax.random.split(jax.random.key(seed), 9)
    frames_in = draw_frames_in(jax.random.fold_in(keys[8], 71), 0)
    norm_gain = jnp.clip(jnp.exp(math.log(2.0) - 1.3862944 * jax.random.uniform(keys[1], (D,), jnp.float32) ** block_scale(keys[1], (D,), ((0, 2),), -0.2, 0.2)), 0.5, 2.0)
    value_weight = scatter_about(keys[2], (D, D), D ** -0.5, 0.15625, ((0, 2),))
    gate_weight = scatter_about(keys[3], (D, D), D ** -0.5, 0.15625, ((0, 2),))
    depth_kernel = draw_depth_kernel(jax.random.fold_in(keys[8], 71), 0)
    conv_gain = jnp.clip(jnp.exp(math.log(2.0) - 1.3862944 * jax.random.uniform(keys[5], (D,), jnp.float32) ** block_scale(keys[5], (D,), ((0, 2),), -0.2, 0.2)), 0.5, 2.0)
    out_weight = scatter_about(keys[6], (D, D), D ** -0.5, 0.15625, ((0, 2),))
    cotangent = draw_cotangent(jax.random.fold_in(keys[8], 71), 0)
    return {"frames_in": frames_in, "norm_gain": norm_gain, "value_weight": value_weight, "gate_weight": gate_weight, "depth_kernel": depth_kernel, "conv_gain": conv_gain, "out_weight": out_weight, "cotangent": cotangent}


EPS = 1e-05

def widen(values):
    return lax.optimization_barrier(values).astype(jnp.float32)

def norm_parts(values):
    mean = lax.optimization_barrier(jnp.mean(values, axis=0, keepdims=True))
    centred = values - mean
    spread = lax.optimization_barrier(jnp.mean(centred * centred, axis=0, keepdims=True))
    inverse = lax.rsqrt(spread + EPS)
    return (centred * inverse, inverse)

def norm_back(d_hat, hat, inverse):
    first = lax.optimization_barrier(jnp.mean(d_hat, axis=0, keepdims=True))
    second = lax.optimization_barrier(jnp.mean(d_hat * hat, axis=0, keepdims=True))
    return (d_hat - first - hat * second) * inverse

def block_sum(pairs, frames):
    block = D // N_TP
    total = jnp.zeros((D, frames), jnp.float32)
    for index in range(N_TP):
        low = index * block
        term = jnp.zeros((D, frames), jnp.float32)
        for values, weight in pairs:
            term = term + jnp.dot(weight[low:low + block].T, values[low:low + block], preferred_element_type=jnp.float32)
        total = total + widen(term.astype(jnp.bfloat16))
    return total

def reference(frames_in, norm_gain, value_weight, gate_weight, depth_kernel, conv_gain, out_weight, cotangent):
    frames = frames_in.shape[1]
    reach = KERNEL // 2
    scale = jnp.float32(FRAMES) ** (-0.5)
    inputs = frames_in.astype(jnp.float32)
    hat_in, inverse_in = norm_parts(inputs)
    normed = (hat_in * norm_gain[:, None]).astype(jnp.bfloat16)
    value = jnp.dot(value_weight, normed, preferred_element_type=jnp.float32)
    gate = jnp.dot(gate_weight, normed, preferred_element_type=jnp.float32)
    gate_sig = jax.nn.sigmoid(gate)
    glu = (value * gate_sig).astype(jnp.bfloat16)
    glu_wide = jnp.pad(widen(glu), ((0, 0), (reach, reach)))
    conv = jnp.zeros((D, frames), jnp.float32)
    for tap in range(KERNEL):
        conv = conv + depth_kernel[:, tap:tap + 1] * glu_wide[:, tap:tap + frames]
    hat_conv, inverse_conv = norm_parts(conv)
    scaled = hat_conv * conv_gain[:, None]
    swish_sig = jax.nn.sigmoid(scaled)
    act = (scaled * swish_sig).astype(jnp.bfloat16)
    block_out = (inputs + jnp.dot(out_weight, act, preferred_element_type=jnp.float32)).astype(jnp.bfloat16)
    grad_out = (jnp.dot(cotangent, act.T, preferred_element_type=jnp.float32) * scale).astype(jnp.bfloat16)
    d_act = block_sum(((cotangent, out_weight),), frames)
    d_scaled = d_act * (swish_sig + scaled * swish_sig * (1.0 - swish_sig))
    grad_conv_gain = lax.optimization_barrier(jnp.sum(d_scaled * hat_conv, axis=1)) * scale
    d_conv = norm_back(d_scaled * conv_gain[:, None], hat_conv, inverse_conv).astype(jnp.bfloat16)
    d_conv_f = widen(d_conv)
    d_conv_wide = jnp.pad(d_conv_f, ((0, 0), (reach, reach)))
    d_glu = jnp.zeros((D, frames), jnp.float32)
    kernel_cols = []
    for tap in range(KERNEL):
        start = 2 * reach - tap
        d_glu = d_glu + depth_kernel[:, tap:tap + 1] * d_conv_wide[:, start:start + frames]
        kernel_cols.append(lax.optimization_barrier(jnp.sum(glu_wide[:, tap:tap + frames] * d_conv_f, axis=1)))
    grad_kernel = jnp.stack(kernel_cols, axis=1) * scale
    d_value = (d_glu * gate_sig).astype(jnp.bfloat16)
    d_gate = (d_glu * value * gate_sig * (1.0 - gate_sig)).astype(jnp.bfloat16)
    grad_value = (jnp.dot(d_value, normed.T, preferred_element_type=jnp.float32) * scale).astype(jnp.bfloat16)
    grad_gate = (jnp.dot(d_gate, normed.T, preferred_element_type=jnp.float32) * scale).astype(jnp.bfloat16)
    d_normed = block_sum(((d_value, value_weight), (d_gate, gate_weight)), frames)
    grad_norm_gain = lax.optimization_barrier(jnp.sum(d_normed * hat_in, axis=1)) * scale
    input_grad = (cotangent.astype(jnp.float32) + norm_back(d_normed * norm_gain[:, None], hat_in, inverse_in)).astype(jnp.bfloat16)
    return (block_out, input_grad, grad_norm_gain, grad_value, grad_gate, grad_kernel, grad_conv_gain, grad_out)
```

```python
import jax
import jax.numpy as jnp
from jax import lax
from jax.sharding import PartitionSpec as P

EPS = 1e-05
F32 = jnp.float32
BF16 = jnp.bfloat16


def ring_of(count):
    chips = count // 2
    if chips % 2 == 0:
        cols = chips // 2
        order = [2 * col for col in range(cols)] + [2 * col + 1 for col in reversed(range(cols))]
    else:
        order = list(range(chips))
    place = [0] * count
    ahead, behind = [], []
    for spot, chip in enumerate(order):
        after = order[(spot + 1) % chips]
        for core in range(2):
            place[2 * chip + core] = spot
            ahead.append((2 * chip + core, 2 * after + core))
            behind.append((2 * after + core, 2 * chip + core))
    return chips, place, ahead, behind


def pairs_of(count, step):
    return [(i, i ^ step) for i in range(count)]


def add(left, right):
    return (left.astype(F32) + right.astype(F32)).astype(BF16)


def ring_sum(sets):
    count = lax.axis_size("seq")
    chips, place, ahead, behind = ring_of(count)
    spot = jnp.asarray(place, jnp.int32)[lax.axis_index("seq")]
    reach = chips // 2

    def part(cells, step):
        return lax.dynamic_index_in_dim(cells, (spot + step + chips) % chips, 0, keepdims=False)

    def up(cells):
        return lax.ppermute(cells, "seq", ahead)

    def down(cells):
        return lax.ppermute(cells, "seq", behind)

    half = sets[0].shape[1] // 2
    flows = [(up(part(x, reach)[half:]), down(part(x, -reach)[:half])) for x in sets]
    for hop in range(reach - 1, 0, -1):
        later = []
        for x, (u, d) in zip(sets, flows):
            own_u, own_d = part(x, hop), part(x, -hop)
            if hop == reach - 1:
                u = jnp.concatenate([own_u[:half], add(own_u[half:], u)])
                d = jnp.concatenate([add(own_d[:half], d), own_d[half:]])
            else:
                u, d = add(own_u, u), add(own_d, d)
            later.append((up(u), down(d)))
        flows = later
    owns = [
        (part(x, 0).astype(F32) + u.astype(F32) + d.astype(F32)).astype(BF16)
        for x, (u, d) in zip(sets, flows)
    ]
    outs = []
    for x, own in zip(sets, owns):
        outs.append(lax.dynamic_update_index_in_dim(jnp.zeros_like(x), own, spot, 0))
    flows = [(own, own) for own in owns]
    for hop in range(1, reach):
        flows = [(up(u), down(d)) for u, d in flows]
        for i, (u, d) in enumerate(flows):
            out = lax.dynamic_update_index_in_dim(outs[i], u, (spot - hop + chips) % chips, 0)
            outs[i] = lax.dynamic_update_index_in_dim(out, d, (spot + hop) % chips, 0)
    for i, (u, d) in enumerate(flows):
        far = jnp.concatenate([down(d[:half]), up(u[half:])])
        outs[i] = lax.dynamic_update_index_in_dim(outs[i], far, (spot + reach) % chips, 0)
    return outs


def weight_sums(grads):
    count = lax.axis_size("seq")
    rows, cols = grads[0].shape
    chips = count // 2
    if count % 4 or rows % (2 * chips) or rows // (2 * chips) < 2:
        return [lax.psum(g.astype(BF16), "seq") for g in grads]
    core = lax.axis_index("seq") % 2
    swap = pairs_of(count, 1)
    half = rows // 2
    sets = []
    for g in grads:
        g = g.astype(BF16)
        theirs = lax.dynamic_slice_in_dim(g, (1 - core) * half, half, 0)
        mine = lax.dynamic_slice_in_dim(g, core * half, half, 0)
        mine = add(mine, lax.ppermute(theirs, "seq", swap))
        sets.append(mine.reshape(chips, half // chips, cols))
    outs = []
    for mine in ring_sum(sets):
        mine = mine.reshape(half, cols)
        theirs = lax.ppermute(mine, "seq", swap)
        outs.append(
            jnp.where(
                core == 0,
                jnp.concatenate([mine, theirs]),
                jnp.concatenate([theirs, mine]),
            )
        )
    return outs


def small_sum(values):
    count = lax.axis_size("seq")
    if count & (count - 1):
        return lax.psum(values, "seq")
    step = 1
    while step < count:
        values = values + lax.ppermute(values, "seq", pairs_of(count, step))
        step *= 2
    return values


def other(values):
    return lax.ppermute(values, "tp", [(0, 1), (1, 0)])


def tp_sum(values):
    if lax.axis_size("tp") == 2:
        return values + other(values)
    return lax.psum(values, "tp")


def tp_gather(values):
    if lax.axis_size("tp") == 2:
        theirs = other(values)
        first = lax.axis_index("tp") == 0
        return jnp.where(
            first, jnp.concatenate([values, theirs]), jnp.concatenate([theirs, values])
        )
    return lax.all_gather(values, "tp", axis=0, tiled=True)


def tp_scatter(term):
    term = term.astype(BF16)
    if lax.axis_size("tp") == 2:
        rows = term.shape[0] // 2
        me = lax.axis_index("tp")
        theirs = lax.dynamic_slice_in_dim(term, (1 - me) * rows, rows, 0)
        mine = lax.dynamic_slice_in_dim(term, me * rows, rows, 0)
        return mine.astype(F32) + other(theirs).astype(F32)
    return lax.psum_scatter(term, "tp", scatter_dimension=0, tiled=True).astype(F32)


def halo(cells, reach):
    count = lax.axis_size("seq")
    size = cells.shape[1]
    right = [(i, i + 1) for i in range(count - 1)]
    left = [(i + 1, i) for i in range(count - 1)]
    before = lax.ppermute(cells[:, size - reach :], "seq", right)
    after = lax.ppermute(cells[:, :reach], "seq", left)
    return jnp.concatenate([before, cells, after], axis=1)


def norm_back(d_hat, hat, inverse, width):
    sums = jnp.concatenate(
        [jnp.sum(d_hat, axis=0, keepdims=True), jnp.sum(d_hat * hat, axis=0, keepdims=True)]
    )
    sums = tp_sum(sums) / width
    return (d_hat - sums[:1] - hat * sums[1:]) * inverse


def contract_rows(left, right):
    return lax.dot_general(left, right, (((0,), (0,)), ((), ())), preferred_element_type=F32)


def contract_cols(left, right):
    return lax.dot_general(left, right, (((1,), (1,)), ((), ())), preferred_element_type=F32)


def local(
    frames_in, norm_gain, value_weight, gate_weight, depth_kernel, conv_gain, out_weight, cotangent
):
    chans, row_count = frames_in.shape
    parts = lax.axis_size("tp")
    me = lax.axis_index("tp")
    width = chans * parts
    taps = depth_kernel.shape[1]
    reach = taps // 2
    scale = float(row_count * lax.axis_size("seq")) ** (-0.5)

    frames_all = tp_gather(frames_in)
    gain_all = lax.all_gather(norm_gain, "tp", axis=0, tiled=True)
    d_act = tp_scatter(contract_rows(out_weight, cotangent))

    wide = frames_all.astype(F32)
    centred = wide - jnp.mean(wide, axis=0, keepdims=True)
    inverse_in = lax.rsqrt(jnp.mean(centred * centred, axis=0, keepdims=True) + EPS)
    hat_all = centred * inverse_in
    normed_all = (hat_all * gain_all[:, None]).astype(BF16)
    value = jnp.dot(value_weight, normed_all, preferred_element_type=F32)
    gate = jnp.dot(gate_weight, normed_all, preferred_element_type=F32)
    gate_sig = jax.nn.sigmoid(gate)
    glu = (value * gate_sig).astype(BF16)
    glu_wide = halo(glu, reach).astype(F32)
    conv = jnp.zeros((chans, row_count), F32)
    for tap in range(taps):
        conv = conv + depth_kernel[:, tap : tap + 1] * glu_wide[:, tap : tap + row_count]

    mean = jnp.mean(conv, axis=0, keepdims=True)
    spread = jnp.sum((conv - mean) ** 2, axis=0, keepdims=True)
    if parts == 2:
        there = other(jnp.concatenate([mean, spread]))
        gap = mean - there[:1]
        mean = (mean + there[:1]) * 0.5
        spread = (spread + there[1:] + gap * gap * (chans * 0.5)) / width
    else:
        whole = lax.pmean(mean, "tp")
        spread = lax.psum(spread + chans * (mean - whole) ** 2, "tp") / width
        mean = whole
    inverse_conv = lax.rsqrt(spread + EPS)
    hat_conv = (conv - mean) * inverse_conv
    scaled = hat_conv * conv_gain[:, None]
    swish_sig = jax.nn.sigmoid(scaled)
    act = (scaled * swish_sig).astype(BF16)
    act_all = tp_gather(act)
    block_out = (
        frames_in.astype(F32) + jnp.dot(out_weight, act_all, preferred_element_type=F32)
    ).astype(BF16)
    grad_out = contract_cols(cotangent, act_all) * scale

    d_scaled = d_act * (swish_sig + scaled * swish_sig * (1.0 - swish_sig))
    grad_conv_gain = jnp.sum(d_scaled * hat_conv, axis=1) * scale
    d_conv = norm_back(d_scaled * conv_gain[:, None], hat_conv, inverse_conv, width).astype(BF16)
    d_conv_f = d_conv.astype(F32)
    d_conv_wide = halo(d_conv, reach).astype(F32)
    d_glu = jnp.zeros((chans, row_count), F32)
    kernel_cols = []
    for tap in range(taps):
        start = 2 * reach - tap
        d_glu = d_glu + depth_kernel[:, tap : tap + 1] * d_conv_wide[:, start : start + row_count]
        kernel_cols.append(jnp.sum(glu_wide[:, tap : tap + row_count] * d_conv_f, axis=1))
    grad_kernel = jnp.stack(kernel_cols, axis=0) * scale
    d_value = (d_glu * gate_sig).astype(BF16)
    d_gate = (d_glu * value * gate_sig * (1.0 - gate_sig)).astype(BF16)
    grad_value = contract_cols(d_value, normed_all) * scale
    grad_gate = contract_cols(d_gate, normed_all) * scale
    d_normed = tp_scatter(
        contract_rows(value_weight, d_value) + contract_rows(gate_weight, d_gate)
    )
    hat_in = lax.dynamic_slice_in_dim(hat_all, me * chans, chans, 0)
    grad_norm_gain = jnp.sum(d_normed * hat_in, axis=1) * scale
    input_grad = (
        cotangent.astype(F32) + norm_back(d_normed * norm_gain[:, None], hat_in, inverse_in, width)
    ).astype(BF16)
    small = small_sum(
        jnp.concatenate([grad_kernel, grad_conv_gain[None], grad_norm_gain[None]], axis=0)
    )
    grad_out, grad_value, grad_gate = weight_sums([grad_out, grad_value, grad_gate])
    return (
        block_out,
        input_grad,
        small[taps + 1],
        grad_value,
        grad_gate,
        small[:taps].T,
        small[taps],
        grad_out,
    )


def solution(mesh):
    return jax.shard_map(
        local,
        mesh=mesh,
        in_specs=(
            P("tp", "seq"),
            P("tp"),
            P("tp", None),
            P("tp", None),
            P("tp", None),
            P("tp"),
            P("tp", None),
            P("tp", "seq"),
        ),
        out_specs=(
            P("tp", "seq"),
            P("tp", "seq"),
            P("tp"),
            P("tp", None),
            P("tp", None),
            P("tp", None),
            P("tp"),
            P("tp", None),
        ),
        check_vma=False,
    )
```

```python
import functools

import jax
import jax.numpy as jnp
from jax import lax
from jax.experimental import pallas as pl
from jax.experimental.pallas import tpu as pltpu
from jax.sharding import PartitionSpec as P

EPS = 1e-05
F32 = jnp.float32
BF16 = jnp.bfloat16
LANES = 128


def dot(left, right, contract):
    return lax.dot_general(left, right, (contract, ((), ())), preferred_element_type=F32)


NT = ((1,), (1,))
NN = ((1,), (0,))
TN = ((0,), (0,))


def call(body, name, places, grid, ins, outs, args, scratch=(), flops=0):
    size = sum(a.size * a.dtype.itemsize for a in args)
    size += sum(s.size * s.dtype.itemsize for s, _ in outs)
    return pl.pallas_call(
        body,
        out_shape=[s for s, _ in outs],
        grid_spec=pltpu.PrefetchScalarGridSpec(
            num_scalar_prefetch=1,
            grid=grid,
            in_specs=ins,
            out_specs=[b for _, b in outs],
            scratch_shapes=list(scratch),
        ),
        compiler_params=pltpu.CompilerParams(vmem_limit_bytes=48 * 2**20),
        cost_estimate=pl.CostEstimate(flops=flops, bytes_accessed=size, transcendentals=0),
        name=name,
    )(places, *args)


def shape(dims, kind):
    return jax.ShapeDtypeStruct(dims, kind)


def whole(dims):
    return pl.BlockSpec(dims, lambda i, p: (0,) * len(dims))


def lanes(rows, width):
    return pl.BlockSpec((rows, width), lambda i, p: (0, i))


def rows_of(height, cols):
    return pl.BlockSpec((height, cols), lambda i, p: (i, 0))


def d_act_terms(places, cotangent, weight):
    chans, frames = cotangent.shape

    def body(p, cot, w, theirs, mine, turned):
        @pl.when(pl.program_id(0) == 0)
        def _():
            turned[...] = cot[...].T
            theirs[...] = dot(turned[...], w[...], NN).astype(BF16)

        @pl.when(pl.program_id(0) == 1)
        def _():
            mine[...] = dot(turned[...], w[...], NN).astype(BF16)

    out = (shape((frames, chans), BF16), whole((frames, chans)))
    return call(
        body,
        "d_act_terms",
        places,
        (2,),
        [
            whole((chans, frames)),
            pl.BlockSpec((chans, chans), lambda i, p: (0, jnp.where(i == 0, 1 - p[0], p[0]))),
        ],
        [out, out],
        [cotangent, weight],
        [pltpu.VMEM((frames, chans), BF16)],
        4 * chans * chans * frames,
    )


def glu_forward(places, mine, theirs, gain_mine, gain_theirs, value_weight, gate_weight):
    chans, frames = mine.shape
    width = 2 * chans
    step = 256

    def body(p, xm, xt, gm, gt, wv, wg, normed, hat, inv, glu, sig, slope, edge):
        @pl.when(pl.program_id(0) == 0)
        def _():
            low = pl.multiple_of(p[0] * chans, LANES)
            high = pl.multiple_of((1 - p[0]) * chans, LANES)
            for at in range(0, frames, LANES):
                some = pl.ds(at, LANES)
                a = xm[:, some].T.astype(F32)
                b = xt[:, some].T.astype(F32)
                total = jnp.sum(a, axis=1, keepdims=True) + jnp.sum(b, axis=1, keepdims=True)
                mean = total / width
                a = a - mean
                b = b - mean
                spread = jnp.sum(a * a, axis=1, keepdims=True)
                spread = spread + jnp.sum(b * b, axis=1, keepdims=True)
                scale = lax.rsqrt(spread / width + EPS)
                a = a * scale
                b = b * scale
                hat[some, :] = a
                inv[some, :] = jnp.broadcast_to(scale, (LANES, LANES))
                normed[some, pl.ds(low, chans)] = (a * gm[...]).astype(BF16)
                normed[some, pl.ds(high, chans)] = (b * gt[...]).astype(BF16)

        value = dot(normed[...], wv[...], NT)
        gate = dot(normed[...], wg[...], NT)
        s = jax.nn.sigmoid(gate)
        g = (value * s).astype(BF16)
        glu[...] = g
        edge[0] = g[:16]
        edge[1] = g[frames - 16 :]
        sig[...] = s
        slope[...] = value * s * (1.0 - s)

    block = lanes(frames, step)
    return call(
        body,
        "glu_forward",
        places,
        (chans // step,),
        [whole((chans, frames))] * 2
        + [whole((1, chans))] * 2
        + [rows_of(step, width)] * 2,
        [
            (shape((frames, width), BF16), whole((frames, width))),
            (shape((frames, chans), F32), whole((frames, chans))),
            (shape((frames, LANES), F32), whole((frames, LANES))),
            (shape((frames, chans), BF16), block),
            (shape((frames, chans), F32), block),
            (shape((frames, chans), F32), block),
            (shape((2, 16, chans), BF16), pl.BlockSpec((2, 16, step), lambda i, p: (0, 0, i))),
        ],
        [mine, theirs, gain_mine, gain_theirs, value_weight, gate_weight],
        (),
        4 * chans * width * frames,
    )


def fill(wide, before, own, after):
    frames = own.shape[0]
    wide[:16, :] = before[...].astype(F32)
    wide[16 : 16 + frames, :] = own[...].astype(F32)
    wide[16 + frames :, :] = after[...].astype(F32)


def to_rows(first, second):
    size = first.shape[0]
    lane = lax.broadcasted_iota(jnp.int32, (size, LANES), 1)
    both = jnp.where(lane == 0, first, jnp.where(lane == 1, second, 0.0))
    return both.T[:8]


def to_cols(rows):
    turned = jnp.concatenate([rows] * (LANES // 8)).T
    return turned[:, 0:1], turned[:, 1:2]


STEP = 64


def conv_forward(places, before, glu, after, taps):
    frames, chans = glu.shape
    blocks = chans // LANES

    def body(p, b, g, a, w, conv, stats, wide):
        at = pl.program_id(0)
        fill(wide, b, g, a)

        def chunk(i, carry):
            start = pl.multiple_of(i * STEP, STEP)
            total = jnp.zeros((STEP, LANES), F32)
            for r in range(8):
                x = wide[pl.ds(start + r, STEP + 24), :]
                for q in range(4):
                    tap = 8 * q + r
                    total = total + w[tap : tap + 1, :] * x[8 * q : 8 * q + STEP]
            conv[pl.ds(start, STEP), pl.ds(pl.multiple_of(at * LANES, LANES), LANES)] = total
            return carry

        lax.fori_loop(0, frames // STEP, chunk, 0)

        @pl.when(at == blocks - 1)
        def _():
            for low in range(0, frames, LANES):
                x = conv[low : low + LANES, :]
                mean = jnp.sum(x, axis=1, keepdims=True) / chans
                x = x - mean
                stats[:, low : low + LANES] = to_rows(mean, jnp.sum(x * x, axis=1, keepdims=True))

    return call(
        body,
        "conv_forward",
        places,
        (blocks,),
        [lanes(16, LANES), lanes(frames, LANES), lanes(16, LANES), lanes(32, LANES)],
        [
            (shape((frames, chans), F32), whole((frames, chans))),
            (shape((8, frames), F32), whole((8, frames))),
        ],
        [before, glu, after, taps],
        [pltpu.VMEM((frames + 32, LANES), F32)],
        64 * frames * chans,
    )


def merge(mine, theirs, chans):
    mean, spread = to_cols(mine)
    there, more = to_cols(theirs)
    gap = mean - there
    whole_spread = spread + more + gap * gap * (chans * 0.5)
    return (mean + there) * 0.5, lax.rsqrt(whole_spread / (2 * chans) + EPS)


def act_step(places, conv, mine, theirs, term, recv, gain):
    frames, chans = conv.shape
    height = LANES

    def body(p, x, sm, st, tm, tr, g, act, hat, e, sums, gain_grad):
        mean, inverse = merge(sm[...], st[...], chans)
        h = (x[...] - mean) * inverse
        hat[...] = h
        scaled = h * g[...]
        s = jax.nn.sigmoid(scaled)
        soft = scaled * s
        act[...] = soft.astype(BF16)
        d = tm[...].astype(F32) + tr[...].astype(F32)
        d = d * (s + soft * (1.0 - s))

        @pl.when(pl.program_id(0) == 0)
        def _():
            gain_grad[...] = jnp.zeros_like(gain_grad)

        gain_grad[...] += jnp.sum(d * h, axis=0, keepdims=True)
        d = d * g[...]
        e[...] = d
        sums[...] = to_rows(
            jnp.sum(d, axis=1, keepdims=True), jnp.sum(d * h, axis=1, keepdims=True)
        )

    some = rows_of(height, chans)
    line = lanes(8, height)
    return call(
        body,
        "act_step",
        places,
        (frames // height,),
        [some, line, line, some, some, whole((1, chans))],
        [
            (shape((frames, chans), BF16), some),
            (shape((frames, chans), F32), some),
            (shape((frames, chans), F32), some),
            (shape((8, frames), F32), line),
            (shape((1, chans), F32), whole((1, chans))),
        ],
        [conv, mine, theirs, term, recv, gain],
        (),
        30 * frames * chans,
    )


def d_conv_step(places, e, hat, mine, theirs, sums_mine, sums_theirs):
    frames, chans = e.shape
    height = LANES
    steps = frames // height

    def body(p, d, h, sm, st, um, ut, out, head, tail):
        _, inverse = merge(sm[...], st[...], chans)
        first, second = to_cols(um[...] + ut[...])
        width = 2 * chans
        got = (d[...] - first / width - h[...] * (second / width)) * inverse
        got = got.astype(BF16)
        out[...] = got

        @pl.when(pl.program_id(0) == 0)
        def _():
            head[...] = got[:16]

        @pl.when(pl.program_id(0) == steps - 1)
        def _():
            tail[...] = got[height - 16 :]

    some = rows_of(height, chans)
    line = lanes(8, height)
    rim = (shape((16, chans), BF16), whole((16, chans)))
    return call(
        body,
        "d_conv_step",
        places,
        (steps,),
        [some, some, line, line, line, line],
        [(shape((frames, chans), BF16), some), rim, rim],
        [e, hat, mine, theirs, sums_mine, sums_theirs],
        (),
        10 * frames * chans,
    )


def d_glu_step(places, before, d_conv, after, taps, sig, slope, own):
    frames, chans = d_conv.shape
    blocks = chans // LANES // 2

    def body(p, b, d, a, w, s, h, d_value, d_gate, wide):
        fill(wide, b, d, a)

        def chunk(i, carry):
            start = pl.multiple_of(i * STEP, STEP)
            total = jnp.zeros((STEP, LANES), F32)
            for r in range(8):
                x = wide[pl.ds(start + r + 1, STEP + 24), :]
                for q in range(4):
                    tap = 31 - (8 * q + r)
                    total = total + w[tap : tap + 1, :] * x[8 * q : 8 * q + STEP]
            some = pl.ds(start, STEP)
            d_value[some, :] = (total * s[some, :]).astype(BF16)
            d_gate[some, :] = (total * h[some, :]).astype(BF16)
            return carry

        lax.fori_loop(0, frames // STEP, chunk, 0)

    def pick(height):
        if own:
            return pl.BlockSpec((height, LANES), lambda i, p: (0, i + blocks * p[1]))
        return pl.BlockSpec((height, LANES), lambda i, p: (0, i + blocks * (1 - p[1])))

    out = (shape((frames, chans // 2), BF16), lanes(frames, LANES))
    return call(
        body,
        "d_glu_own" if own else "d_glu_other",
        places,
        (blocks,),
        [pick(16), pick(frames), pick(16), pick(32), pick(frames), pick(frames)],
        [out, out],
        [before, d_conv, after, taps, sig, slope],
        [pltpu.VMEM((frames + 32, LANES), F32)],
        32 * frames * chans,
    )


def taps_grad(places, before, glu, after, d_conv, scale):
    frames, chans = glu.shape
    part = 32

    def body(p, b, g, a, d, out, wide, sums):
        fill(wide, b, g, a)
        sums[...] = jnp.zeros_like(sums)

        def chunk(i, carry):
            start = pl.multiple_of(i * part, part)
            mine = d[pl.ds(start, part), :].astype(F32)
            for r in range(8):
                x = wide[pl.ds(start + r, part + 24), :]
                for q in range(4):
                    both = mine * x[8 * q : 8 * q + part]
                    sums[8 * q + r] += jnp.sum(both.reshape(part // 8, 8, LANES), axis=0)
            return carry

        lax.fori_loop(0, frames // part, chunk, 0)
        out[...] = jnp.sum(sums[...], axis=1) * scale

    return call(
        body,
        "taps_grad",
        places,
        (chans // LANES,),
        [lanes(16, LANES), lanes(frames, LANES), lanes(16, LANES), lanes(frames, LANES)],
        [(shape((32, chans), F32), lanes(32, LANES))],
        [before, glu, after, d_conv],
        [pltpu.VMEM((frames + 32, LANES), F32), pltpu.VMEM((32, 8, LANES), F32)],
        64 * frames * chans,
    )[0]


def pair_grads(places, mine, theirs, normed, normed_theirs, scale):
    frames, half = mine.shape
    width = normed.shape[1]
    step = 512

    def body(p, m, t, n, nt, out, turned):
        @pl.when(pl.program_id(0) == 0)
        def _():
            turned[:, :frames] = m[...].T
            turned[:, frames:] = t[...].T

        total = dot(turned[:, :frames], n[...], NN) + dot(turned[:, frames:], nt[...], NN)
        out[...] = (total * scale).astype(BF16)

    return call(
        body,
        "pair_grads",
        places,
        (width // step,),
        [whole((frames, half))] * 2 + [lanes(frames, step)] * 2,
        [(shape((half, width), BF16), lanes(half, step))],
        [mine, theirs, normed, normed_theirs],
        [pltpu.VMEM((half, 2 * frames), BF16)],
        4 * half * width * frames,
    )[0]


def out_grads(places, cot, cot_theirs, acts, scale):
    chans, frames = cot.shape
    half = chans // 2

    def body(p, c, ct, a, b, a_theirs, b_theirs, out):
        @pl.when(pl.program_id(0) == 0)
        def _():
            total = dot(c[...], a[...], NN) + dot(ct[...], a_theirs[...], NN)
            out[...] = (total * scale).astype(BF16)

        @pl.when(pl.program_id(0) == 1)
        def _():
            total = dot(c[...], b[...], NN) + dot(ct[...], b_theirs[...], NN)
            out[...] = (total * scale).astype(BF16)

    return call(
        body,
        "out_grads",
        places,
        (2,),
        [pl.BlockSpec((half, frames), lambda i, p: (p[1], 0)), whole((half, frames))]
        + [whole((frames, chans))] * 4,
        [
            (
                shape((half, 2 * chans), BF16),
                pl.BlockSpec((half, chans), lambda i, p: (0, jnp.where(i == 0, p[0], 1 - p[0]))),
            )
        ],
        [cot, cot_theirs, *acts],
        (),
        8 * half * chans * frames,
    )[0]


def d_normed_terms(places, values, gates, value_weight, gate_weight):
    frames, half = values[0].shape
    chans = 2 * half

    def body(p, vo, vt, go, gt, wv, wg, theirs, mine):
        own = pl.ds(pl.multiple_of(p[1] * half, LANES), half)
        other = pl.ds(pl.multiple_of((1 - p[1]) * half, LANES), half)
        total = dot(vo[...], wv[own, :], NN) + dot(vt[...], wv[other, :], NN)
        total = total + dot(go[...], wg[own, :], NN) + dot(gt[...], wg[other, :], NN)

        @pl.when(pl.program_id(0) == 0)
        def _():
            theirs[...] = total.astype(BF16)

        @pl.when(pl.program_id(0) == 1)
        def _():
            mine[...] = total.astype(BF16)

    out = (shape((frames, chans), BF16), whole((frames, chans)))
    weight = pl.BlockSpec((chans, chans), lambda i, p: (0, jnp.where(i == 0, 1 - p[0], p[0])))
    return call(
        body,
        "d_normed_terms",
        places,
        (2,),
        [whole((frames, half))] * 4 + [weight] * 2,
        [out, out],
        [*values, *gates, value_weight, gate_weight],
        (),
        8 * chans * chans * frames,
    )


def norm_sums(places, term, recv, hat, gain):
    frames, chans = hat.shape
    height = LANES

    def body(p, tm, tr, h, g, sums, gain_grad):
        d = tm[...].astype(F32) + tr[...].astype(F32)

        @pl.when(pl.program_id(0) == 0)
        def _():
            gain_grad[...] = jnp.zeros_like(gain_grad)

        gain_grad[...] += jnp.sum(d * h[...], axis=0, keepdims=True)
        d = d * g[...]
        sums[...] = to_rows(
            jnp.sum(d, axis=1, keepdims=True), jnp.sum(d * h[...], axis=1, keepdims=True)
        )

    some = rows_of(height, chans)
    return call(
        body,
        "norm_sums",
        places,
        (frames // height,),
        [some, some, some, whole((1, chans))],
        [
            (shape((8, frames), F32), lanes(8, height)),
            (shape((1, chans), F32), whole((1, chans))),
        ],
        [term, recv, hat, gain],
        (),
        10 * frames * chans,
    )


def input_step(places, term, recv, hat, gain, inv, mine, theirs, cot):
    frames, chans = hat.shape
    height = LANES
    width = 2 * chans

    def body(p, tm, tr, h, g, i, um, ut, c, out):
        d = (tm[...].astype(F32) + tr[...].astype(F32)) * g[...]
        first, second = to_cols(um[...] + ut[...])
        got = (d - first / width - h[...] * (second / width)) * i[:, 0:1]
        out[...] = (c[...].astype(F32) + got.T).astype(BF16)

    some = rows_of(height, chans)
    line = lanes(8, height)
    return call(
        body,
        "input_step",
        places,
        (frames // height,),
        [some, some, some, whole((1, chans)), rows_of(height, LANES), line, line, lanes(chans, height)],
        [(shape((chans, frames), BF16), lanes(chans, height))],
        [term, recv, hat, gain, inv, mine, theirs, cot],
        (),
        10 * frames * chans,
    )[0]


def out_step(places, frames_in, weight, act, act_theirs):
    chans, frames = frames_in.shape
    step = 256

    def body(p, x, w, a, b, out):
        own = pl.ds(pl.multiple_of(p[0] * chans, LANES), chans)
        other = pl.ds(pl.multiple_of((1 - p[0]) * chans, LANES), chans)
        total = dot(w[:, own], a[...], NT) + dot(w[:, other], b[...], NT)
        out[...] = (x[...].astype(F32) + total).astype(BF16)

    return call(
        body,
        "out_step",
        places,
        (chans // step,),
        [rows_of(step, frames), rows_of(step, 2 * chans)] + [whole((frames, chans))] * 2,
        [(shape((chans, frames), BF16), rows_of(step, frames))],
        [frames_in, weight, act, act_theirs],
        (),
        4 * chans * chans * frames,
    )[0]


def join_halves(places, mine, theirs):
    half, cols = mine.shape
    parts = 2
    step = half // parts

    def body(p, m, t, out):
        lower = pl.program_id(0) < parts

        @pl.when(lower == (p[1] == 0))
        def _():
            out[...] = m[...]

        @pl.when(lower != (p[1] == 0))
        def _():
            out[...] = t[...]

    def hold(first, i):
        return jnp.where(first, jnp.minimum(i, parts - 1), jnp.maximum(i - parts, 0))

    return call(
        body,
        "join_halves",
        places,
        (2 * parts,),
        [
            pl.BlockSpec((step, cols), lambda i, p: (hold(p[1] == 0, i), 0)),
            pl.BlockSpec((step, cols), lambda i, p: (hold(p[1] == 1, i), 0)),
        ],
        [(shape((2 * half, cols), BF16), rows_of(step, cols))],
        [mine, theirs],
    )[0]


def ring_of(count):
    chips = count // 2
    if chips % 2 == 0:
        cols = chips // 2
        order = [2 * col for col in range(cols)] + [2 * col + 1 for col in reversed(range(cols))]
    else:
        order = list(range(chips))
    place = [0] * count
    ahead, behind = [], []
    for spot, chip in enumerate(order):
        after = order[(spot + 1) % chips]
        for core in range(2):
            place[2 * chip + core] = spot
            ahead.append((2 * chip + core, 2 * after + core))
            behind.append((2 * after + core, 2 * chip + core))
    return chips, place, ahead, behind


def pairs_of(count, step):
    return [(i, i ^ step) for i in range(count)]


def add(left, right):
    return (left.astype(F32) + right.astype(F32)).astype(BF16)


def ring_sum(sets):
    count = lax.axis_size("seq")
    chips, place, ahead, behind = ring_of(count)
    spot = jnp.asarray(place, jnp.int32)[lax.axis_index("seq")]
    reach = chips // 2

    def at(step):
        return (spot + step + chips) % chips

    def part(cells, step):
        return lax.dynamic_index_in_dim(cells, at(step), 0, keepdims=False)

    def put(cells, some, step):
        return lax.dynamic_update_index_in_dim(cells, some, at(step), 0)

    def up(cells):
        return lax.ppermute(cells, "seq", ahead)

    def down(cells):
        return lax.ppermute(cells, "seq", behind)

    half = sets[0].shape[1] // 2
    flows = [(up(part(x, reach)[half:]), down(part(x, -reach)[:half])) for x in sets]
    for hop in range(reach - 1, 0, -1):
        later = []
        for x, (u, d) in zip(sets, flows):
            own_u, own_d = part(x, hop), part(x, -hop)
            if hop == reach - 1:
                u = jnp.concatenate([own_u[:half], add(own_u[half:], u)])
                d = jnp.concatenate([add(own_d[:half], d), own_d[half:]])
            else:
                u, d = add(own_u, u), add(own_d, d)
            later.append((up(u), down(d)))
        flows = later
    owns = [
        (part(x, 0).astype(F32) + u.astype(F32) + d.astype(F32)).astype(BF16)
        for x, (u, d) in zip(sets, flows)
    ]
    outs = [put(x, own, 0) for x, own in zip(sets, owns)]
    flows = [(own, own) for own in owns]
    for hop in range(1, reach):
        flows = [(up(u), down(d)) for u, d in flows]
        outs = [put(put(x, u, -hop), d, hop) for x, (u, d) in zip(outs, flows)]
    for i, (u, d) in enumerate(flows):
        outs[i] = put(outs[i], jnp.concatenate([down(d[:half]), up(u[half:])]), reach)
    return outs


def weight_sums(grads):
    count = lax.axis_size("seq")
    rows, cols = grads[0].shape
    chips = count // 2
    if count % 4 or rows % (2 * chips) or rows // (2 * chips) < 2:
        return [lax.psum(g.astype(BF16), "seq") for g in grads]
    core = lax.axis_index("seq") % 2
    swap = pairs_of(count, 1)
    half = rows // 2
    sets = []
    for g in grads:
        g = g.astype(BF16)
        theirs = lax.dynamic_slice_in_dim(g, (1 - core) * half, half, 0)
        mine = lax.dynamic_slice_in_dim(g, core * half, half, 0)
        mine = add(mine, lax.ppermute(theirs, "seq", swap))
        sets.append(mine.reshape(chips, half // chips, cols))
    outs = []
    for mine in ring_sum(sets):
        mine = mine.reshape(half, cols)
        theirs = lax.ppermute(mine, "seq", swap)
        outs.append(
            jnp.where(
                core == 0,
                jnp.concatenate([mine, theirs]),
                jnp.concatenate([theirs, mine]),
            )
        )
    return outs


def small_sum(values):
    count = lax.axis_size("seq")
    if count & (count - 1):
        return lax.psum(values, "seq")
    step = 1
    while step < count:
        values = values + lax.ppermute(values, "seq", pairs_of(count, step))
        step *= 2
    return values


def other(values):
    return lax.ppermute(values, "tp", [(0, 1), (1, 0)])


def tp_sum(values):
    if lax.axis_size("tp") == 2:
        return values + other(values)
    return lax.psum(values, "tp")


def tp_gather(values):
    if lax.axis_size("tp") == 2:
        theirs = other(values)
        first = lax.axis_index("tp") == 0
        return jnp.where(
            first, jnp.concatenate([values, theirs]), jnp.concatenate([theirs, values])
        )
    return lax.all_gather(values, "tp", axis=0, tiled=True)


def tp_scatter(term):
    term = term.astype(BF16)
    if lax.axis_size("tp") == 2:
        rows = term.shape[0] // 2
        me = lax.axis_index("tp")
        theirs = lax.dynamic_slice_in_dim(term, (1 - me) * rows, rows, 0)
        mine = lax.dynamic_slice_in_dim(term, me * rows, rows, 0)
        return mine.astype(F32) + other(theirs).astype(F32)
    return lax.psum_scatter(term, "tp", scatter_dimension=0, tiled=True).astype(F32)


def halo(cells, reach):
    count = lax.axis_size("seq")
    size = cells.shape[1]
    right = [(i, i + 1) for i in range(count - 1)]
    left = [(i + 1, i) for i in range(count - 1)]
    before = lax.ppermute(cells[:, size - reach :], "seq", right)
    after = lax.ppermute(cells[:, :reach], "seq", left)
    return jnp.concatenate([before, cells, after], axis=1)


def norm_back(d_hat, hat, inverse, width):
    sums = jnp.concatenate(
        [jnp.sum(d_hat, axis=0, keepdims=True), jnp.sum(d_hat * hat, axis=0, keepdims=True)]
    )
    sums = tp_sum(sums) / width
    return (d_hat - sums[:1] - hat * sums[1:]) * inverse


def contract_rows(left, right):
    return lax.dot_general(left, right, (((0,), (0,)), ((), ())), preferred_element_type=F32)


def contract_cols(left, right):
    return lax.dot_general(left, right, (((1,), (1,)), ((), ())), preferred_element_type=F32)


def plain(
    frames_in, norm_gain, value_weight, gate_weight, depth_kernel, conv_gain, out_weight, cotangent
):
    chans, row_count = frames_in.shape
    parts = lax.axis_size("tp")
    me = lax.axis_index("tp")
    width = chans * parts
    taps = depth_kernel.shape[1]
    reach = taps // 2
    scale = float(row_count * lax.axis_size("seq")) ** (-0.5)

    frames_all = tp_gather(frames_in)
    gain_all = lax.all_gather(norm_gain, "tp", axis=0, tiled=True)
    d_act = tp_scatter(contract_rows(out_weight, cotangent))

    wide = frames_all.astype(F32)
    centred = wide - jnp.mean(wide, axis=0, keepdims=True)
    inverse_in = lax.rsqrt(jnp.mean(centred * centred, axis=0, keepdims=True) + EPS)
    hat_all = centred * inverse_in
    normed_all = (hat_all * gain_all[:, None]).astype(BF16)
    value = jnp.dot(value_weight, normed_all, preferred_element_type=F32)
    gate = jnp.dot(gate_weight, normed_all, preferred_element_type=F32)
    gate_sig = jax.nn.sigmoid(gate)
    glu = (value * gate_sig).astype(BF16)
    glu_wide = halo(glu, reach).astype(F32)
    conv = jnp.zeros((chans, row_count), F32)
    for tap in range(taps):
        conv = conv + depth_kernel[:, tap : tap + 1] * glu_wide[:, tap : tap + row_count]

    mean = jnp.mean(conv, axis=0, keepdims=True)
    spread = jnp.sum((conv - mean) ** 2, axis=0, keepdims=True)
    if parts == 2:
        there = other(jnp.concatenate([mean, spread]))
        gap = mean - there[:1]
        mean = (mean + there[:1]) * 0.5
        spread = (spread + there[1:] + gap * gap * (chans * 0.5)) / width
    else:
        whole = lax.pmean(mean, "tp")
        spread = lax.psum(spread + chans * (mean - whole) ** 2, "tp") / width
        mean = whole
    inverse_conv = lax.rsqrt(spread + EPS)
    hat_conv = (conv - mean) * inverse_conv
    scaled = hat_conv * conv_gain[:, None]
    swish_sig = jax.nn.sigmoid(scaled)
    act = (scaled * swish_sig).astype(BF16)
    act_all = tp_gather(act)
    block_out = (
        frames_in.astype(F32) + jnp.dot(out_weight, act_all, preferred_element_type=F32)
    ).astype(BF16)
    grad_out = contract_cols(cotangent, act_all) * scale

    d_scaled = d_act * (swish_sig + scaled * swish_sig * (1.0 - swish_sig))
    grad_conv_gain = jnp.sum(d_scaled * hat_conv, axis=1) * scale
    d_conv = norm_back(d_scaled * conv_gain[:, None], hat_conv, inverse_conv, width).astype(BF16)
    d_conv_f = d_conv.astype(F32)
    d_conv_wide = halo(d_conv, reach).astype(F32)
    d_glu = jnp.zeros((chans, row_count), F32)
    kernel_cols = []
    for tap in range(taps):
        start = 2 * reach - tap
        d_glu = d_glu + depth_kernel[:, tap : tap + 1] * d_conv_wide[:, start : start + row_count]
        kernel_cols.append(jnp.sum(glu_wide[:, tap : tap + row_count] * d_conv_f, axis=1))
    grad_kernel = jnp.stack(kernel_cols, axis=0) * scale
    d_value = (d_glu * gate_sig).astype(BF16)
    d_gate = (d_glu * value * gate_sig * (1.0 - gate_sig)).astype(BF16)
    grad_value = contract_cols(d_value, normed_all) * scale
    grad_gate = contract_cols(d_gate, normed_all) * scale
    d_normed = tp_scatter(
        contract_rows(value_weight, d_value) + contract_rows(gate_weight, d_gate)
    )
    hat_in = lax.dynamic_slice_in_dim(hat_all, me * chans, chans, 0)
    grad_norm_gain = jnp.sum(d_normed * hat_in, axis=1) * scale
    input_grad = (
        cotangent.astype(F32) + norm_back(d_normed * norm_gain[:, None], hat_in, inverse_in, width)
    ).astype(BF16)
    small = small_sum(
        jnp.concatenate([grad_kernel, grad_conv_gain[None], grad_norm_gain[None]], axis=0)
    )
    grad_out, grad_value, grad_gate = weight_sums([grad_out, grad_value, grad_gate])
    return (
        block_out,
        input_grad,
        small[taps + 1],
        grad_value,
        grad_gate,
        small[:taps].T,
        small[taps],
        grad_out,
    )


def core_swap(values):
    return lax.ppermute(values, "seq", pairs_of(lax.axis_size("seq"), 1))


def rims(tail, head):
    count = lax.axis_size("seq")
    before = lax.ppermute(tail, "seq", [(i, i + 1) for i in range(count - 1)])
    after = lax.ppermute(head, "seq", [(i + 1, i) for i in range(count - 1)])
    return before, after


def tied(values, *after):
    return lax.optimization_barrier((values, *after))[0]


def fused(
    frames_in, norm_gain, value_weight, gate_weight, depth_kernel, conv_gain, out_weight, cotangent
):
    chans, frames = frames_in.shape
    taps = depth_kernel.shape[1]
    half = chans // 2
    count = lax.axis_size("seq")
    scale = float(frames * count) ** (-0.5)
    core = lax.axis_index("seq") % 2
    places = jnp.stack([lax.axis_index("tp"), core]).astype(jnp.int32)

    gain = norm_gain[None]
    gain_theirs = other(gain)
    frames_theirs = other(frames_in)
    taps_by = depth_kernel.T
    cot_theirs = core_swap(lax.dynamic_slice_in_dim(cotangent, (1 - core) * half, half, 0))

    theirs, d_act_mine = d_act_terms(places, cotangent, out_weight)
    d_act_recv = other(theirs)

    normed, hat_in, inv_in, glu, sig, slope, edge = glu_forward(
        places, frames_in, frames_theirs, gain, gain_theirs, value_weight, gate_weight
    )
    normed_theirs = core_swap(normed)
    before, after = rims(edge[1], edge[0])
    conv, stats = conv_forward(places, before, glu, after, taps_by)
    stats_theirs = other(stats)
    act, hat_conv, e, sums, gain_grad = act_step(
        places, conv, stats, stats_theirs, d_act_mine, d_act_recv, conv_gain[None]
    )
    sums_theirs = other(sums)
    act_theirs = other(act)
    d_conv, head, tail = d_conv_step(places, e, hat_conv, stats, stats_theirs, sums, sums_theirs)
    d_before, d_after = rims(tail, head)
    sent_v, sent_g = d_glu_step(places, d_before, d_conv, d_after, taps_by, sig, slope, False)
    recv_v, recv_g = core_swap(sent_v), core_swap(sent_g)
    own_v, own_g = d_glu_step(places, d_before, d_conv, d_after, taps_by, sig, slope, True)

    acts = [act, act_theirs, core_swap(act), core_swap(act_theirs)]
    grad_out = out_grads(places, cotangent, cot_theirs, acts, scale)
    grad_value = pair_grads(places, own_v, recv_v, normed, normed_theirs, scale)
    grad_gate = pair_grads(places, own_g, recv_g, normed, normed_theirs, scale)

    chips = count // 2
    sets = [g.reshape(chips, half // chips, 2 * chans) for g in (grad_out, grad_value, grad_gate)]
    sums_out = [g.reshape(half, 2 * chans) for g in ring_sum(sets)]
    swapped = [core_swap(g) for g in sums_out]
    grad_out, grad_value, grad_gate = [
        join_halves(places, mine, there) for mine, there in zip(sums_out, swapped)
    ]

    held = tied(own_v, sets[1])
    theirs, mine = d_normed_terms(
        places, [held, sent_v], [own_g, sent_g], value_weight, gate_weight
    )
    recv = other(theirs)
    kernel_grad = taps_grad(places, before, glu, after, tied(d_conv, theirs), scale)
    block_out = out_step(places, frames_in, out_weight, act, tied(act_theirs, theirs))
    sums_in, norm_grad = norm_sums(places, mine, recv, hat_in, gain)
    input_grad = input_step(
        places, mine, recv, hat_in, gain, inv_in, sums_in, other(sums_in), cotangent
    )
    small = small_sum(jnp.concatenate([kernel_grad, gain_grad * scale, norm_grad * scale]))
    return (
        block_out,
        input_grad,
        small[taps + 1],
        grad_value,
        grad_gate,
        small[:taps].T,
        small[taps],
        grad_out,
    )


def local(*arrays):
    chans, frames = arrays[0].shape
    taps = arrays[4].shape[1]
    count = lax.axis_size("seq")
    fits = lax.axis_size("tp") == 2 and taps == 32 and chans % 256 == 0 and frames % 128 == 0
    fits = fits and count % 4 == 0 and chans % (16 * count) == 0
    return (fused if fits else plain)(*arrays)


def solution(mesh):
    return jax.shard_map(
        local,
        mesh=mesh,
        in_specs=(
            P("tp", "seq"),
            P("tp"),
            P("tp", None),
            P("tp", None),
            P("tp", None),
            P("tp"),
            P("tp", None),
            P("tp", "seq"),
        ),
        out_specs=(
            P("tp", "seq"),
            P("tp", "seq"),
            P("tp"),
            P("tp", None),
            P("tp", None),
            P("tp", None),
            P("tp"),
            P("tp", None),
        ),
        check_vma=False,
    )
```

```python
import functools

import jax
import jax.numpy as jnp
from jax import lax
from jax.experimental import pallas as pl
from jax.experimental.pallas import tpu as pltpu
from jax.sharding import PartitionSpec as P

EPS = 1e-05
F32 = jnp.float32
BF16 = jnp.bfloat16
LANES = 128


def dot(left, right, contract):
    return lax.dot_general(left, right, (contract, ((), ())), preferred_element_type=F32)


NT = ((1,), (1,))
NN = ((1,), (0,))
TN = ((0,), (0,))


def call(body, name, places, grid, ins, outs, args, scratch=(), flops=0, aliases=()):
    return pl.pallas_call(
        body,
        out_shape=[s for s, _ in outs],
        grid_spec=pltpu.PrefetchScalarGridSpec(
            num_scalar_prefetch=1,
            grid=grid,
            in_specs=ins,
            out_specs=[b for _, b in outs],
            scratch_shapes=list(scratch),
        ),
        compiler_params=pltpu.CompilerParams(vmem_limit_bytes=24 * 2**20),
        cost_estimate=pl.CostEstimate(flops=1000, bytes_accessed=1000, transcendentals=0),
        input_output_aliases=dict(aliases),
        name=name,
    )(places, *args)


def shape(dims, kind):
    return jax.ShapeDtypeStruct(dims, kind)


def whole(dims):
    return pl.BlockSpec(dims, lambda i, p: (0,) * len(dims))


def lanes(rows, width):
    return pl.BlockSpec((rows, width), lambda i, p: (0, i))


def rows_of(height, cols):
    return pl.BlockSpec((height, cols), lambda i, p: (i, 0))


def d_act_terms(places, cotangent, weight):
    chans, frames = cotangent.shape

    def body(p, cot, w, theirs, mine, turned):
        @pl.when(pl.program_id(0) == 0)
        def _():
            turned[...] = cot[...].T
            theirs[...] = dot(turned[...], w[...], NN).astype(BF16)

        @pl.when(pl.program_id(0) == 1)
        def _():
            mine[...] = dot(turned[...], w[...], NN).astype(BF16)

    out = (shape((frames, chans), BF16), whole((frames, chans)))
    return call(
        body,
        "d_act_terms",
        places,
        (2,),
        [
            whole((chans, frames)),
            pl.BlockSpec((chans, chans), lambda i, p: (0, jnp.where(i == 0, 1 - p[0], p[0]))),
        ],
        [out, out],
        [cotangent, weight],
        [pltpu.VMEM((frames, chans), BF16)],
        4 * chans * chans * frames,
    )


def edges_first(index, count):
    quarter = count // 4
    inner = jnp.where(index < 2 * quarter, index + 2 * quarter, index - quarter)
    return jnp.where(index < quarter, index, inner)


def pack_edges(places, frames_in, gain):
    chans, frames = frames_in.shape
    quarter = frames // 4

    def body(p, first, last, g, out):
        out[:chans, :quarter] = first[...]
        out[:chans, quarter:] = last[...]
        out[chans:, :] = jnp.zeros_like(out[chans:, :])
        rest = g[...]
        rows = []
        for _ in range(3):
            term = rest.astype(BF16).astype(F32)
            rest = rest - term
            rows += [term[:, at : at + 2 * quarter] for at in range(0, chans, 2 * quarter)]
        rows.append(jnp.zeros((16 - len(rows), 2 * quarter), F32))
        out[chans:, :] = jnp.concatenate(rows).astype(BF16)

    return call(
        body,
        "pack_edges",
        places,
        (1,),
        [
            pl.BlockSpec((chans, quarter), lambda i, p: (0, 0)),
            pl.BlockSpec((chans, quarter), lambda i, p: (0, 3)),
            whole((1, chans)),
        ],
        [(shape((chans + 16, 2 * quarter), BF16), whole((chans + 16, 2 * quarter)))],
        [frames_in, frames_in, gain],
    )[0]


def glu_forward(places, mine, theirs, gain, packed, weights, held):
    chans, frames = mine.shape[0] // 16 * 16, mine.shape[1]
    if not held:
        chans = chans - 16
    width = 2 * chans
    step = 256
    half = 1 if held else 0

    def body(p, xm, xt, gm, gt, wv, wg, *refs):
        normed, hat, inv, glu, sig, slope, edge = refs[len(held) :]

        @pl.when(pl.program_id(0) == 0)
        def _():
            low = pl.multiple_of(p[0] * chans, LANES)
            high = pl.multiple_of((1 - p[0]) * chans, LANES)
            terms = gt[...].astype(F32)
            count = chans // frames
            gain_theirs = jnp.concatenate(
                [
                    terms[k : k + 1] + terms[count + k : count + k + 1]
                    + terms[2 * count + k : 2 * count + k + 1]
                    for k in range(count)
                ],
                axis=1,
            )
            for at in range(0, frames, LANES):
                some = pl.ds(at, LANES)
                a = xm[:chans, some].T.astype(F32)
                b = xt[:chans, some].T.astype(F32)
                total = jnp.sum(a, axis=1, keepdims=True) + jnp.sum(b, axis=1, keepdims=True)
                mean = total / width
                a = a - mean
                b = b - mean
                spread = jnp.sum(a * a, axis=1, keepdims=True)
                spread = spread + jnp.sum(b * b, axis=1, keepdims=True)
                scale = lax.rsqrt(spread / width + EPS)
                a = a * scale
                b = b * scale
                hat[some, :] = a
                inv[some, :] = jnp.broadcast_to(scale, (LANES, LANES))
                normed[some, pl.ds(low, chans)] = (a * gm[...]).astype(BF16)
                normed[some, pl.ds(high, chans)] = (b * gain_theirs).astype(BF16)

        value = dot(normed[...], wv[...], NT)
        gate = dot(normed[...], wg[...], NT)
        s = jax.nn.sigmoid(gate)
        g = (value * s).astype(BF16)
        glu[...] = g
        edge[0] = g[:16]
        edge[1] = g[frames - 16 :]
        sig[...] = s
        slope[...] = value * s * (1.0 - s)

    block = pl.BlockSpec((frames, step), lambda i, p: (half, i))

    def full(cols):
        return pl.BlockSpec((frames, cols), lambda i, p: (half, 0))

    return call(
        body,
        "glu_middle" if held else "glu_edges",
        places,
        (chans // step,),
        [whole(mine.shape)] * 2
        + [whole((1, chans)), pl.BlockSpec((16, frames), lambda i, p: (chans // 16, 0))]
        + [rows_of(step, width)] * 2
        + [pl.BlockSpec(memory_space=pl.ANY)] * len(held),
        [
            (shape((2 * frames, width), BF16), full(width)),
            (shape((2 * frames, chans), F32), full(chans)),
            (shape((2 * frames, LANES), F32), full(LANES)),
            (shape((2 * frames, chans), BF16), block),
            (shape((2 * frames, chans), F32), block),
            (shape((2 * frames, chans), F32), block),
            (shape((2, 16, chans), BF16), pl.BlockSpec((2, 16, step), lambda i, p: (0, 0, i))),
        ],
        [mine, theirs, gain, packed, *weights, *held],
        (),
        4 * chans * width * frames,
        [(7 + i, i) for i in range(len(held))],
    )


def fill_edges_first(wide, before, own, after):
    frames = own.shape[0]
    quarter = frames // 4
    wide[:16, :] = before[...].astype(F32)
    wide[16 : 16 + quarter, :] = own[:quarter, :].astype(F32)
    wide[16 + quarter : 16 + 3 * quarter, :] = own[2 * quarter :, :].astype(F32)
    wide[16 + 3 * quarter : 16 + frames, :] = own[quarter : 2 * quarter, :].astype(F32)
    wide[16 + frames :, :] = after[...].astype(F32)


def fill(wide, before, own, after):
    frames = own.shape[0]
    wide[:16, :] = before[...].astype(F32)
    wide[16 : 16 + frames, :] = own[...].astype(F32)
    wide[16 + frames :, :] = after[...].astype(F32)


def to_rows(first, second):
    size = first.shape[0]
    lane = lax.broadcasted_iota(jnp.int32, (size, LANES), 1)
    both = jnp.where(lane == 0, first, jnp.where(lane == 1, second, 0.0))
    return both.T[:8]


def to_cols(rows):
    turned = jnp.concatenate([rows] * (LANES // 8)).T
    return turned[:, 0:1], turned[:, 1:2]


STEP = 64


def conv_forward(places, before, glu, after, taps):
    frames, chans = glu.shape
    blocks = chans // LANES

    def body(p, b, g, a, w, conv, stats, wide):
        at = pl.program_id(0)
        fill_edges_first(wide, b, g, a)

        def chunk(i, carry):
            start = pl.multiple_of(i * STEP, STEP)
            total = jnp.zeros((STEP, LANES), F32)
            for r in range(8):
                x = wide[pl.ds(start + r, STEP + 24), :]
                for q in range(4):
                    tap = 8 * q + r
                    total = total + w[tap : tap + 1, :] * x[8 * q : 8 * q + STEP]
            conv[pl.ds(start, STEP), pl.ds(pl.multiple_of(at * LANES, LANES), LANES)] = total
            return carry

        lax.fori_loop(0, frames // STEP, chunk, 0)

        @pl.when(at == blocks - 1)
        def _():
            for low in range(0, frames, LANES):
                x = conv[low : low + LANES, :]
                mean = jnp.sum(x, axis=1, keepdims=True) / chans
                x = x - mean
                stats[:, low : low + LANES] = to_rows(mean, jnp.sum(x * x, axis=1, keepdims=True))

    return call(
        body,
        "conv_forward",
        places,
        (blocks,),
        [lanes(16, LANES), lanes(frames, LANES), lanes(16, LANES), lanes(32, LANES)],
        [
            (shape((frames, chans), F32), whole((frames, chans))),
            (shape((8, frames), F32), whole((8, frames))),
        ],
        [before, glu, after, taps],
        [pltpu.VMEM((frames + 32, LANES), F32)],
        64 * frames * chans,
    )


def merge(mine, theirs, chans):
    mean, spread = to_cols(mine)
    there, more = to_cols(theirs)
    gap = mean - there
    whole_spread = spread + more + gap * gap * (chans * 0.5)
    return (mean + there) * 0.5, lax.rsqrt(whole_spread / (2 * chans) + EPS)


def act_step(places, conv, mine, theirs, term, recv, gain):
    frames, chans = conv.shape
    height = LANES

    def body(p, x, sm, st, tm, tr, g, hat, e, sums, gain_grad):
        mean, inverse = merge(sm[...], st[...], chans)
        h = (x[...] - mean) * inverse
        hat[...] = h
        scaled = h * g[...]
        s = jax.nn.sigmoid(scaled)
        soft = scaled * s
        d = tm[...].astype(F32) + tr[...].astype(F32)
        d = d * (s + soft * (1.0 - s))

        @pl.when(pl.program_id(0) == 0)
        def _():
            gain_grad[...] = jnp.zeros_like(gain_grad)

        gain_grad[...] += jnp.sum(d * h, axis=0, keepdims=True)
        d = d * g[...]
        e[...] = d
        sums[...] = to_rows(
            jnp.sum(d, axis=1, keepdims=True), jnp.sum(d * h, axis=1, keepdims=True)
        )

    some = rows_of(height, chans)
    line = lanes(8, height)
    return call(
        body,
        "act_step",
        places,
        (frames // height,),
        [some, line, line, some, some, whole((1, chans))],
        [
            (shape((frames, chans), F32), some),
            (shape((frames, chans), F32), some),
            (shape((8, frames), F32), line),
            (shape((1, chans), F32), whole((1, chans))),
        ],
        [conv, mine, theirs, term, recv, gain],
        (),
        30 * frames * chans,
    )


def d_conv_step(places, e, hat, gain, mine, theirs, sums_mine, sums_theirs):
    frames, chans = e.shape
    height = LANES
    steps = frames // height

    def body(p, d, h, g, sm, st, um, ut, out, act, head, tail):
        _, inverse = merge(sm[...], st[...], chans)
        first, second = to_cols(um[...] + ut[...])
        width = 2 * chans
        got = (d[...] - first / width - h[...] * (second / width)) * inverse
        got = got.astype(BF16)
        out[...] = got
        scaled = h[...] * g[...]
        act[...] = (scaled * jax.nn.sigmoid(scaled)).astype(BF16)

        @pl.when(pl.program_id(0) == 0)
        def _():
            head[...] = got[:16]

        @pl.when(pl.program_id(0) == steps - 1)
        def _():
            tail[...] = got[height - 16 :]

    some = rows_of(height, chans)
    line = lanes(8, height)
    rim = (shape((16, chans), BF16), whole((16, chans)))
    return call(
        body,
        "d_conv_step",
        places,
        (steps,),
        [some, some, whole((1, chans)), line, line, line, line],
        [(shape((frames, chans), BF16), some)] * 2 + [rim, rim],
        [e, hat, gain, mine, theirs, sums_mine, sums_theirs],
        (),
        10 * frames * chans,
    )


def d_glu_step(places, before, d_conv, after, taps, sig, slope, own):
    frames, chans = d_conv.shape
    blocks = chans // LANES // 2

    def body(p, b, d, a, w, s, h, d_value, d_gate, wide):
        fill(wide, b, d, a)

        def chunk(i, carry):
            start = pl.multiple_of(i * STEP, STEP)
            total = jnp.zeros((STEP, LANES), F32)
            for r in range(8):
                x = wide[pl.ds(start + r + 1, STEP + 24), :]
                for q in range(4):
                    tap = 31 - (8 * q + r)
                    total = total + w[tap : tap + 1, :] * x[8 * q : 8 * q + STEP]
            quarter = frames // 4
            inner = jnp.where(start < 3 * quarter, start + quarter, start - 2 * quarter)
            there = jnp.where(start < quarter, start, inner)
            some = pl.ds(pl.multiple_of(there, STEP), STEP)
            d_value[some, :] = (total * s[some, :]).astype(BF16)
            d_gate[some, :] = (total * h[some, :]).astype(BF16)
            return carry

        lax.fori_loop(0, frames // STEP, chunk, 0)

    def pick(height):
        if own:
            return pl.BlockSpec((height, LANES), lambda i, p: (0, i + blocks * p[1]))
        return pl.BlockSpec((height, LANES), lambda i, p: (0, i + blocks * (1 - p[1])))

    out = (shape((frames, chans // 2), BF16), lanes(frames, LANES))
    return call(
        body,
        "d_glu_own" if own else "d_glu_other",
        places,
        (blocks,),
        [pick(16), pick(frames), pick(16), pick(32), pick(frames), pick(frames)],
        [out, out],
        [before, d_conv, after, taps, sig, slope],
        [pltpu.VMEM((frames + 32, LANES), F32)],
        32 * frames * chans,
    )


def taps_grad(places, before, glu, after, d_conv, scale):
    frames, chans = glu.shape
    part = 32

    def body(p, b, g, a, d, out, wide, sums):
        fill_edges_first(wide, b, g, a)
        sums[...] = jnp.zeros_like(sums)

        def chunk(i, carry):
            start = pl.multiple_of(i * part, part)
            mine = d[pl.ds(start, part), :].astype(F32)
            for r in range(8):
                x = wide[pl.ds(start + r, part + 24), :]
                for q in range(4):
                    both = mine * x[8 * q : 8 * q + part]
                    sums[8 * q + r] += jnp.sum(both.reshape(part // 8, 8, LANES), axis=0)
            return carry

        lax.fori_loop(0, frames // part, chunk, 0)
        out[...] = jnp.sum(sums[...], axis=1) * scale

    return call(
        body,
        "taps_grad",
        places,
        (chans // LANES,),
        [lanes(16, LANES), lanes(frames, LANES), lanes(16, LANES), lanes(frames, LANES)],
        [(shape((32, chans), F32), lanes(32, LANES))],
        [before, glu, after, d_conv],
        [pltpu.VMEM((frames + 32, LANES), F32), pltpu.VMEM((32, 8, LANES), F32)],
        64 * frames * chans,
    )[0]


def pair_grads(places, chips, mine, theirs, normed, normed_theirs, scale):
    frames, half = mine[0].shape
    width = normed.shape[1]
    step = 512

    def body(p, mv, mg, tv, tg, n, nt, out, turned):
        @pl.when(pl.program_id(0) == 0)
        def _():
            for k, (m, t) in enumerate(((mv, tv), (mg, tg))):
                turned[k, :, :frames] = m[...].T
                turned[k, :, frames:] = t[...].T

        for k in range(2):
            total = dot(turned[k, :, :frames], n[...], NN)
            total = total + dot(turned[k, :, frames:], nt[...], NN)
            out[:, k] = (total * scale).astype(BF16).reshape(chips, half // chips, step)

    dims = (chips, 2, half // chips)
    return call(
        body,
        "pair_grads",
        places,
        (width // step,),
        [whole((frames, half))] * 4 + [lanes(frames, step)] * 2,
        [(shape((*dims, width), BF16), pl.BlockSpec((*dims, step), lambda i, p: (0, 0, 0, i)))],
        [*mine, *theirs, normed, normed_theirs],
        [pltpu.VMEM((2, half, 2 * frames), BF16)],
        8 * half * width * frames,
    )[0]


def out_grads(places, cot, cot_theirs, acts, scale):
    chans, frames = cot.shape
    half = chans // 2

    def body(p, c, ct, a, b, a_theirs, b_theirs, out):
        first = pl.program_id(0) == 0
        left = jnp.where(first, a[...], b[...])
        right = jnp.where(first, a_theirs[...], b_theirs[...])
        total = dot(c[...], left, NN) + dot(ct[...], right, NN)
        out[...] = (total * scale).astype(BF16)

    out = (
        shape((half, 2 * chans), BF16),
        pl.BlockSpec((half, chans), lambda i, p: (0, jnp.where(i == 0, p[0], 1 - p[0]))),
    )
    return call(
        body,
        "out_grads",
        places,
        (2,),
        [pl.BlockSpec((half, frames), lambda i, p: (p[1], 0)), whole((half, frames))]
        + [whole((frames, chans))] * 4,
        [out],
        [cot, cot_theirs, *acts],
        (),
        8 * half * chans * frames,
    )[0]


def d_normed_terms(places, values, gates, value_weight, gate_weight):
    frames, half = values[0].shape
    chans = 2 * half

    def body(p, vo, vt, go, gt, wv, wg, theirs, mine):
        own = pl.ds(pl.multiple_of(p[1] * half, LANES), half)
        other = pl.ds(pl.multiple_of((1 - p[1]) * half, LANES), half)
        total = dot(vo[...], wv[own, :], NN) + dot(vt[...], wv[other, :], NN)
        total = total + dot(go[...], wg[own, :], NN) + dot(gt[...], wg[other, :], NN)

        @pl.when(pl.program_id(0) == 0)
        def _():
            theirs[...] = total.astype(BF16)

        @pl.when(pl.program_id(0) == 1)
        def _():
            mine[...] = total.astype(BF16)

    out = (shape((frames, chans), BF16), whole((frames, chans)))
    weight = pl.BlockSpec((chans, chans), lambda i, p: (0, jnp.where(i == 0, 1 - p[0], p[0])))
    return call(
        body,
        "d_normed_terms",
        places,
        (2,),
        [whole((frames, half))] * 4 + [weight] * 2,
        [out, out],
        [*values, *gates, value_weight, gate_weight],
        (),
        8 * chans * chans * frames,
    )


def norm_sums(places, term, recv, hat, gain):
    frames, chans = hat.shape
    height = LANES

    def body(p, tm, tr, h, g, sums, gain_grad):
        d = tm[...].astype(F32) + tr[...].astype(F32)

        @pl.when(pl.program_id(0) == 0)
        def _():
            gain_grad[...] = jnp.zeros_like(gain_grad)

        gain_grad[...] += jnp.sum(d * h[...], axis=0, keepdims=True)
        d = d * g[...]
        sums[...] = to_rows(
            jnp.sum(d, axis=1, keepdims=True), jnp.sum(d * h[...], axis=1, keepdims=True)
        )

    some = rows_of(height, chans)
    return call(
        body,
        "norm_sums",
        places,
        (frames // height,),
        [some, some, some, whole((1, chans))],
        [
            (shape((8, frames), F32), lanes(8, height)),
            (shape((1, chans), F32), whole((1, chans))),
        ],
        [term, recv, hat, gain],
        (),
        10 * frames * chans,
    )


def input_step(places, term, recv, hat, gain, inv, mine, theirs, cot):
    frames, chans = hat.shape
    height = LANES
    width = 2 * chans

    def body(p, tm, tr, h, g, i, um, ut, c, out):
        d = (tm[...].astype(F32) + tr[...].astype(F32)) * g[...]
        first, second = to_cols(um[...] + ut[...])
        got = (d - first / width - h[...] * (second / width)) * i[:, 0:1]
        out[...] = (c[...].astype(F32) + got.T).astype(BF16)

    some = rows_of(height, chans)
    line = lanes(8, height)
    block = pl.BlockSpec((chans, height), lambda i, p: (0, edges_first(i, frames // height)))
    return call(
        body,
        "input_step",
        places,
        (frames // height,),
        [some, some, some, whole((1, chans)), rows_of(height, LANES), line, line, block],
        [(shape((chans, frames), BF16), block)],
        [term, recv, hat, gain, inv, mine, theirs, cot],
        (),
        10 * frames * chans,
    )[0]


def out_step(places, frames_in, weight, act, act_theirs):
    chans, frames = frames_in.shape
    step = 256

    def body(p, x, w, a, b, out):
        own = pl.ds(pl.multiple_of(p[0] * chans, LANES), chans)
        other = pl.ds(pl.multiple_of((1 - p[0]) * chans, LANES), chans)
        total = dot(w[:, own], a[...], NT) + dot(w[:, other], b[...], NT)
        out[...] = (x[...].astype(F32) + total).astype(BF16)

    return call(
        body,
        "out_step",
        places,
        (chans // step,),
        [rows_of(step, frames), rows_of(step, 2 * chans)] + [whole((frames, chans))] * 2,
        [(shape((chans, frames), BF16), rows_of(step, frames))],
        [frames_in, weight, act, act_theirs],
        (),
        4 * chans * chans * frames,
    )[0]


def join_halves(places, pair, pair_theirs, single, single_theirs):
    chips, _, rows, cols = pair.shape

    def body(p, a, at, b, bt, *refs):
        outs, done = refs[:3], refs[3]
        copies = []
        for core, (two, one) in ((p[1], (a, b)), (1 - p[1], (at, bt))):
            for source, out in zip((two.at[:, 0], two.at[:, 1], one.at[:, 0]), outs):
                copies.append(pltpu.make_async_copy(source, out.at[core], done.at[len(copies)]))
        for copy in copies:
            copy.start()
        for copy in copies:
            copy.wait()

    anywhere = pl.BlockSpec(memory_space=pl.ANY)
    outs = call(
        body,
        "join_halves",
        places,
        (1,),
        [anywhere] * 4,
        [(shape((2, chips, rows, cols), BF16), anywhere)] * 3,
        [pair, pair_theirs, single, single_theirs],
        [pltpu.SemaphoreType.DMA((6,))],
    )
    return [out.reshape(2 * chips * rows, cols) for out in outs]


def ring_of(count):
    chips = count // 2
    if chips % 2 == 0:
        cols = chips // 2
        order = [2 * col for col in range(cols)] + [2 * col + 1 for col in reversed(range(cols))]
    else:
        order = list(range(chips))
    place = [0] * count
    ahead, behind = [], []
    for spot, chip in enumerate(order):
        after = order[(spot + 1) % chips]
        for core in range(2):
            place[2 * chip + core] = spot
            ahead.append((2 * chip + core, 2 * after + core))
            behind.append((2 * after + core, 2 * chip + core))
    return chips, place, ahead, behind


def pairs_of(count, step):
    return [(i, i ^ step) for i in range(count)]


def add(left, right):
    return (left.astype(F32) + right.astype(F32)).astype(BF16)


def ring_sum(sets):
    count = lax.axis_size("seq")
    chips, place, ahead, behind = ring_of(count)
    spot = jnp.asarray(place, jnp.int32)[lax.axis_index("seq")]
    reach = chips // 2

    def part(cells, step):
        return lax.dynamic_index_in_dim(cells, (spot + step + chips) % chips, 0, keepdims=False)

    def up(cells):
        return lax.ppermute(cells, "seq", ahead)

    def down(cells):
        return lax.ppermute(cells, "seq", behind)

    half = sets[0].shape[1] // 2
    flows = [(up(part(x, reach)[half:]), down(part(x, -reach)[:half])) for x in sets]
    for hop in range(reach - 1, 0, -1):
        later = []
        for x, (u, d) in zip(sets, flows):
            own_u, own_d = part(x, hop), part(x, -hop)
            if hop == reach - 1:
                u = jnp.concatenate([own_u[:half], add(own_u[half:], u)])
                d = jnp.concatenate([add(own_d[:half], d), own_d[half:]])
            else:
                u, d = add(own_u, u), add(own_d, d)
            later.append((up(u), down(d)))
        flows = later
    owns = [
        (part(x, 0).astype(F32) + u.astype(F32) + d.astype(F32)).astype(BF16)
        for x, (u, d) in zip(sets, flows)
    ]
    outs = []
    for x, own in zip(sets, owns):
        outs.append(lax.dynamic_update_index_in_dim(jnp.zeros_like(x), own, spot, 0))
    flows = [(own, own) for own in owns]
    for hop in range(1, reach):
        flows = [(up(u), down(d)) for u, d in flows]
        for i, (u, d) in enumerate(flows):
            out = lax.dynamic_update_index_in_dim(outs[i], u, (spot - hop + chips) % chips, 0)
            outs[i] = lax.dynamic_update_index_in_dim(out, d, (spot + hop) % chips, 0)
    for i, (u, d) in enumerate(flows):
        far = jnp.concatenate([down(d[:half]), up(u[half:])])
        outs[i] = lax.dynamic_update_index_in_dim(outs[i], far, (spot + reach) % chips, 0)
    return outs


def weight_sums(grads):
    count = lax.axis_size("seq")
    rows, cols = grads[0].shape
    chips = count // 2
    if count % 4 or rows % (2 * chips) or rows // (2 * chips) < 2:
        return [lax.psum(g.astype(BF16), "seq") for g in grads]
    core = lax.axis_index("seq") % 2
    swap = pairs_of(count, 1)
    half = rows // 2
    sets = []
    for g in grads:
        g = g.astype(BF16)
        theirs = lax.dynamic_slice_in_dim(g, (1 - core) * half, half, 0)
        mine = lax.dynamic_slice_in_dim(g, core * half, half, 0)
        mine = add(mine, lax.ppermute(theirs, "seq", swap))
        sets.append(mine.reshape(chips, half // chips, cols))
    outs = []
    for mine in ring_sum(sets):
        mine = mine.reshape(half, cols)
        theirs = lax.ppermute(mine, "seq", swap)
        outs.append(
            jnp.where(
                core == 0,
                jnp.concatenate([mine, theirs]),
                jnp.concatenate([theirs, mine]),
            )
        )
    return outs


def small_sum(values):
    count = lax.axis_size("seq")
    if count & (count - 1):
        return lax.psum(values, "seq"), []
    rests = []
    step = 1
    while step < count:
        values = values + lax.ppermute(values, "seq", pairs_of(count, step))
        rests.append(values)
        step *= 2
    return values, rests


def other(values):
    return lax.ppermute(values, "tp", [(0, 1), (1, 0)])


def tp_sum(values):
    if lax.axis_size("tp") == 2:
        return values + other(values)
    return lax.psum(values, "tp")


def tp_gather(values):
    if lax.axis_size("tp") == 2:
        theirs = other(values)
        first = lax.axis_index("tp") == 0
        return jnp.where(
            first, jnp.concatenate([values, theirs]), jnp.concatenate([theirs, values])
        )
    return lax.all_gather(values, "tp", axis=0, tiled=True)


def tp_scatter(term):
    term = term.astype(BF16)
    if lax.axis_size("tp") == 2:
        rows = term.shape[0] // 2
        me = lax.axis_index("tp")
        theirs = lax.dynamic_slice_in_dim(term, (1 - me) * rows, rows, 0)
        mine = lax.dynamic_slice_in_dim(term, me * rows, rows, 0)
        return mine.astype(F32) + other(theirs).astype(F32)
    return lax.psum_scatter(term, "tp", scatter_dimension=0, tiled=True).astype(F32)


def halo(cells, reach):
    count = lax.axis_size("seq")
    size = cells.shape[1]
    right = [(i, i + 1) for i in range(count - 1)]
    left = [(i + 1, i) for i in range(count - 1)]
    before = lax.ppermute(cells[:, size - reach :], "seq", right)
    after = lax.ppermute(cells[:, :reach], "seq", left)
    return jnp.concatenate([before, cells, after], axis=1)


def norm_back(d_hat, hat, inverse, width):
    sums = jnp.concatenate(
        [jnp.sum(d_hat, axis=0, keepdims=True), jnp.sum(d_hat * hat, axis=0, keepdims=True)]
    )
    sums = tp_sum(sums) / width
    return (d_hat - sums[:1] - hat * sums[1:]) * inverse


def contract_rows(left, right):
    return lax.dot_general(left, right, (((0,), (0,)), ((), ())), preferred_element_type=F32)


def contract_cols(left, right):
    return lax.dot_general(left, right, (((1,), (1,)), ((), ())), preferred_element_type=F32)


def plain(
    frames_in, norm_gain, value_weight, gate_weight, depth_kernel, conv_gain, out_weight, cotangent
):
    chans, row_count = frames_in.shape
    parts = lax.axis_size("tp")
    me = lax.axis_index("tp")
    width = chans * parts
    taps = depth_kernel.shape[1]
    reach = taps // 2
    scale = float(row_count * lax.axis_size("seq")) ** (-0.5)

    frames_all = tp_gather(frames_in)
    gain_all = lax.all_gather(norm_gain, "tp", axis=0, tiled=True)
    d_act = tp_scatter(contract_rows(out_weight, cotangent))

    wide = frames_all.astype(F32)
    centred = wide - jnp.mean(wide, axis=0, keepdims=True)
    inverse_in = lax.rsqrt(jnp.mean(centred * centred, axis=0, keepdims=True) + EPS)
    hat_all = centred * inverse_in
    normed_all = (hat_all * gain_all[:, None]).astype(BF16)
    value = jnp.dot(value_weight, normed_all, preferred_element_type=F32)
    gate = jnp.dot(gate_weight, normed_all, preferred_element_type=F32)
    gate_sig = jax.nn.sigmoid(gate)
    glu = (value * gate_sig).astype(BF16)
    glu_wide = halo(glu, reach).astype(F32)
    conv = jnp.zeros((chans, row_count), F32)
    for tap in range(taps):
        conv = conv + depth_kernel[:, tap : tap + 1] * glu_wide[:, tap : tap + row_count]

    mean = jnp.mean(conv, axis=0, keepdims=True)
    spread = jnp.sum((conv - mean) ** 2, axis=0, keepdims=True)
    if parts == 2:
        there = other(jnp.concatenate([mean, spread]))
        gap = mean - there[:1]
        mean = (mean + there[:1]) * 0.5
        spread = (spread + there[1:] + gap * gap * (chans * 0.5)) / width
    else:
        whole = lax.pmean(mean, "tp")
        spread = lax.psum(spread + chans * (mean - whole) ** 2, "tp") / width
        mean = whole
    inverse_conv = lax.rsqrt(spread + EPS)
    hat_conv = (conv - mean) * inverse_conv
    scaled = hat_conv * conv_gain[:, None]
    swish_sig = jax.nn.sigmoid(scaled)
    act = (scaled * swish_sig).astype(BF16)
    act_all = tp_gather(act)
    block_out = (
        frames_in.astype(F32) + jnp.dot(out_weight, act_all, preferred_element_type=F32)
    ).astype(BF16)
    grad_out = contract_cols(cotangent, act_all) * scale

    d_scaled = d_act * (swish_sig + scaled * swish_sig * (1.0 - swish_sig))
    grad_conv_gain = jnp.sum(d_scaled * hat_conv, axis=1) * scale
    d_conv = norm_back(d_scaled * conv_gain[:, None], hat_conv, inverse_conv, width).astype(BF16)
    d_conv_f = d_conv.astype(F32)
    d_conv_wide = halo(d_conv, reach).astype(F32)
    d_glu = jnp.zeros((chans, row_count), F32)
    kernel_cols = []
    for tap in range(taps):
        start = 2 * reach - tap
        d_glu = d_glu + depth_kernel[:, tap : tap + 1] * d_conv_wide[:, start : start + row_count]
        kernel_cols.append(jnp.sum(glu_wide[:, tap : tap + row_count] * d_conv_f, axis=1))
    grad_kernel = jnp.stack(kernel_cols, axis=0) * scale
    d_value = (d_glu * gate_sig).astype(BF16)
    d_gate = (d_glu * value * gate_sig * (1.0 - gate_sig)).astype(BF16)
    grad_value = contract_cols(d_value, normed_all) * scale
    grad_gate = contract_cols(d_gate, normed_all) * scale
    d_normed = tp_scatter(
        contract_rows(value_weight, d_value) + contract_rows(gate_weight, d_gate)
    )
    hat_in = lax.dynamic_slice_in_dim(hat_all, me * chans, chans, 0)
    grad_norm_gain = jnp.sum(d_normed * hat_in, axis=1) * scale
    input_grad = (
        cotangent.astype(F32) + norm_back(d_normed * norm_gain[:, None], hat_in, inverse_in, width)
    ).astype(BF16)
    small, _ = small_sum(
        jnp.concatenate([grad_kernel, grad_conv_gain[None], grad_norm_gain[None]], axis=0)
    )
    grad_out, grad_value, grad_gate = weight_sums([grad_out, grad_value, grad_gate])
    return (
        block_out,
        input_grad,
        small[taps + 1],
        grad_value,
        grad_gate,
        small[:taps].T,
        small[taps],
        grad_out,
    )


def core_swap(values):
    return lax.ppermute(values, "seq", pairs_of(lax.axis_size("seq"), 1))


def rims(tail, head):
    count = lax.axis_size("seq")
    before = lax.ppermute(tail, "seq", [(i, i + 1) for i in range(count - 1)])
    after = lax.ppermute(head, "seq", [(i + 1, i) for i in range(count - 1)])
    return before, after


def tied(values, *after):
    return lax.optimization_barrier((values, *after))[0]


class Ring:
    def __init__(self, cells):
        self.chips, _, self.ahead, self.behind = ring_of(lax.axis_size("seq"))
        chip = lax.axis_index("seq") // 2
        self.spot = jnp.where(chip % 2 == 0, chip // 2, self.chips - 1 - chip // 2)
        self.reach = self.chips // 2
        self.half = cells.shape[1] // 2
        self.cells = cells
        self.count = 0
        self.up = self.down = None
        self.extra = None

    def at(self, step):
        return (self.spot + step + self.chips) % self.chips

    def part(self, step):
        return lax.dynamic_index_in_dim(self.cells, self.at(step), 0, keepdims=False)

    def put(self, some, step):
        rows = self.cells.shape[1]
        self.cells = lax.dynamic_update_index_in_dim(self.cells, some[:rows], self.at(step), 0)
        if self.extra is not None:
            self.gathered.append(some[rows:])

    def send(self, up, down, after):
        if after:
            up, down = lax.optimization_barrier((up, down, *after))[:2]
        self.up = lax.ppermute(up, "seq", self.ahead)
        self.down = lax.ppermute(down, "seq", self.behind)

    def hop(self, *after):
        reach, half = self.reach, self.half
        self.count += 1
        left = reach + 1 - self.count
        u, d = self.up, self.down
        if self.count == 1:
            self.send(self.part(reach)[half:], self.part(-reach)[:half], after)
        elif left > 0:
            own_u, own_d = self.part(left), self.part(-left)
            if self.count == 2:
                u = jnp.concatenate([own_u[:half], add(own_u[half:], u)])
                d = jnp.concatenate([add(own_d[:half], d), own_d[half:]])
            else:
                u, d = add(own_u, u), add(own_d, d)
            self.send(u, d, after)
        else:
            if left == 0:
                own = self.part(0).astype(F32) + u.astype(F32) + d.astype(F32)
                u = d = own.astype(BF16)
                if self.extra is not None:
                    u = d = jnp.concatenate([u, self.extra])
                    self.gathered = []
                self.put(u, 0)
            if left > 1 - reach:
                self.send(u, d, after)
                self.put(self.up, left - 1)
                self.put(self.down, 1 - left)
            else:
                self.send(u[half:], d[:half], after)
                self.put(jnp.concatenate([self.down, self.up]), reach)

    def gather(self, extra):
        self.extra = extra


def fused(
    frames_in, norm_gain, value_weight, gate_weight, depth_kernel, conv_gain, out_weight, cotangent
):
    chans, frames = frames_in.shape
    taps = depth_kernel.shape[1]
    half = chans // 2
    quarter = frames // 4
    count = lax.axis_size("seq")
    chips = count // 2
    scale = float(frames * count) ** (-0.5)
    place = lax.axis_index("seq")
    core = place % 2
    places = jnp.stack([lax.axis_index("tp"), core, place // 2 % 2, place // 4 % 2])
    places = places.astype(jnp.int32)

    gain = norm_gain[None]
    edges = pack_edges(places, frames_in, gain)
    edges_theirs = other(edges)
    middle = frames_in[:, quarter : 3 * quarter]
    middle_theirs = other(middle)
    taps_by = depth_kernel.T
    cot_half = lax.dynamic_slice_in_dim(cotangent, (1 - core) * half, half, 0)

    theirs, d_act_mine = d_act_terms(places, tied(cotangent, cot_half, middle), out_weight)
    cot_theirs = core_swap(cot_half)
    d_act_recv = other(theirs)

    weights = (value_weight, gate_weight)
    *held, edge = glu_forward(places, edges, tied(edges_theirs, theirs, cot_theirs), gain, edges_theirs, weights, ())
    before, after = rims(edge[1], edge[0])
    normed, hat_in, inv_in, glu, sig, slope, _ = glu_forward(
        places,
        middle,
        middle_theirs,
        gain,
        edges_theirs,
        weights,
        tuple(held),
    )
    conv, stats = conv_forward(places, before, glu, after, taps_by)
    normed_theirs = core_swap(normed)
    stats_theirs = other(stats)
    hat_conv, e, sums, gain_grad = act_step(
        places, conv, stats, stats_theirs, d_act_mine, d_act_recv, conv_gain[None]
    )
    sums_theirs = other(sums)
    d_conv, act, head, tail = d_conv_step(
        places, e, hat_conv, conv_gain[None], stats, stats_theirs, sums, sums_theirs
    )
    d_before, d_after = rims(tail, head)
    act_theirs = other(act)
    sent_v, sent_g = d_glu_step(places, d_before, d_conv, d_after, taps_by, sig, slope, False)
    recv_v, recv_g = core_swap(sent_v), core_swap(sent_g)
    own_v, own_g = d_glu_step(
        places, d_before, tied(d_conv, sent_v), d_after, taps_by, sig, slope, True
    )

    grads = pair_grads(
        places, chips, (own_v, own_g), (recv_v, recv_g), normed, normed_theirs, scale
    )
    a = Ring(grads.reshape(chips, -1, 2 * chans))
    a.hop()
    act, act_theirs = lax.optimization_barrier((act, act_theirs, grads))[:2]
    acts = [act, act_theirs, core_swap(act), core_swap(act_theirs)]
    cot = tied(cotangent, a.up, a.down)
    grad_out = out_grads(places, cot, cot_theirs, acts, scale)
    b = Ring(grad_out.reshape(chips, -1, 2 * chans))
    b.hop()
    a.hop()
    theirs, mine = d_normed_terms(
        places, [tied(own_v, grad_out), sent_v], [own_g, sent_g], value_weight, gate_weight
    )
    recv = other(theirs)
    b.hop(theirs)
    a.hop()
    kernel_grad = taps_grad(places, before, glu, after, tied(d_conv, theirs), scale)
    b.hop(kernel_grad)
    a.hop()
    block_out = out_step(places, frames_in, out_weight, act, tied(act_theirs, kernel_grad))
    b.hop(block_out)
    a.hop()
    sums_in, norm_grad = norm_sums(places, mine, tied(recv, block_out), hat_in, gain)
    sums_in_theirs = other(sums_in)
    small = jnp.concatenate([kernel_grad, gain_grad * scale, norm_grad * scale])
    small = small + core_swap(small)
    depth = (taps + 2 + 15) // 16 * 8
    small = jnp.pad(small, ((0, 2 * depth - taps - 2), (0, 0)))
    b.gather(jnp.concatenate([small[:depth], small[depth:]], axis=1).astype(BF16))
    b.hop()
    input_grad = input_step(
        places, mine, recv, hat_in, gain, inv_in, sums_in, sums_in_theirs, cotangent
    )
    a.hop()
    b.hop(input_grad)
    a.hop()
    b.hop()
    a.hop()
    b.hop()
    small = sum(some.astype(F32) for some in b.gathered)
    small = jnp.concatenate([small[:, :chans], small[:, chans:]])

    pair = a.cells.reshape(chips, 2, half // chips, 2 * chans)
    single = b.cells.reshape(chips, 1, half // chips, 2 * chans)
    grad_value, grad_gate, grad_out = join_halves(
        places, pair, core_swap(pair), single, core_swap(single)
    )
    return (
        block_out,
        input_grad,
        small[taps + 1],
        grad_value,
        grad_gate,
        small[:taps].T,
        small[taps],
        grad_out,
    )


def local(*arrays):
    chans, frames = arrays[0].shape
    taps = arrays[4].shape[1]
    count = lax.axis_size("seq")
    fits = lax.axis_size("tp") == 2 and taps == 32 and chans % 256 == 0 and frames % 512 == 0
    fits = fits and count == 16 and chans % (16 * count) == 0
    return (fused if fits else plain)(*arrays)


def solution(mesh):
    return jax.shard_map(
        local,
        mesh=mesh,
        in_specs=(
            P("tp", "seq"),
            P("tp"),
            P("tp", None),
            P("tp", None),
            P("tp", None),
            P("tp"),
            P("tp", None),
            P("tp", "seq"),
        ),
        out_specs=(
            P("tp", "seq"),
            P("tp", "seq"),
            P("tp"),
            P("tp", None),
            P("tp", None),
            P("tp", None),
            P("tp"),
            P("tp", None),
        ),
        check_vma=False,
    )
```

```python
import functools

import jax
import jax.numpy as jnp
from jax import lax
from jax.experimental import pallas as pl
from jax.experimental.pallas import tpu as pltpu
from jax.sharding import PartitionSpec as P

EPS = 1e-05
F32 = jnp.float32
BF16 = jnp.bfloat16
LANES = 128
REAL = ()


def dot(left, right, contract):
    return lax.dot_general(left, right, (contract, ((), ())), preferred_element_type=F32)


NT = ((1,), (1,))
NN = ((1,), (0,))
TN = ((0,), (0,))


def call(body, name, places, grid, ins, outs, args, scratch=(), flops=0, aliases=()):
    real = name in REAL
    size = sum(a.size * a.dtype.itemsize for a in args)
    size += sum(s.size * s.dtype.itemsize for s, _ in outs)
    return pl.pallas_call(
        body,
        out_shape=[s for s, _ in outs],
        grid_spec=pltpu.PrefetchScalarGridSpec(
            num_scalar_prefetch=1,
            grid=grid,
            in_specs=ins,
            out_specs=[b for _, b in outs],
            scratch_shapes=list(scratch),
        ),
        compiler_params=pltpu.CompilerParams(vmem_limit_bytes=24 * 2**20),
        cost_estimate=pl.CostEstimate(
            flops=flops if real else 1000, bytes_accessed=size if real else 1000, transcendentals=0
        ),
        input_output_aliases=dict(aliases),
        name=name,
    )(places, *args)


def shape(dims, kind):
    return jax.ShapeDtypeStruct(dims, kind)


def whole(dims):
    return pl.BlockSpec(dims, lambda i, p: (0,) * len(dims))


def lanes(rows, width):
    return pl.BlockSpec((rows, width), lambda i, p: (0, i))


def rows_of(height, cols):
    return pl.BlockSpec((height, cols), lambda i, p: (i, 0))


def d_act_terms(places, cotangent, weight):
    chans, frames = cotangent.shape

    def body(p, cot, w, theirs, mine, turned):
        @pl.when(pl.program_id(0) == 0)
        def _():
            turned[...] = cot[...].T
            theirs[...] = dot(turned[...], w[...], NN).astype(BF16)

        @pl.when(pl.program_id(0) == 1)
        def _():
            mine[...] = dot(turned[...], w[...], NN).astype(BF16)

    out = (shape((frames, chans), BF16), whole((frames, chans)))
    return call(
        body,
        "d_act_terms",
        places,
        (2,),
        [
            whole((chans, frames)),
            pl.BlockSpec((chans, chans), lambda i, p: (0, jnp.where(i == 0, 1 - p[0], p[0]))),
        ],
        [out, out],
        [cotangent, weight],
        [pltpu.VMEM((frames, chans), BF16)],
        4 * chans * chans * frames,
    )


def edges_first(index, count):
    quarter = count // 4
    inner = jnp.where(index < 2 * quarter, index + 2 * quarter, index - quarter)
    return jnp.where(index < quarter, index, inner)


def pack_edges(places, frames_in, gain):
    chans, frames = frames_in.shape
    quarter = frames // 4

    def body(p, first, last, g, out):
        out[:chans, :quarter] = first[...]
        out[:chans, quarter:] = last[...]
        out[chans:, :] = jnp.zeros_like(out[chans:, :])
        rest = g[...]
        rows = []
        for _ in range(3):
            term = rest.astype(BF16).astype(F32)
            rest = rest - term
            rows += [term[:, at : at + 2 * quarter] for at in range(0, chans, 2 * quarter)]
        rows.append(jnp.zeros((16 - len(rows), 2 * quarter), F32))
        out[chans:, :] = jnp.concatenate(rows).astype(BF16)

    return call(
        body,
        "pack_edges",
        places,
        (1,),
        [
            pl.BlockSpec((chans, quarter), lambda i, p: (0, 0)),
            pl.BlockSpec((chans, quarter), lambda i, p: (0, 3)),
            whole((1, chans)),
        ],
        [(shape((chans + 16, 2 * quarter), BF16), whole((chans + 16, 2 * quarter)))],
        [frames_in, frames_in, gain],
    )[0]


def glu_forward(places, mine, theirs, gain, packed, weights, held):
    chans, frames = mine.shape[0] // 16 * 16, mine.shape[1]
    if not held:
        chans = chans - 16
    width = 2 * chans
    step = 256
    half = 1 if held else 0

    def body(p, xm, xt, gm, gt, wv, wg, *refs):
        normed, hat, inv, glu, sig, slope, edge = refs[len(held) :]

        @pl.when(pl.program_id(0) == 0)
        def _():
            low = pl.multiple_of(p[0] * chans, LANES)
            high = pl.multiple_of((1 - p[0]) * chans, LANES)
            terms = gt[...].astype(F32)
            count = chans // frames
            gain_theirs = jnp.concatenate(
                [
                    terms[k : k + 1] + terms[count + k : count + k + 1]
                    + terms[2 * count + k : 2 * count + k + 1]
                    for k in range(count)
                ],
                axis=1,
            )
            for at in range(0, frames, LANES):
                some = pl.ds(at, LANES)
                a = xm[:chans, some].T.astype(F32)
                b = xt[:chans, some].T.astype(F32)
                total = jnp.sum(a, axis=1, keepdims=True) + jnp.sum(b, axis=1, keepdims=True)
                mean = total / width
                a = a - mean
                b = b - mean
                spread = jnp.sum(a * a, axis=1, keepdims=True)
                spread = spread + jnp.sum(b * b, axis=1, keepdims=True)
                scale = lax.rsqrt(spread / width + EPS)
                a = a * scale
                b = b * scale
                hat[some, :] = a
                inv[some, :] = jnp.broadcast_to(scale, (LANES, LANES))
                normed[some, pl.ds(low, chans)] = (a * gm[...]).astype(BF16)
                normed[some, pl.ds(high, chans)] = (b * gain_theirs).astype(BF16)

        value = dot(normed[...], wv[...], NT)
        gate = dot(normed[...], wg[...], NT)
        s = jax.nn.sigmoid(gate)
        g = (value * s).astype(BF16)
        glu[...] = g
        edge[0] = g[:16]
        edge[1] = g[frames - 16 :]
        sig[...] = s
        slope[...] = value * s * (1.0 - s)

    block = pl.BlockSpec((frames, step), lambda i, p: (half, i))

    def full(cols):
        return pl.BlockSpec((frames, cols), lambda i, p: (half, 0))

    return call(
        body,
        "glu_middle" if held else "glu_edges",
        places,
        (chans // step,),
        [whole(mine.shape)] * 2
        + [whole((1, chans)), pl.BlockSpec((16, frames), lambda i, p: (chans // 16, 0))]
        + [rows_of(step, width)] * 2
        + [pl.BlockSpec(memory_space=pl.ANY)] * len(held),
        [
            (shape((2 * frames, width), BF16), full(width)),
            (shape((2 * frames, chans), F32), full(chans)),
            (shape((2 * frames, LANES), F32), full(LANES)),
            (shape((2 * frames, chans), BF16), block),
            (shape((2 * frames, chans), F32), block),
            (shape((2 * frames, chans), F32), block),
            (shape((2, 16, chans), BF16), pl.BlockSpec((2, 16, step), lambda i, p: (0, 0, i))),
        ],
        [mine, theirs, gain, packed, *weights, *held],
        (),
        4 * chans * width * frames,
        [(7 + i, i) for i in range(len(held))],
    )


def fill_edges_first(wide, before, own, after):
    frames = own.shape[0]
    quarter = frames // 4
    wide[:16, :] = before[...].astype(F32)
    wide[16 : 16 + quarter, :] = own[:quarter, :].astype(F32)
    wide[16 + quarter : 16 + 3 * quarter, :] = own[2 * quarter :, :].astype(F32)
    wide[16 + 3 * quarter : 16 + frames, :] = own[quarter : 2 * quarter, :].astype(F32)
    wide[16 + frames :, :] = after[...].astype(F32)


def fill(wide, before, own, after):
    frames = own.shape[0]
    wide[:16, :] = before[...].astype(F32)
    wide[16 : 16 + frames, :] = own[...].astype(F32)
    wide[16 + frames :, :] = after[...].astype(F32)


def to_rows(first, second):
    size = first.shape[0]
    lane = lax.broadcasted_iota(jnp.int32, (size, LANES), 1)
    both = jnp.where(lane == 0, first, jnp.where(lane == 1, second, 0.0))
    return both.T[:8]


def to_cols(rows):
    turned = jnp.concatenate([rows] * (LANES // 8)).T
    return turned[:, 0:1], turned[:, 1:2]


STEP = 64


def conv_forward(places, before, glu, after, taps):
    frames, chans = glu.shape
    blocks = chans // LANES

    def body(p, b, g, a, w, conv, stats, wide):
        at = pl.program_id(0)
        fill_edges_first(wide, b, g, a)

        def chunk(i, carry):
            start = pl.multiple_of(i * STEP, STEP)
            total = jnp.zeros((STEP, LANES), F32)
            for r in range(8):
                x = wide[pl.ds(start + r, STEP + 24), :]
                for q in range(4):
                    tap = 8 * q + r
                    total = total + w[tap : tap + 1, :] * x[8 * q : 8 * q + STEP]
            conv[pl.ds(start, STEP), pl.ds(pl.multiple_of(at * LANES, LANES), LANES)] = total
            return carry

        lax.fori_loop(0, frames // STEP, chunk, 0)

        @pl.when(at == blocks - 1)
        def _():
            for low in range(0, frames, LANES):
                x = conv[low : low + LANES, :]
                mean = jnp.sum(x, axis=1, keepdims=True) / chans
                x = x - mean
                stats[:, low : low + LANES] = to_rows(mean, jnp.sum(x * x, axis=1, keepdims=True))

    return call(
        body,
        "conv_forward",
        places,
        (blocks,),
        [lanes(16, LANES), lanes(frames, LANES), lanes(16, LANES), lanes(32, LANES)],
        [
            (shape((frames, chans), F32), whole((frames, chans))),
            (shape((8, frames), F32), whole((8, frames))),
        ],
        [before, glu, after, taps],
        [pltpu.VMEM((frames + 32, LANES), F32)],
        64 * frames * chans,
    )


def merge(mine, theirs, chans):
    mean, spread = to_cols(mine)
    there, more = to_cols(theirs)
    gap = mean - there
    whole_spread = spread + more + gap * gap * (chans * 0.5)
    return (mean + there) * 0.5, lax.rsqrt(whole_spread / (2 * chans) + EPS)


def act_step(places, conv, mine, theirs, term, recv, gain):
    frames, chans = conv.shape
    height = LANES

    def body(p, x, sm, st, tm, tr, g, hat, e, sums, gain_grad):
        mean, inverse = merge(sm[...], st[...], chans)
        h = (x[...] - mean) * inverse
        hat[...] = h
        scaled = h * g[...]
        s = jax.nn.sigmoid(scaled)
        soft = scaled * s
        d = tm[...].astype(F32) + tr[...].astype(F32)
        d = d * (s + soft * (1.0 - s))

        @pl.when(pl.program_id(0) == 0)
        def _():
            gain_grad[...] = jnp.zeros_like(gain_grad)

        gain_grad[...] += jnp.sum(d * h, axis=0, keepdims=True)
        d = d * g[...]
        e[...] = d
        sums[...] = to_rows(
            jnp.sum(d, axis=1, keepdims=True), jnp.sum(d * h, axis=1, keepdims=True)
        )

    some = rows_of(height, chans)
    line = lanes(8, height)
    return call(
        body,
        "act_step",
        places,
        (frames // height,),
        [some, line, line, some, some, whole((1, chans))],
        [
            (shape((frames, chans), F32), some),
            (shape((frames, chans), F32), some),
            (shape((8, frames), F32), line),
            (shape((1, chans), F32), whole((1, chans))),
        ],
        [conv, mine, theirs, term, recv, gain],
        (),
        30 * frames * chans,
    )


def d_conv_step(places, e, hat, gain, mine, theirs, sums_mine, sums_theirs):
    frames, chans = e.shape
    height = LANES
    steps = frames // height

    def body(p, d, h, g, sm, st, um, ut, out, act, head, tail):
        _, inverse = merge(sm[...], st[...], chans)
        first, second = to_cols(um[...] + ut[...])
        width = 2 * chans
        got = (d[...] - first / width - h[...] * (second / width)) * inverse
        got = got.astype(BF16)
        out[...] = got
        scaled = h[...] * g[...]
        act[...] = (scaled * jax.nn.sigmoid(scaled)).astype(BF16)

        @pl.when(pl.program_id(0) == 0)
        def _():
            head[...] = got[:16]

        @pl.when(pl.program_id(0) == steps - 1)
        def _():
            tail[...] = got[height - 16 :]

    some = rows_of(height, chans)
    line = lanes(8, height)
    rim = (shape((16, chans), BF16), whole((16, chans)))
    return call(
        body,
        "d_conv_step",
        places,
        (steps,),
        [some, some, whole((1, chans)), line, line, line, line],
        [(shape((frames, chans), BF16), some)] * 2 + [rim, rim],
        [e, hat, gain, mine, theirs, sums_mine, sums_theirs],
        (),
        10 * frames * chans,
    )


def d_glu_step(places, before, d_conv, after, taps, sig, slope, own):
    frames, chans = d_conv.shape
    blocks = chans // LANES // 2

    def body(p, b, d, a, w, s, h, d_value, d_gate, wide):
        fill(wide, b, d, a)

        def chunk(i, carry):
            start = pl.multiple_of(i * STEP, STEP)
            total = jnp.zeros((STEP, LANES), F32)
            for r in range(8):
                x = wide[pl.ds(start + r + 1, STEP + 24), :]
                for q in range(4):
                    tap = 31 - (8 * q + r)
                    total = total + w[tap : tap + 1, :] * x[8 * q : 8 * q + STEP]
            quarter = frames // 4
            inner = jnp.where(start < 3 * quarter, start + quarter, start - 2 * quarter)
            there = jnp.where(start < quarter, start, inner)
            some = pl.ds(pl.multiple_of(there, STEP), STEP)
            d_value[some, :] = (total * s[some, :]).astype(BF16)
            d_gate[some, :] = (total * h[some, :]).astype(BF16)
            return carry

        lax.fori_loop(0, frames // STEP, chunk, 0)

    def pick(height):
        if own:
            return pl.BlockSpec((height, LANES), lambda i, p: (0, i + blocks * p[1]))
        return pl.BlockSpec((height, LANES), lambda i, p: (0, i + blocks * (1 - p[1])))

    out = (shape((frames, chans // 2), BF16), lanes(frames, LANES))
    return call(
        body,
        "d_glu_own" if own else "d_glu_other",
        places,
        (blocks,),
        [pick(16), pick(frames), pick(16), pick(32), pick(frames), pick(frames)],
        [out, out],
        [before, d_conv, after, taps, sig, slope],
        [pltpu.VMEM((frames + 32, LANES), F32)],
        32 * frames * chans,
    )


def taps_grad(places, before, glu, after, d_conv, scale):
    frames, chans = glu.shape
    part = 32

    def body(p, b, g, a, d, out, wide, sums):
        fill_edges_first(wide, b, g, a)
        sums[...] = jnp.zeros_like(sums)

        def chunk(i, carry):
            start = pl.multiple_of(i * part, part)
            mine = d[pl.ds(start, part), :].astype(F32)
            for r in range(8):
                x = wide[pl.ds(start + r, part + 24), :]
                for q in range(4):
                    both = mine * x[8 * q : 8 * q + part]
                    sums[8 * q + r] += jnp.sum(both.reshape(part // 8, 8, LANES), axis=0)
            return carry

        lax.fori_loop(0, frames // part, chunk, 0)
        out[...] = jnp.sum(sums[...], axis=1) * scale

    return call(
        body,
        "taps_grad",
        places,
        (chans // LANES,),
        [lanes(16, LANES), lanes(frames, LANES), lanes(16, LANES), lanes(frames, LANES)],
        [(shape((32, chans), F32), lanes(32, LANES))],
        [before, glu, after, d_conv],
        [pltpu.VMEM((frames + 32, LANES), F32), pltpu.VMEM((32, 8, LANES), F32)],
        64 * frames * chans,
    )[0]


def pair_grads(places, chips, mine, theirs, normed, normed_theirs, scale):
    frames, half = mine[0].shape
    width = normed.shape[1]
    step = 512

    def body(p, mv, mg, tv, tg, n, nt, out, turned):
        @pl.when(pl.program_id(0) == 0)
        def _():
            for k, (m, t) in enumerate(((mv, tv), (mg, tg))):
                turned[k, :, :frames] = m[...].T
                turned[k, :, frames:] = t[...].T

        for k in range(2):
            total = dot(turned[k, :, :frames], n[...], NN)
            total = total + dot(turned[k, :, frames:], nt[...], NN)
            out[:, k] = (total * scale).astype(BF16).reshape(chips, half // chips, step)

    dims = (chips, 2, half // chips)
    return call(
        body,
        "pair_grads",
        places,
        (width // step,),
        [whole((frames, half))] * 4 + [lanes(frames, step)] * 2,
        [(shape((*dims, width), BF16), pl.BlockSpec((*dims, step), lambda i, p: (0, 0, 0, i)))],
        [*mine, *theirs, normed, normed_theirs],
        [pltpu.VMEM((2, half, 2 * frames), BF16)],
        8 * half * width * frames,
    )[0]


def out_grads(places, cot, cot_theirs, acts, scale):
    chans, frames = cot.shape
    half = chans // 2

    def body(p, c, ct, a, b, a_theirs, b_theirs, out):
        first = pl.program_id(0) == 0
        left = jnp.where(first, a[...], b[...])
        right = jnp.where(first, a_theirs[...], b_theirs[...])
        total = dot(c[...], left, NN) + dot(ct[...], right, NN)
        out[...] = (total * scale).astype(BF16)

    out = (
        shape((half, 2 * chans), BF16),
        pl.BlockSpec((half, chans), lambda i, p: (0, jnp.where(i == 0, p[0], 1 - p[0]))),
    )
    return call(
        body,
        "out_grads",
        places,
        (2,),
        [pl.BlockSpec((half, frames), lambda i, p: (p[1], 0)), whole((half, frames))]
        + [whole((frames, chans))] * 4,
        [out],
        [cot, cot_theirs, *acts],
        (),
        8 * half * chans * frames,
    )[0]


def d_normed_terms(places, values, gates, value_weight, gate_weight):
    frames, half = values[0].shape
    chans = 2 * half

    def body(p, vo, vt, go, gt, wv, wg, theirs, mine):
        own = pl.ds(pl.multiple_of(p[1] * half, LANES), half)
        other = pl.ds(pl.multiple_of((1 - p[1]) * half, LANES), half)
        total = dot(vo[...], wv[own, :], NN) + dot(vt[...], wv[other, :], NN)
        total = total + dot(go[...], wg[own, :], NN) + dot(gt[...], wg[other, :], NN)

        @pl.when(pl.program_id(0) == 0)
        def _():
            theirs[...] = total.astype(BF16)

        @pl.when(pl.program_id(0) == 1)
        def _():
            mine[...] = total.astype(BF16)

    out = (shape((frames, chans), BF16), whole((frames, chans)))
    weight = pl.BlockSpec((chans, chans), lambda i, p: (0, jnp.where(i == 0, 1 - p[0], p[0])))
    return call(
        body,
        "d_normed_terms",
        places,
        (2,),
        [whole((frames, half))] * 4 + [weight] * 2,
        [out, out],
        [*values, *gates, value_weight, gate_weight],
        (),
        8 * chans * chans * frames,
    )


def norm_sums(places, term, recv, hat, gain):
    frames, chans = hat.shape
    height = LANES

    def body(p, tm, tr, h, g, sums, gain_grad):
        d = tm[...].astype(F32) + tr[...].astype(F32)

        @pl.when(pl.program_id(0) == 0)
        def _():
            gain_grad[...] = jnp.zeros_like(gain_grad)

        gain_grad[...] += jnp.sum(d * h[...], axis=0, keepdims=True)
        d = d * g[...]
        sums[...] = to_rows(
            jnp.sum(d, axis=1, keepdims=True), jnp.sum(d * h[...], axis=1, keepdims=True)
        )

    some = rows_of(height, chans)
    return call(
        body,
        "norm_sums",
        places,
        (frames // height,),
        [some, some, some, whole((1, chans))],
        [
            (shape((8, frames), F32), lanes(8, height)),
            (shape((1, chans), F32), whole((1, chans))),
        ],
        [term, recv, hat, gain],
        (),
        10 * frames * chans,
    )


def input_step(places, term, recv, hat, gain, inv, mine, theirs, cot):
    frames, chans = hat.shape
    height = LANES
    width = 2 * chans

    def body(p, tm, tr, h, g, i, um, ut, c, out):
        d = (tm[...].astype(F32) + tr[...].astype(F32)) * g[...]
        first, second = to_cols(um[...] + ut[...])
        got = (d - first / width - h[...] * (second / width)) * i[:, 0:1]
        out[...] = (c[...].astype(F32) + got.T).astype(BF16)

    some = rows_of(height, chans)
    line = lanes(8, height)
    block = pl.BlockSpec((chans, height), lambda i, p: (0, edges_first(i, frames // height)))
    return call(
        body,
        "input_step",
        places,
        (frames // height,),
        [some, some, some, whole((1, chans)), rows_of(height, LANES), line, line, block],
        [(shape((chans, frames), BF16), block)],
        [term, recv, hat, gain, inv, mine, theirs, cot],
        (),
        10 * frames * chans,
    )[0]


def out_step(places, frames_in, weight, act, act_theirs):
    chans, frames = frames_in.shape
    step = 256

    def body(p, x, w, a, b, out):
        own = pl.ds(pl.multiple_of(p[0] * chans, LANES), chans)
        other = pl.ds(pl.multiple_of((1 - p[0]) * chans, LANES), chans)
        total = dot(w[:, own], a[...], NT) + dot(w[:, other], b[...], NT)
        out[...] = (x[...].astype(F32) + total).astype(BF16)

    return call(
        body,
        "out_step",
        places,
        (chans // step,),
        [rows_of(step, frames), rows_of(step, 2 * chans)] + [whole((frames, chans))] * 2,
        [(shape((chans, frames), BF16), rows_of(step, frames))],
        [frames_in, weight, act, act_theirs],
        (),
        4 * chans * chans * frames,
    )[0]


def join_halves(places, pair, pair_theirs, single, single_theirs):
    chips, _, rows, cols = pair.shape

    def body(p, a, at, b, bt, *refs):
        outs, done = refs[:3], refs[3]
        copies = []
        for core, (two, one) in ((p[1], (a, b)), (1 - p[1], (at, bt))):
            for source, out in zip((two.at[:, 0], two.at[:, 1], one.at[:, 0]), outs):
                copies.append(pltpu.make_async_copy(source, out.at[core], done.at[len(copies)]))
        for copy in copies:
            copy.start()
        for copy in copies:
            copy.wait()

    anywhere = pl.BlockSpec(memory_space=pl.ANY)
    outs = call(
        body,
        "join_halves",
        places,
        (1,),
        [anywhere] * 4,
        [(shape((2, chips, rows, cols), BF16), anywhere)] * 3,
        [pair, pair_theirs, single, single_theirs],
        [pltpu.SemaphoreType.DMA((6,))],
    )
    return [out.reshape(2 * chips * rows, cols) for out in outs]


def ring_of(count):
    chips = count // 2
    if chips % 2 == 0:
        cols = chips // 2
        order = [2 * col for col in range(cols)] + [2 * col + 1 for col in reversed(range(cols))]
    else:
        order = list(range(chips))
    place = [0] * count
    ahead, behind = [], []
    for spot, chip in enumerate(order):
        after = order[(spot + 1) % chips]
        for core in range(2):
            place[2 * chip + core] = spot
            ahead.append((2 * chip + core, 2 * after + core))
            behind.append((2 * after + core, 2 * chip + core))
    return chips, place, ahead, behind


def pairs_of(count, step):
    return [(i, i ^ step) for i in range(count)]


def add(left, right):
    return (left.astype(F32) + right.astype(F32)).astype(BF16)


def ring_sum(sets):
    count = lax.axis_size("seq")
    chips, place, ahead, behind = ring_of(count)
    spot = jnp.asarray(place, jnp.int32)[lax.axis_index("seq")]
    reach = chips // 2

    def part(cells, step):
        return lax.dynamic_index_in_dim(cells, (spot + step + chips) % chips, 0, keepdims=False)

    def up(cells):
        return lax.ppermute(cells, "seq", ahead)

    def down(cells):
        return lax.ppermute(cells, "seq", behind)

    half = sets[0].shape[1] // 2
    flows = [(up(part(x, reach)[half:]), down(part(x, -reach)[:half])) for x in sets]
    for hop in range(reach - 1, 0, -1):
        later = []
        for x, (u, d) in zip(sets, flows):
            own_u, own_d = part(x, hop), part(x, -hop)
            if hop == reach - 1:
                u = jnp.concatenate([own_u[:half], add(own_u[half:], u)])
                d = jnp.concatenate([add(own_d[:half], d), own_d[half:]])
            else:
                u, d = add(own_u, u), add(own_d, d)
            later.append((up(u), down(d)))
        flows = later
    owns = [
        (part(x, 0).astype(F32) + u.astype(F32) + d.astype(F32)).astype(BF16)
        for x, (u, d) in zip(sets, flows)
    ]
    outs = []
    for x, own in zip(sets, owns):
        outs.append(lax.dynamic_update_index_in_dim(jnp.zeros_like(x), own, spot, 0))
    flows = [(own, own) for own in owns]
    for hop in range(1, reach):
        flows = [(up(u), down(d)) for u, d in flows]
        for i, (u, d) in enumerate(flows):
            out = lax.dynamic_update_index_in_dim(outs[i], u, (spot - hop + chips) % chips, 0)
            outs[i] = lax.dynamic_update_index_in_dim(out, d, (spot + hop) % chips, 0)
    for i, (u, d) in enumerate(flows):
        far = jnp.concatenate([down(d[:half]), up(u[half:])])
        outs[i] = lax.dynamic_update_index_in_dim(outs[i], far, (spot + reach) % chips, 0)
    return outs


def weight_sums(grads):
    count = lax.axis_size("seq")
    rows, cols = grads[0].shape
    chips = count // 2
    if count % 4 or rows % (2 * chips) or rows // (2 * chips) < 2:
        return [lax.psum(g.astype(BF16), "seq") for g in grads]
    core = lax.axis_index("seq") % 2
    swap = pairs_of(count, 1)
    half = rows // 2
    sets = []
    for g in grads:
        g = g.astype(BF16)
        theirs = lax.dynamic_slice_in_dim(g, (1 - core) * half, half, 0)
        mine = lax.dynamic_slice_in_dim(g, core * half, half, 0)
        mine = add(mine, lax.ppermute(theirs, "seq", swap))
        sets.append(mine.reshape(chips, half // chips, cols))
    outs = []
    for mine in ring_sum(sets):
        mine = mine.reshape(half, cols)
        theirs = lax.ppermute(mine, "seq", swap)
        outs.append(
            jnp.where(
                core == 0,
                jnp.concatenate([mine, theirs]),
                jnp.concatenate([theirs, mine]),
            )
        )
    return outs


def small_sum(values):
    count = lax.axis_size("seq")
    if count & (count - 1):
        return lax.psum(values, "seq"), []
    rests = []
    step = 1
    while step < count:
        values = values + lax.ppermute(values, "seq", pairs_of(count, step))
        rests.append(values)
        step *= 2
    return values, rests


def other(values):
    return lax.ppermute(values, "tp", [(0, 1), (1, 0)])


def tp_sum(values):
    if lax.axis_size("tp") == 2:
        return values + other(values)
    return lax.psum(values, "tp")


def tp_gather(values):
    if lax.axis_size("tp") == 2:
        theirs = other(values)
        first = lax.axis_index("tp") == 0
        return jnp.where(
            first, jnp.concatenate([values, theirs]), jnp.concatenate([theirs, values])
        )
    return lax.all_gather(values, "tp", axis=0, tiled=True)


def tp_scatter(term):
    term = term.astype(BF16)
    if lax.axis_size("tp") == 2:
        rows = term.shape[0] // 2
        me = lax.axis_index("tp")
        theirs = lax.dynamic_slice_in_dim(term, (1 - me) * rows, rows, 0)
        mine = lax.dynamic_slice_in_dim(term, me * rows, rows, 0)
        return mine.astype(F32) + other(theirs).astype(F32)
    return lax.psum_scatter(term, "tp", scatter_dimension=0, tiled=True).astype(F32)


def halo(cells, reach):
    count = lax.axis_size("seq")
    size = cells.shape[1]
    right = [(i, i + 1) for i in range(count - 1)]
    left = [(i + 1, i) for i in range(count - 1)]
    before = lax.ppermute(cells[:, size - reach :], "seq", right)
    after = lax.ppermute(cells[:, :reach], "seq", left)
    return jnp.concatenate([before, cells, after], axis=1)


def norm_back(d_hat, hat, inverse, width):
    sums = jnp.concatenate(
        [jnp.sum(d_hat, axis=0, keepdims=True), jnp.sum(d_hat * hat, axis=0, keepdims=True)]
    )
    sums = tp_sum(sums) / width
    return (d_hat - sums[:1] - hat * sums[1:]) * inverse


def contract_rows(left, right):
    return lax.dot_general(left, right, (((0,), (0,)), ((), ())), preferred_element_type=F32)


def contract_cols(left, right):
    return lax.dot_general(left, right, (((1,), (1,)), ((), ())), preferred_element_type=F32)


def plain(
    frames_in, norm_gain, value_weight, gate_weight, depth_kernel, conv_gain, out_weight, cotangent
):
    chans, row_count = frames_in.shape
    parts = lax.axis_size("tp")
    me = lax.axis_index("tp")
    width = chans * parts
    taps = depth_kernel.shape[1]
    reach = taps // 2
    scale = float(row_count * lax.axis_size("seq")) ** (-0.5)

    frames_all = tp_gather(frames_in)
    gain_all = lax.all_gather(norm_gain, "tp", axis=0, tiled=True)
    d_act = tp_scatter(contract_rows(out_weight, cotangent))

    wide = frames_all.astype(F32)
    centred = wide - jnp.mean(wide, axis=0, keepdims=True)
    inverse_in = lax.rsqrt(jnp.mean(centred * centred, axis=0, keepdims=True) + EPS)
    hat_all = centred * inverse_in
    normed_all = (hat_all * gain_all[:, None]).astype(BF16)
    value = jnp.dot(value_weight, normed_all, preferred_element_type=F32)
    gate = jnp.dot(gate_weight, normed_all, preferred_element_type=F32)
    gate_sig = jax.nn.sigmoid(gate)
    glu = (value * gate_sig).astype(BF16)
    glu_wide = halo(glu, reach).astype(F32)
    conv = jnp.zeros((chans, row_count), F32)
    for tap in range(taps):
        conv = conv + depth_kernel[:, tap : tap + 1] * glu_wide[:, tap : tap + row_count]

    mean = jnp.mean(conv, axis=0, keepdims=True)
    spread = jnp.sum((conv - mean) ** 2, axis=0, keepdims=True)
    if parts == 2:
        there = other(jnp.concatenate([mean, spread]))
        gap = mean - there[:1]
        mean = (mean + there[:1]) * 0.5
        spread = (spread + there[1:] + gap * gap * (chans * 0.5)) / width
    else:
        whole = lax.pmean(mean, "tp")
        spread = lax.psum(spread + chans * (mean - whole) ** 2, "tp") / width
        mean = whole
    inverse_conv = lax.rsqrt(spread + EPS)
    hat_conv = (conv - mean) * inverse_conv
    scaled = hat_conv * conv_gain[:, None]
    swish_sig = jax.nn.sigmoid(scaled)
    act = (scaled * swish_sig).astype(BF16)
    act_all = tp_gather(act)
    block_out = (
        frames_in.astype(F32) + jnp.dot(out_weight, act_all, preferred_element_type=F32)
    ).astype(BF16)
    grad_out = contract_cols(cotangent, act_all) * scale

    d_scaled = d_act * (swish_sig + scaled * swish_sig * (1.0 - swish_sig))
    grad_conv_gain = jnp.sum(d_scaled * hat_conv, axis=1) * scale
    d_conv = norm_back(d_scaled * conv_gain[:, None], hat_conv, inverse_conv, width).astype(BF16)
    d_conv_f = d_conv.astype(F32)
    d_conv_wide = halo(d_conv, reach).astype(F32)
    d_glu = jnp.zeros((chans, row_count), F32)
    kernel_cols = []
    for tap in range(taps):
        start = 2 * reach - tap
        d_glu = d_glu + depth_kernel[:, tap : tap + 1] * d_conv_wide[:, start : start + row_count]
        kernel_cols.append(jnp.sum(glu_wide[:, tap : tap + row_count] * d_conv_f, axis=1))
    grad_kernel = jnp.stack(kernel_cols, axis=0) * scale
    d_value = (d_glu * gate_sig).astype(BF16)
    d_gate = (d_glu * value * gate_sig * (1.0 - gate_sig)).astype(BF16)
    grad_value = contract_cols(d_value, normed_all) * scale
    grad_gate = contract_cols(d_gate, normed_all) * scale
    d_normed = tp_scatter(
        contract_rows(value_weight, d_value) + contract_rows(gate_weight, d_gate)
    )
    hat_in = lax.dynamic_slice_in_dim(hat_all, me * chans, chans, 0)
    grad_norm_gain = jnp.sum(d_normed * hat_in, axis=1) * scale
    input_grad = (
        cotangent.astype(F32) + norm_back(d_normed * norm_gain[:, None], hat_in, inverse_in, width)
    ).astype(BF16)
    small, _ = small_sum(
        jnp.concatenate([grad_kernel, grad_conv_gain[None], grad_norm_gain[None]], axis=0)
    )
    grad_out, grad_value, grad_gate = weight_sums([grad_out, grad_value, grad_gate])
    return (
        block_out,
        input_grad,
        small[taps + 1],
        grad_value,
        grad_gate,
        small[:taps].T,
        small[taps],
        grad_out,
    )


def core_swap(values):
    return lax.ppermute(values, "seq", pairs_of(lax.axis_size("seq"), 1))


def rims(tail, head):
    count = lax.axis_size("seq")
    before = lax.ppermute(tail, "seq", [(i, i + 1) for i in range(count - 1)])
    after = lax.ppermute(head, "seq", [(i + 1, i) for i in range(count - 1)])
    return before, after


def tied(values, *after):
    return lax.optimization_barrier((values, *after))[0]


class Ring:
    def __init__(self, cells, mirrored):
        self.chips, _, ahead, behind = ring_of(lax.axis_size("seq"))
        chip = lax.axis_index("seq") // 2
        self.spot = jnp.where(chip % 2 == 0, chip // 2, self.chips - 1 - chip // 2)
        self.reach = self.chips // 2
        self.ways = (behind, ahead) if mirrored else (ahead, behind)
        self.sign = -1 if mirrored else 1
        self.cells = cells
        self.count = 0
        self.here = ()
        self.extra = None

    def at(self, step):
        return (self.spot + self.sign * step + self.chips) % self.chips

    def part(self, step):
        return lax.dynamic_index_in_dim(self.cells, self.at(step), 0, keepdims=False)

    def put(self, some, step):
        rows = self.cells.shape[1]
        self.cells = lax.dynamic_update_index_in_dim(self.cells, some[:rows], self.at(step), 0)
        if self.extra is not None:
            self.gathered.append(some[rows:])

    def send(self, cells, after):
        if after:
            cells = lax.optimization_barrier((*cells, *after))[: len(cells)]
        self.sent = tuple(cells)
        self.here = tuple(lax.ppermute(x, "seq", way) for x, way in zip(cells, self.ways))

    def hop(self, *after):
        reach = self.reach
        self.count += 1
        left = reach + 1 - self.count
        if self.count == 1:
            self.send([self.part(reach)], after)
        elif left > 0:
            near = add(self.part(left), self.here[0])
            far = self.part(-left)
            if self.count > 2:
                far = add(far, self.here[1])
            self.send([near, far], after)
        else:
            cells = self.here
            if left == 0:
                own = sum((x.astype(F32) for x in cells), self.part(0).astype(F32)).astype(BF16)
                if self.extra is not None:
                    own = jnp.concatenate([own, self.extra])
                    self.gathered = []
                self.put(own, 0)
                cells = (own, own)
            if left == 1 - reach:
                cells = cells[:1]
            self.send(cells, after)
            for x, step in zip(self.here, (left - 1, 1 - left)):
                self.put(x, step)

    def gather(self, extra):
        self.extra = extra


def fused(
    frames_in, norm_gain, value_weight, gate_weight, depth_kernel, conv_gain, out_weight, cotangent
):
    chans, frames = frames_in.shape
    taps = depth_kernel.shape[1]
    half = chans // 2
    quarter = frames // 4
    count = lax.axis_size("seq")
    chips = count // 2
    scale = float(frames * count) ** (-0.5)
    place = lax.axis_index("seq")
    core = place % 2
    places = jnp.stack([lax.axis_index("tp"), core, place // 2 % 2, place // 4 % 2])
    places = places.astype(jnp.int32)

    gain = norm_gain[None]
    edges = pack_edges(places, frames_in, gain)
    edges_theirs = other(edges)
    middle = frames_in[:, quarter : 3 * quarter]
    middle_theirs = other(middle)
    taps_by = depth_kernel.T
    cot_half = lax.dynamic_slice_in_dim(cotangent, (1 - core) * half, half, 0)

    theirs, d_act_mine = d_act_terms(places, tied(cotangent, cot_half, middle), out_weight)
    cot_theirs = core_swap(cot_half)
    d_act_recv = other(theirs)

    weights = (value_weight, gate_weight)
    *held, edge = glu_forward(places, edges, tied(edges_theirs, theirs, cot_theirs), gain, edges_theirs, weights, ())
    before, after = rims(edge[1], edge[0])
    normed, hat_in, inv_in, glu, sig, slope, _ = glu_forward(
        places,
        middle,
        middle_theirs,
        gain,
        edges_theirs,
        weights,
        tuple(held),
    )
    conv, stats = conv_forward(places, before, glu, after, taps_by)
    normed_theirs = core_swap(normed)
    stats_theirs = other(stats)
    hat_conv, e, sums, gain_grad = act_step(
        places, conv, stats, stats_theirs, d_act_mine, d_act_recv, conv_gain[None]
    )
    sums_theirs = other(sums)
    d_conv, act, head, tail = d_conv_step(
        places, e, hat_conv, conv_gain[None], stats, stats_theirs, sums, sums_theirs
    )
    d_before, d_after = rims(tail, head)
    act_theirs = other(act)
    sent_v, sent_g = d_glu_step(places, d_before, d_conv, d_after, taps_by, sig, slope, False)
    recv_v, recv_g = core_swap(sent_v), core_swap(sent_g)
    own_v, own_g = d_glu_step(
        places, d_before, tied(d_conv, sent_v), d_after, taps_by, sig, slope, True
    )

    grads = pair_grads(
        places, chips, (own_v, own_g), (recv_v, recv_g), normed, normed_theirs, scale
    )
    a = Ring(grads.reshape(chips, -1, 2 * chans), False)
    a.hop()
    act, act_theirs = lax.optimization_barrier((act, act_theirs, grads))[:2]
    acts = [act, act_theirs, core_swap(act), core_swap(act_theirs)]
    grad_out = out_grads(places, cotangent, cot_theirs, acts, scale)
    b = Ring(grad_out.reshape(chips, -1, 2 * chans), True)

    def step(*after):
        there = a.here
        a.hop()
        b.hop(*after, *there)
        return (*a.sent, *b.sent)

    sent = step()
    own_v = tied(own_v, grad_out, *sent)
    theirs, mine = d_normed_terms(
        places, [own_v, sent_v], [own_g, sent_g], value_weight, gate_weight
    )
    recv = other(theirs)
    sent = step(theirs)
    kernel_grad = taps_grad(places, before, glu, after, tied(d_conv, theirs, *sent), scale)
    sent = step(kernel_grad)
    act_theirs = tied(act_theirs, kernel_grad, *sent)
    block_out = out_step(places, frames_in, out_weight, act, act_theirs)
    sent = step(block_out)
    sums_in, norm_grad = norm_sums(places, mine, tied(recv, block_out, *sent), hat_in, gain)
    sums_in_theirs = other(sums_in)
    small = jnp.concatenate([kernel_grad, gain_grad * scale, norm_grad * scale])
    small = small + core_swap(small)
    depth = (taps + 2 + 15) // 16 * 8
    small = jnp.pad(small, ((0, 2 * depth - taps - 2), (0, 0)))
    b.gather(jnp.concatenate([small[:depth], small[depth:]], axis=1).astype(BF16))
    sent = step()
    sums_in_theirs = tied(sums_in_theirs, *sent)
    input_grad = input_step(
        places, mine, recv, hat_in, gain, inv_in, sums_in, sums_in_theirs, cotangent
    )
    step(input_grad)
    step()
    b.hop()
    small = sum(some.astype(F32) for some in b.gathered)
    small = jnp.concatenate([small[:, :chans], small[:, chans:]])

    pair = a.cells.reshape(chips, 2, half // chips, 2 * chans)
    single = b.cells.reshape(chips, 1, half // chips, 2 * chans)
    grad_value, grad_gate, grad_out = join_halves(
        places, pair, core_swap(pair), single, core_swap(single)
    )
    return (
        block_out,
        input_grad,
        small[taps + 1],
        grad_value,
        grad_gate,
        small[:taps].T,
        small[taps],
        grad_out,
    )


def local(*arrays):
    chans, frames = arrays[0].shape
    taps = arrays[4].shape[1]
    count = lax.axis_size("seq")
    fits = lax.axis_size("tp") == 2 and taps == 32 and chans % 256 == 0 and frames % 512 == 0
    fits = fits and count == 16 and chans % (16 * count) == 0
    return (fused if fits else plain)(*arrays)


def solution(mesh):
    return jax.shard_map(
        local,
        mesh=mesh,
        in_specs=(
            P("tp", "seq"),
            P("tp"),
            P("tp", None),
            P("tp", None),
            P("tp", None),
            P("tp"),
            P("tp", None),
            P("tp", "seq"),
        ),
        out_specs=(
            P("tp", "seq"),
            P("tp", "seq"),
            P("tp"),
            P("tp", None),
            P("tp", None),
            P("tp", None),
            P("tp"),
            P("tp", None),
        ),
        check_vma=False,
    )
```

```python
import functools

import jax
import jax.numpy as jnp
from jax import lax
from jax.experimental import pallas as pl
from jax.experimental.pallas import tpu as pltpu
from jax.sharding import PartitionSpec as P

EPS = 1e-05
F32 = jnp.float32
BF16 = jnp.bfloat16
LANES = 128
REAL = ()


def dot(left, right, contract):
    return lax.dot_general(left, right, (contract, ((), ())), preferred_element_type=F32)


NT = ((1,), (1,))
NN = ((1,), (0,))
TN = ((0,), (0,))


def call(body, name, places, grid, ins, outs, args, scratch=(), flops=0, aliases=()):
    real = name in REAL
    size = sum(a.size * a.dtype.itemsize for a in args)
    size += sum(s.size * s.dtype.itemsize for s, _ in outs)
    return pl.pallas_call(
        body,
        out_shape=[s for s, _ in outs],
        grid_spec=pltpu.PrefetchScalarGridSpec(
            num_scalar_prefetch=1,
            grid=grid,
            in_specs=ins,
            out_specs=[b for _, b in outs],
            scratch_shapes=list(scratch),
        ),
        compiler_params=pltpu.CompilerParams(vmem_limit_bytes=24 * 2**20),
        cost_estimate=pl.CostEstimate(
            flops=flops if real else 1000, bytes_accessed=size if real else 1000, transcendentals=0
        ),
        input_output_aliases=dict(aliases),
        name=name,
    )(places, *args)


def shape(dims, kind):
    return jax.ShapeDtypeStruct(dims, kind)


def whole(dims):
    return pl.BlockSpec(dims, lambda i, p: (0,) * len(dims))


def lanes(rows, width):
    return pl.BlockSpec((rows, width), lambda i, p: (0, i))


def rows_of(height, cols):
    return pl.BlockSpec((height, cols), lambda i, p: (i, 0))


def d_act_terms(places, cotangent, weight):
    chans, frames = cotangent.shape

    def body(p, cot, w, theirs, mine, turned):
        @pl.when(pl.program_id(0) == 0)
        def _():
            turned[...] = cot[...].T
            theirs[...] = dot(turned[...], w[...], NN).astype(BF16)

        @pl.when(pl.program_id(0) == 1)
        def _():
            mine[...] = dot(turned[...], w[...], NN).astype(BF16)

    out = (shape((frames, chans), BF16), whole((frames, chans)))
    return call(
        body,
        "d_act_terms",
        places,
        (2,),
        [
            whole((chans, frames)),
            pl.BlockSpec((chans, chans), lambda i, p: (0, jnp.where(i == 0, 1 - p[0], p[0]))),
        ],
        [out, out],
        [cotangent, weight],
        [pltpu.VMEM((frames, chans), BF16)],
        4 * chans * chans * frames,
    )


def edges_first(index, count):
    quarter = count // 4
    inner = jnp.where(index < 2 * quarter, index + 2 * quarter, index - quarter)
    return jnp.where(index < quarter, index, inner)


def pack_edges(places, frames_in, gain):
    chans, frames = frames_in.shape
    quarter = frames // 4

    def body(p, first, last, g, out):
        out[:chans, :quarter] = first[...]
        out[:chans, quarter:] = last[...]
        out[chans:, :] = jnp.zeros_like(out[chans:, :])
        rest = g[...]
        rows = []
        for _ in range(3):
            term = rest.astype(BF16).astype(F32)
            rest = rest - term
            rows += [term[:, at : at + 2 * quarter] for at in range(0, chans, 2 * quarter)]
        rows.append(jnp.zeros((16 - len(rows), 2 * quarter), F32))
        out[chans:, :] = jnp.concatenate(rows).astype(BF16)

    return call(
        body,
        "pack_edges",
        places,
        (1,),
        [
            pl.BlockSpec((chans, quarter), lambda i, p: (0, 0)),
            pl.BlockSpec((chans, quarter), lambda i, p: (0, 3)),
            whole((1, chans)),
        ],
        [(shape((chans + 16, 2 * quarter), BF16), whole((chans + 16, 2 * quarter)))],
        [frames_in, frames_in, gain],
    )[0]


def glu_forward(places, mine, theirs, gain, packed, weights, held):
    chans, frames = mine.shape[0] // 16 * 16, mine.shape[1]
    if not held:
        chans = chans - 16
    width = 2 * chans
    step = 256
    half = 1 if held else 0

    def body(p, xm, xt, gm, gt, wv, wg, *refs):
        normed, hat, inv, glu, sig, slope, edge = refs[len(held) :]

        @pl.when(pl.program_id(0) == 0)
        def _():
            low = pl.multiple_of(p[0] * chans, LANES)
            high = pl.multiple_of((1 - p[0]) * chans, LANES)
            terms = gt[...].astype(F32)
            count = chans // frames
            gain_theirs = jnp.concatenate(
                [
                    terms[k : k + 1] + terms[count + k : count + k + 1]
                    + terms[2 * count + k : 2 * count + k + 1]
                    for k in range(count)
                ],
                axis=1,
            )
            for at in range(0, frames, LANES):
                some = pl.ds(at, LANES)
                a = xm[:chans, some].T.astype(F32)
                b = xt[:chans, some].T.astype(F32)
                total = jnp.sum(a, axis=1, keepdims=True) + jnp.sum(b, axis=1, keepdims=True)
                mean = total / width
                a = a - mean
                b = b - mean
                spread = jnp.sum(a * a, axis=1, keepdims=True)
                spread = spread + jnp.sum(b * b, axis=1, keepdims=True)
                scale = lax.rsqrt(spread / width + EPS)
                a = a * scale
                b = b * scale
                hat[some, :] = a
                inv[some, :] = jnp.broadcast_to(scale, (LANES, LANES))
                normed[some, pl.ds(low, chans)] = (a * gm[...]).astype(BF16)
                normed[some, pl.ds(high, chans)] = (b * gain_theirs).astype(BF16)

        value = dot(normed[...], wv[...], NT)
        gate = dot(normed[...], wg[...], NT)
        s = jax.nn.sigmoid(gate)
        g = (value * s).astype(BF16)
        glu[...] = g
        edge[0] = g[:16]
        edge[1] = g[frames - 16 :]
        sig[...] = s
        slope[...] = value * s * (1.0 - s)

    block = pl.BlockSpec((frames, step), lambda i, p: (half, i))

    def full(cols):
        return pl.BlockSpec((frames, cols), lambda i, p: (half, 0))

    return call(
        body,
        "glu_middle" if held else "glu_edges",
        places,
        (chans // step,),
        [whole(mine.shape)] * 2
        + [whole((1, chans)), pl.BlockSpec((16, frames), lambda i, p: (chans // 16, 0))]
        + [rows_of(step, width)] * 2
        + [pl.BlockSpec(memory_space=pl.ANY)] * len(held),
        [
            (shape((2 * frames, width), BF16), full(width)),
            (shape((2 * frames, chans), F32), full(chans)),
            (shape((2 * frames, LANES), F32), full(LANES)),
            (shape((2 * frames, chans), BF16), block),
            (shape((2 * frames, chans), F32), block),
            (shape((2 * frames, chans), F32), block),
            (shape((2, 16, chans), BF16), pl.BlockSpec((2, 16, step), lambda i, p: (0, 0, i))),
        ],
        [mine, theirs, gain, packed, *weights, *held],
        (),
        4 * chans * width * frames,
        [(7 + i, i) for i in range(len(held))],
    )


def fill_edges_first(wide, before, own, after):
    frames = own.shape[0]
    quarter = frames // 4
    wide[:16, :] = before[...].astype(F32)
    wide[16 : 16 + quarter, :] = own[:quarter, :].astype(F32)
    wide[16 + quarter : 16 + 3 * quarter, :] = own[2 * quarter :, :].astype(F32)
    wide[16 + 3 * quarter : 16 + frames, :] = own[quarter : 2 * quarter, :].astype(F32)
    wide[16 + frames :, :] = after[...].astype(F32)


def fill(wide, before, own, after):
    frames = own.shape[0]
    wide[:16, :] = before[...].astype(F32)
    wide[16 : 16 + frames, :] = own[...].astype(F32)
    wide[16 + frames :, :] = after[...].astype(F32)


def to_rows(first, second):
    size = first.shape[0]
    lane = lax.broadcasted_iota(jnp.int32, (size, LANES), 1)
    both = jnp.where(lane == 0, first, jnp.where(lane == 1, second, 0.0))
    return both.T[:8]


def to_cols(rows):
    turned = jnp.concatenate([rows] * (LANES // 8)).T
    return turned[:, 0:1], turned[:, 1:2]


STEP = 64


def conv_forward(places, before, glu, after, taps):
    frames, chans = glu.shape
    blocks = chans // LANES

    def body(p, b, g, a, w, conv, stats, wide):
        at = pl.program_id(0)
        fill_edges_first(wide, b, g, a)

        def chunk(i, carry):
            start = pl.multiple_of(i * STEP, STEP)
            total = jnp.zeros((STEP, LANES), F32)
            for r in range(8):
                x = wide[pl.ds(start + r, STEP + 24), :]
                for q in range(4):
                    tap = 8 * q + r
                    total = total + w[tap : tap + 1, :] * x[8 * q : 8 * q + STEP]
            conv[pl.ds(start, STEP), pl.ds(pl.multiple_of(at * LANES, LANES), LANES)] = total
            return carry

        lax.fori_loop(0, frames // STEP, chunk, 0)

        @pl.when(at == blocks - 1)
        def _():
            for low in range(0, frames, LANES):
                x = conv[low : low + LANES, :]
                mean = jnp.sum(x, axis=1, keepdims=True) / chans
                x = x - mean
                stats[:, low : low + LANES] = to_rows(mean, jnp.sum(x * x, axis=1, keepdims=True))

    return call(
        body,
        "conv_forward",
        places,
        (blocks,),
        [lanes(16, LANES), lanes(frames, LANES), lanes(16, LANES), lanes(32, LANES)],
        [
            (shape((frames, chans), F32), whole((frames, chans))),
            (shape((8, frames), F32), whole((8, frames))),
        ],
        [before, glu, after, taps],
        [pltpu.VMEM((frames + 32, LANES), F32)],
        64 * frames * chans,
    )


def merge(mine, theirs, chans):
    mean, spread = to_cols(mine)
    there, more = to_cols(theirs)
    gap = mean - there
    whole_spread = spread + more + gap * gap * (chans * 0.5)
    return (mean + there) * 0.5, lax.rsqrt(whole_spread / (2 * chans) + EPS)


def act_step(places, conv, mine, theirs, term, recv, gain):
    frames, chans = conv.shape
    height = LANES

    def body(p, x, sm, st, tm, tr, g, hat, e, sums, gain_grad):
        mean, inverse = merge(sm[...], st[...], chans)
        h = (x[...] - mean) * inverse
        hat[...] = h
        scaled = h * g[...]
        s = jax.nn.sigmoid(scaled)
        soft = scaled * s
        d = tm[...].astype(F32) + tr[...].astype(F32)
        d = d * (s + soft * (1.0 - s))

        @pl.when(pl.program_id(0) == 0)
        def _():
            gain_grad[...] = jnp.zeros_like(gain_grad)

        gain_grad[...] += jnp.sum(d * h, axis=0, keepdims=True)
        d = d * g[...]
        e[...] = d
        sums[...] = to_rows(
            jnp.sum(d, axis=1, keepdims=True), jnp.sum(d * h, axis=1, keepdims=True)
        )

    some = rows_of(height, chans)
    line = lanes(8, height)
    return call(
        body,
        "act_step",
        places,
        (frames // height,),
        [some, line, line, some, some, whole((1, chans))],
        [
            (shape((frames, chans), F32), some),
            (shape((frames, chans), F32), some),
            (shape((8, frames), F32), line),
            (shape((1, chans), F32), whole((1, chans))),
        ],
        [conv, mine, theirs, term, recv, gain],
        (),
        30 * frames * chans,
    )


def d_conv_step(places, e, hat, gain, mine, theirs, sums_mine, sums_theirs):
    frames, chans = e.shape
    height = LANES
    steps = frames // height

    def body(p, d, h, g, sm, st, um, ut, out, act, head, tail):
        _, inverse = merge(sm[...], st[...], chans)
        first, second = to_cols(um[...] + ut[...])
        width = 2 * chans
        got = (d[...] - first / width - h[...] * (second / width)) * inverse
        got = got.astype(BF16)
        out[...] = got
        scaled = h[...] * g[...]
        act[...] = (scaled * jax.nn.sigmoid(scaled)).astype(BF16)

        @pl.when(pl.program_id(0) == 0)
        def _():
            head[...] = got[:16]

        @pl.when(pl.program_id(0) == steps - 1)
        def _():
            tail[...] = got[height - 16 :]

    some = rows_of(height, chans)
    line = lanes(8, height)
    rim = (shape((16, chans), BF16), whole((16, chans)))
    return call(
        body,
        "d_conv_step",
        places,
        (steps,),
        [some, some, whole((1, chans)), line, line, line, line],
        [(shape((frames, chans), BF16), some)] * 2 + [rim, rim],
        [e, hat, gain, mine, theirs, sums_mine, sums_theirs],
        (),
        10 * frames * chans,
    )


def d_glu_step(places, before, d_conv, after, taps, sig, slope, own):
    frames, chans = d_conv.shape
    blocks = chans // LANES // 2

    def body(p, b, d, a, w, s, h, d_value, d_gate, wide):
        fill(wide, b, d, a)

        def chunk(i, carry):
            start = pl.multiple_of(i * STEP, STEP)
            total = jnp.zeros((STEP, LANES), F32)
            for r in range(8):
                x = wide[pl.ds(start + r + 1, STEP + 24), :]
                for q in range(4):
                    tap = 31 - (8 * q + r)
                    total = total + w[tap : tap + 1, :] * x[8 * q : 8 * q + STEP]
            quarter = frames // 4
            inner = jnp.where(start < 3 * quarter, start + quarter, start - 2 * quarter)
            there = jnp.where(start < quarter, start, inner)
            some = pl.ds(pl.multiple_of(there, STEP), STEP)
            d_value[some, :] = (total * s[some, :]).astype(BF16)
            d_gate[some, :] = (total * h[some, :]).astype(BF16)
            return carry

        lax.fori_loop(0, frames // STEP, chunk, 0)

    def pick(height):
        if own:
            return pl.BlockSpec((height, LANES), lambda i, p: (0, i + blocks * p[1]))
        return pl.BlockSpec((height, LANES), lambda i, p: (0, i + blocks * (1 - p[1])))

    out = (shape((frames, chans // 2), BF16), lanes(frames, LANES))
    return call(
        body,
        "d_glu_own" if own else "d_glu_other",
        places,
        (blocks,),
        [pick(16), pick(frames), pick(16), pick(32), pick(frames), pick(frames)],
        [out, out],
        [before, d_conv, after, taps, sig, slope],
        [pltpu.VMEM((frames + 32, LANES), F32)],
        32 * frames * chans,
    )


def taps_grad(places, before, glu, after, d_conv, scale):
    frames, chans = glu.shape
    part = 32

    def body(p, b, g, a, d, out, wide, sums):
        fill_edges_first(wide, b, g, a)
        sums[...] = jnp.zeros_like(sums)

        def chunk(i, carry):
            start = pl.multiple_of(i * part, part)
            mine = d[pl.ds(start, part), :].astype(F32)
            for r in range(8):
                x = wide[pl.ds(start + r, part + 24), :]
                for q in range(4):
                    both = mine * x[8 * q : 8 * q + part]
                    sums[8 * q + r] += jnp.sum(both.reshape(part // 8, 8, LANES), axis=0)
            return carry

        lax.fori_loop(0, frames // part, chunk, 0)
        out[...] = jnp.sum(sums[...], axis=1) * scale

    return call(
        body,
        "taps_grad",
        places,
        (chans // LANES,),
        [lanes(16, LANES), lanes(frames, LANES), lanes(16, LANES), lanes(frames, LANES)],
        [(shape((32, chans), F32), lanes(32, LANES))],
        [before, glu, after, d_conv],
        [pltpu.VMEM((frames + 32, LANES), F32), pltpu.VMEM((32, 8, LANES), F32)],
        64 * frames * chans,
    )[0]


def pair_grads(places, chips, mine, theirs, normed, normed_theirs, scale):
    frames, half = mine[0].shape
    width = normed.shape[1]
    step = 512

    def body(p, mv, mg, tv, tg, n, nt, out, turned):
        @pl.when(pl.program_id(0) == 0)
        def _():
            for k, (m, t) in enumerate(((mv, tv), (mg, tg))):
                turned[k, :, :frames] = m[...].T
                turned[k, :, frames:] = t[...].T

        for k in range(2):
            total = dot(turned[k, :, :frames], n[...], NN)
            total = total + dot(turned[k, :, frames:], nt[...], NN)
            out[:, k] = (total * scale).astype(BF16).reshape(chips, half // chips, step)

    dims = (chips, 2, half // chips)
    return call(
        body,
        "pair_grads",
        places,
        (width // step,),
        [whole((frames, half))] * 4 + [lanes(frames, step)] * 2,
        [(shape((*dims, width), BF16), pl.BlockSpec((*dims, step), lambda i, p: (0, 0, 0, i)))],
        [*mine, *theirs, normed, normed_theirs],
        [pltpu.VMEM((2, half, 2 * frames), BF16)],
        8 * half * width * frames,
    )[0]


def out_grads(places, cot, cot_theirs, acts, scale):
    chans, frames = cot.shape
    half = chans // 2

    def body(p, c, ct, a, b, a_theirs, b_theirs, out):
        first = pl.program_id(0) == 0
        left = jnp.where(first, a[...], b[...])
        right = jnp.where(first, a_theirs[...], b_theirs[...])
        total = dot(c[...], left, NN) + dot(ct[...], right, NN)
        out[...] = (total * scale).astype(BF16)

    out = (
        shape((half, 2 * chans), BF16),
        pl.BlockSpec((half, chans), lambda i, p: (0, jnp.where(i == 0, p[0], 1 - p[0]))),
    )
    return call(
        body,
        "out_grads",
        places,
        (2,),
        [pl.BlockSpec((half, frames), lambda i, p: (p[1], 0)), whole((half, frames))]
        + [whole((frames, chans))] * 4,
        [out],
        [cot, cot_theirs, *acts],
        (),
        8 * half * chans * frames,
    )[0]


def d_normed_terms(places, values, gates, value_weight, gate_weight):
    frames, half = values[0].shape
    chans = 2 * half

    def body(p, vo, vt, go, gt, wv, wg, theirs, mine):
        own = pl.ds(pl.multiple_of(p[1] * half, LANES), half)
        other = pl.ds(pl.multiple_of((1 - p[1]) * half, LANES), half)
        total = dot(vo[...], wv[own, :], NN) + dot(vt[...], wv[other, :], NN)
        total = total + dot(go[...], wg[own, :], NN) + dot(gt[...], wg[other, :], NN)

        @pl.when(pl.program_id(0) == 0)
        def _():
            theirs[...] = total.astype(BF16)

        @pl.when(pl.program_id(0) == 1)
        def _():
            mine[...] = total.astype(BF16)

    out = (shape((frames, chans), BF16), whole((frames, chans)))
    weight = pl.BlockSpec((chans, chans), lambda i, p: (0, jnp.where(i == 0, 1 - p[0], p[0])))
    return call(
        body,
        "d_normed_terms",
        places,
        (2,),
        [whole((frames, half))] * 4 + [weight] * 2,
        [out, out],
        [*values, *gates, value_weight, gate_weight],
        (),
        8 * chans * chans * frames,
    )


def norm_sums(places, term, recv, hat, gain):
    frames, chans = hat.shape
    height = LANES

    def body(p, tm, tr, h, g, sums, gain_grad):
        d = tm[...].astype(F32) + tr[...].astype(F32)

        @pl.when(pl.program_id(0) == 0)
        def _():
            gain_grad[...] = jnp.zeros_like(gain_grad)

        gain_grad[...] += jnp.sum(d * h[...], axis=0, keepdims=True)
        d = d * g[...]
        sums[...] = to_rows(
            jnp.sum(d, axis=1, keepdims=True), jnp.sum(d * h[...], axis=1, keepdims=True)
        )

    some = rows_of(height, chans)
    return call(
        body,
        "norm_sums",
        places,
        (frames // height,),
        [some, some, some, whole((1, chans))],
        [
            (shape((8, frames), F32), lanes(8, height)),
            (shape((1, chans), F32), whole((1, chans))),
        ],
        [term, recv, hat, gain],
        (),
        10 * frames * chans,
    )


def input_step(places, term, recv, hat, gain, inv, mine, theirs, cot):
    frames, chans = hat.shape
    height = LANES
    width = 2 * chans

    def body(p, tm, tr, h, g, i, um, ut, c, out):
        d = (tm[...].astype(F32) + tr[...].astype(F32)) * g[...]
        first, second = to_cols(um[...] + ut[...])
        got = (d - first / width - h[...] * (second / width)) * i[:, 0:1]
        out[...] = (c[...].astype(F32) + got.T).astype(BF16)

    some = rows_of(height, chans)
    line = lanes(8, height)
    block = pl.BlockSpec((chans, height), lambda i, p: (0, edges_first(i, frames // height)))
    return call(
        body,
        "input_step",
        places,
        (frames // height,),
        [some, some, some, whole((1, chans)), rows_of(height, LANES), line, line, block],
        [(shape((chans, frames), BF16), block)],
        [term, recv, hat, gain, inv, mine, theirs, cot],
        (),
        10 * frames * chans,
    )[0]


def out_step(places, frames_in, weight, act, act_theirs):
    chans, frames = frames_in.shape
    step = 256

    def body(p, x, w, a, b, out):
        own = pl.ds(pl.multiple_of(p[0] * chans, LANES), chans)
        other = pl.ds(pl.multiple_of((1 - p[0]) * chans, LANES), chans)
        total = dot(w[:, own], a[...], NT) + dot(w[:, other], b[...], NT)
        out[...] = (x[...].astype(F32) + total).astype(BF16)

    return call(
        body,
        "out_step",
        places,
        (chans // step,),
        [rows_of(step, frames), rows_of(step, 2 * chans)] + [whole((frames, chans))] * 2,
        [(shape((chans, frames), BF16), rows_of(step, frames))],
        [frames_in, weight, act, act_theirs],
        (),
        4 * chans * chans * frames,
    )[0]


def join_halves(places, pair, pair_theirs, single, single_theirs):
    chips, _, rows, cols = pair.shape

    def body(p, a, at, b, bt, *refs):
        outs, done = refs[:3], refs[3]
        copies = []
        for core, (two, one) in ((p[1], (a, b)), (1 - p[1], (at, bt))):
            for source, out in zip((two.at[:, 0], two.at[:, 1], one.at[:, 0]), outs):
                copies.append(pltpu.make_async_copy(source, out.at[core], done.at[len(copies)]))
        for copy in copies:
            copy.start()
        for copy in copies:
            copy.wait()

    anywhere = pl.BlockSpec(memory_space=pl.ANY)
    outs = call(
        body,
        "join_halves",
        places,
        (1,),
        [anywhere] * 4,
        [(shape((2, chips, rows, cols), BF16), anywhere)] * 3,
        [pair, pair_theirs, single, single_theirs],
        [pltpu.SemaphoreType.DMA((6,))],
    )
    return [out.reshape(2 * chips * rows, cols) for out in outs]


def ring_of(count):
    chips = count // 2
    if chips % 2 == 0:
        cols = chips // 2
        order = [2 * col for col in range(cols)] + [2 * col + 1 for col in reversed(range(cols))]
    else:
        order = list(range(chips))
    place = [0] * count
    ahead, behind = [], []
    for spot, chip in enumerate(order):
        after = order[(spot + 1) % chips]
        for core in range(2):
            place[2 * chip + core] = spot
            ahead.append((2 * chip + core, 2 * after + core))
            behind.append((2 * after + core, 2 * chip + core))
    return chips, place, ahead, behind


def pairs_of(count, step):
    return [(i, i ^ step) for i in range(count)]


def add(left, right):
    return (left.astype(F32) + right.astype(F32)).astype(BF16)


def ring_sum(sets):
    count = lax.axis_size("seq")
    chips, place, ahead, behind = ring_of(count)
    spot = jnp.asarray(place, jnp.int32)[lax.axis_index("seq")]
    reach = chips // 2

    def part(cells, step):
        return lax.dynamic_index_in_dim(cells, (spot + step + chips) % chips, 0, keepdims=False)

    def up(cells):
        return lax.ppermute(cells, "seq", ahead)

    def down(cells):
        return lax.ppermute(cells, "seq", behind)

    half = sets[0].shape[1] // 2
    flows = [(up(part(x, reach)[half:]), down(part(x, -reach)[:half])) for x in sets]
    for hop in range(reach - 1, 0, -1):
        later = []
        for x, (u, d) in zip(sets, flows):
            own_u, own_d = part(x, hop), part(x, -hop)
            if hop == reach - 1:
                u = jnp.concatenate([own_u[:half], add(own_u[half:], u)])
                d = jnp.concatenate([add(own_d[:half], d), own_d[half:]])
            else:
                u, d = add(own_u, u), add(own_d, d)
            later.append((up(u), down(d)))
        flows = later
    owns = [
        (part(x, 0).astype(F32) + u.astype(F32) + d.astype(F32)).astype(BF16)
        for x, (u, d) in zip(sets, flows)
    ]
    outs = []
    for x, own in zip(sets, owns):
        outs.append(lax.dynamic_update_index_in_dim(jnp.zeros_like(x), own, spot, 0))
    flows = [(own, own) for own in owns]
    for hop in range(1, reach):
        flows = [(up(u), down(d)) for u, d in flows]
        for i, (u, d) in enumerate(flows):
            out = lax.dynamic_update_index_in_dim(outs[i], u, (spot - hop + chips) % chips, 0)
            outs[i] = lax.dynamic_update_index_in_dim(out, d, (spot + hop) % chips, 0)
    for i, (u, d) in enumerate(flows):
        far = jnp.concatenate([down(d[:half]), up(u[half:])])
        outs[i] = lax.dynamic_update_index_in_dim(outs[i], far, (spot + reach) % chips, 0)
    return outs


def weight_sums(grads):
    count = lax.axis_size("seq")
    rows, cols = grads[0].shape
    chips = count // 2
    if count % 4 or rows % (2 * chips) or rows // (2 * chips) < 2:
        return [lax.psum(g.astype(BF16), "seq") for g in grads]
    core = lax.axis_index("seq") % 2
    swap = pairs_of(count, 1)
    half = rows // 2
    sets = []
    for g in grads:
        g = g.astype(BF16)
        theirs = lax.dynamic_slice_in_dim(g, (1 - core) * half, half, 0)
        mine = lax.dynamic_slice_in_dim(g, core * half, half, 0)
        mine = add(mine, lax.ppermute(theirs, "seq", swap))
        sets.append(mine.reshape(chips, half // chips, cols))
    outs = []
    for mine in ring_sum(sets):
        mine = mine.reshape(half, cols)
        theirs = lax.ppermute(mine, "seq", swap)
        outs.append(
            jnp.where(
                core == 0,
                jnp.concatenate([mine, theirs]),
                jnp.concatenate([theirs, mine]),
            )
        )
    return outs


def small_sum(values):
    count = lax.axis_size("seq")
    if count & (count - 1):
        return lax.psum(values, "seq"), []
    rests = []
    step = 1
    while step < count:
        values = values + lax.ppermute(values, "seq", pairs_of(count, step))
        rests.append(values)
        step *= 2
    return values, rests


def other(values):
    return lax.ppermute(values, "tp", [(0, 1), (1, 0)])


def tp_sum(values):
    if lax.axis_size("tp") == 2:
        return values + other(values)
    return lax.psum(values, "tp")


def tp_gather(values):
    if lax.axis_size("tp") == 2:
        theirs = other(values)
        first = lax.axis_index("tp") == 0
        return jnp.where(
            first, jnp.concatenate([values, theirs]), jnp.concatenate([theirs, values])
        )
    return lax.all_gather(values, "tp", axis=0, tiled=True)


def tp_scatter(term):
    term = term.astype(BF16)
    if lax.axis_size("tp") == 2:
        rows = term.shape[0] // 2
        me = lax.axis_index("tp")
        theirs = lax.dynamic_slice_in_dim(term, (1 - me) * rows, rows, 0)
        mine = lax.dynamic_slice_in_dim(term, me * rows, rows, 0)
        return mine.astype(F32) + other(theirs).astype(F32)
    return lax.psum_scatter(term, "tp", scatter_dimension=0, tiled=True).astype(F32)


def halo(cells, reach):
    count = lax.axis_size("seq")
    size = cells.shape[1]
    right = [(i, i + 1) for i in range(count - 1)]
    left = [(i + 1, i) for i in range(count - 1)]
    before = lax.ppermute(cells[:, size - reach :], "seq", right)
    after = lax.ppermute(cells[:, :reach], "seq", left)
    return jnp.concatenate([before, cells, after], axis=1)


def norm_back(d_hat, hat, inverse, width):
    sums = jnp.concatenate(
        [jnp.sum(d_hat, axis=0, keepdims=True), jnp.sum(d_hat * hat, axis=0, keepdims=True)]
    )
    sums = tp_sum(sums) / width
    return (d_hat - sums[:1] - hat * sums[1:]) * inverse


def contract_rows(left, right):
    return lax.dot_general(left, right, (((0,), (0,)), ((), ())), preferred_element_type=F32)


def contract_cols(left, right):
    return lax.dot_general(left, right, (((1,), (1,)), ((), ())), preferred_element_type=F32)


def plain(
    frames_in, norm_gain, value_weight, gate_weight, depth_kernel, conv_gain, out_weight, cotangent
):
    chans, row_count = frames_in.shape
    parts = lax.axis_size("tp")
    me = lax.axis_index("tp")
    width = chans * parts
    taps = depth_kernel.shape[1]
    reach = taps // 2
    scale = float(row_count * lax.axis_size("seq")) ** (-0.5)

    frames_all = tp_gather(frames_in)
    gain_all = lax.all_gather(norm_gain, "tp", axis=0, tiled=True)
    d_act = tp_scatter(contract_rows(out_weight, cotangent))

    wide = frames_all.astype(F32)
    centred = wide - jnp.mean(wide, axis=0, keepdims=True)
    inverse_in = lax.rsqrt(jnp.mean(centred * centred, axis=0, keepdims=True) + EPS)
    hat_all = centred * inverse_in
    normed_all = (hat_all * gain_all[:, None]).astype(BF16)
    value = jnp.dot(value_weight, normed_all, preferred_element_type=F32)
    gate = jnp.dot(gate_weight, normed_all, preferred_element_type=F32)
    gate_sig = jax.nn.sigmoid(gate)
    glu = (value * gate_sig).astype(BF16)
    glu_wide = halo(glu, reach).astype(F32)
    conv = jnp.zeros((chans, row_count), F32)
    for tap in range(taps):
        conv = conv + depth_kernel[:, tap : tap + 1] * glu_wide[:, tap : tap + row_count]

    mean = jnp.mean(conv, axis=0, keepdims=True)
    spread = jnp.sum((conv - mean) ** 2, axis=0, keepdims=True)
    if parts == 2:
        there = other(jnp.concatenate([mean, spread]))
        gap = mean - there[:1]
        mean = (mean + there[:1]) * 0.5
        spread = (spread + there[1:] + gap * gap * (chans * 0.5)) / width
    else:
        whole = lax.pmean(mean, "tp")
        spread = lax.psum(spread + chans * (mean - whole) ** 2, "tp") / width
        mean = whole
    inverse_conv = lax.rsqrt(spread + EPS)
    hat_conv = (conv - mean) * inverse_conv
    scaled = hat_conv * conv_gain[:, None]
    swish_sig = jax.nn.sigmoid(scaled)
    act = (scaled * swish_sig).astype(BF16)
    act_all = tp_gather(act)
    block_out = (
        frames_in.astype(F32) + jnp.dot(out_weight, act_all, preferred_element_type=F32)
    ).astype(BF16)
    grad_out = contract_cols(cotangent, act_all) * scale

    d_scaled = d_act * (swish_sig + scaled * swish_sig * (1.0 - swish_sig))
    grad_conv_gain = jnp.sum(d_scaled * hat_conv, axis=1) * scale
    d_conv = norm_back(d_scaled * conv_gain[:, None], hat_conv, inverse_conv, width).astype(BF16)
    d_conv_f = d_conv.astype(F32)
    d_conv_wide = halo(d_conv, reach).astype(F32)
    d_glu = jnp.zeros((chans, row_count), F32)
    kernel_cols = []
    for tap in range(taps):
        start = 2 * reach - tap
        d_glu = d_glu + depth_kernel[:, tap : tap + 1] * d_conv_wide[:, start : start + row_count]
        kernel_cols.append(jnp.sum(glu_wide[:, tap : tap + row_count] * d_conv_f, axis=1))
    grad_kernel = jnp.stack(kernel_cols, axis=0) * scale
    d_value = (d_glu * gate_sig).astype(BF16)
    d_gate = (d_glu * value * gate_sig * (1.0 - gate_sig)).astype(BF16)
    grad_value = contract_cols(d_value, normed_all) * scale
    grad_gate = contract_cols(d_gate, normed_all) * scale
    d_normed = tp_scatter(
        contract_rows(value_weight, d_value) + contract_rows(gate_weight, d_gate)
    )
    hat_in = lax.dynamic_slice_in_dim(hat_all, me * chans, chans, 0)
    grad_norm_gain = jnp.sum(d_normed * hat_in, axis=1) * scale
    input_grad = (
        cotangent.astype(F32) + norm_back(d_normed * norm_gain[:, None], hat_in, inverse_in, width)
    ).astype(BF16)
    small, _ = small_sum(
        jnp.concatenate([grad_kernel, grad_conv_gain[None], grad_norm_gain[None]], axis=0)
    )
    grad_out, grad_value, grad_gate = weight_sums([grad_out, grad_value, grad_gate])
    return (
        block_out,
        input_grad,
        small[taps + 1],
        grad_value,
        grad_gate,
        small[:taps].T,
        small[taps],
        grad_out,
    )


def core_swap(values):
    return lax.ppermute(values, "seq", pairs_of(lax.axis_size("seq"), 1))


def rims(tail, head):
    count = lax.axis_size("seq")
    before = lax.ppermute(tail, "seq", [(i, i + 1) for i in range(count - 1)])
    after = lax.ppermute(head, "seq", [(i + 1, i) for i in range(count - 1)])
    return before, after


def tied(values, *after):
    return lax.optimization_barrier((values, *after))[0]


class Ring:
    def __init__(self, cells, mirrored):
        self.chips, _, ahead, behind = ring_of(lax.axis_size("seq"))
        chip = lax.axis_index("seq") // 2
        self.spot = jnp.where(chip % 2 == 0, chip // 2, self.chips - 1 - chip // 2)
        self.reach = self.chips // 2
        self.ways = (behind, ahead) if mirrored else (ahead, behind)
        self.sign = -1 if mirrored else 1
        self.cells = cells
        self.count = 0
        self.here = ()
        self.extra = None

    def at(self, step):
        return (self.spot + self.sign * step + self.chips) % self.chips

    def part(self, step):
        return lax.dynamic_index_in_dim(self.cells, self.at(step), 0, keepdims=False)

    def put(self, some, step):
        rows = self.cells.shape[1]
        self.cells = lax.dynamic_update_index_in_dim(self.cells, some[:rows], self.at(step), 0)
        if self.extra is not None:
            self.gathered.append(some[rows:])

    def send(self, cells, after):
        if after:
            cells = lax.optimization_barrier((*cells, *after))[: len(cells)]
        self.sent = tuple(cells)
        self.here = tuple(lax.ppermute(x, "seq", way) for x, way in zip(cells, self.ways))

    def hop(self, *after):
        reach = self.reach
        self.count += 1
        left = reach + 1 - self.count
        if left > 0:
            cells = [self.part(left)]
            if left > 1:
                cells.append(self.part(1 - left))
            else:
                self.early = self.here[1]
            if self.count > 1:
                cells = [add(mine, there) for mine, there in zip(cells, self.here)]
            self.send(cells, after)
        else:
            cells = self.here
            if left == 0:
                own = self.part(0).astype(F32) + self.here[0].astype(F32)
                own = (own + self.early.astype(F32)).astype(BF16)
                if self.extra is not None:
                    own = jnp.concatenate([own, self.extra])
                    self.gathered = []
                self.put(own, 0)
                cells = (own, own)
            if left == 1 - reach:
                cells = cells[:1]
            self.send(cells, after)
            for x, step in zip(self.here, (left - 1, 1 - left)):
                self.put(x, step)

    def gather(self, extra):
        self.extra = extra


def fused(
    frames_in, norm_gain, value_weight, gate_weight, depth_kernel, conv_gain, out_weight, cotangent
):
    chans, frames = frames_in.shape
    taps = depth_kernel.shape[1]
    half = chans // 2
    quarter = frames // 4
    count = lax.axis_size("seq")
    chips = count // 2
    scale = float(frames * count) ** (-0.5)
    place = lax.axis_index("seq")
    core = place % 2
    places = jnp.stack([lax.axis_index("tp"), core, place // 2 % 2, place // 4 % 2])
    places = places.astype(jnp.int32)

    gain = norm_gain[None]
    edges = pack_edges(places, frames_in, gain)
    edges_theirs = other(edges)
    middle = frames_in[:, quarter : 3 * quarter]
    middle_theirs = other(middle)
    taps_by = depth_kernel.T
    cot_half = lax.dynamic_slice_in_dim(cotangent, (1 - core) * half, half, 0)

    theirs, d_act_mine = d_act_terms(places, tied(cotangent, cot_half, middle), out_weight)
    cot_theirs = core_swap(cot_half)
    d_act_recv = other(theirs)

    weights = (value_weight, gate_weight)
    *held, edge = glu_forward(places, edges, tied(edges_theirs, theirs, cot_theirs), gain, edges_theirs, weights, ())
    before, after = rims(edge[1], edge[0])
    normed, hat_in, inv_in, glu, sig, slope, _ = glu_forward(
        places,
        middle,
        middle_theirs,
        gain,
        edges_theirs,
        weights,
        tuple(held),
    )
    conv, stats = conv_forward(places, before, glu, after, taps_by)
    normed_theirs = core_swap(normed)
    stats_theirs = other(stats)
    hat_conv, e, sums, gain_grad = act_step(
        places, conv, stats, stats_theirs, d_act_mine, d_act_recv, conv_gain[None]
    )
    sums_theirs = other(sums)
    d_conv, act, head, tail = d_conv_step(
        places, e, hat_conv, conv_gain[None], stats, stats_theirs, sums, sums_theirs
    )
    d_before, d_after = rims(tail, head)
    act_theirs = other(act)
    sent_v, sent_g = d_glu_step(places, d_before, d_conv, d_after, taps_by, sig, slope, False)
    recv_v, recv_g = core_swap(sent_v), core_swap(sent_g)
    own_v, own_g = d_glu_step(
        places, d_before, tied(d_conv, sent_v), d_after, taps_by, sig, slope, True
    )

    grads = pair_grads(
        places, chips, (own_v, own_g), (recv_v, recv_g), normed, normed_theirs, scale
    )
    a = Ring(grads.reshape(chips, -1, 2 * chans), False)
    a.hop()
    act, act_theirs = lax.optimization_barrier((act, act_theirs, grads))[:2]
    acts = [act, act_theirs, core_swap(act), core_swap(act_theirs)]
    grad_out = out_grads(places, cotangent, cot_theirs, acts, scale)
    b = Ring(grad_out.reshape(chips, -1, 2 * chans), True)

    def step(*after):
        there = a.here
        a.hop()
        b.hop(*after, *there)
        return (*a.sent, *b.sent)

    sent = step()
    own_v = tied(own_v, grad_out, *sent)
    theirs, mine = d_normed_terms(
        places, [own_v, sent_v], [own_g, sent_g], value_weight, gate_weight
    )
    recv = other(theirs)
    sent = step(theirs)
    kernel_grad = taps_grad(places, before, glu, after, tied(d_conv, theirs, *sent), scale)
    sent = step(kernel_grad)
    sent = step()
    sums_in, norm_grad = norm_sums(places, mine, tied(recv, kernel_grad, *sent), hat_in, gain)
    sums_in_theirs = other(sums_in)
    small = jnp.concatenate([kernel_grad, gain_grad * scale, norm_grad * scale])
    small = small + core_swap(small)
    depth = (taps + 2 + 15) // 16 * 8
    small = jnp.pad(small, ((0, 2 * depth - taps - 2), (0, 0)))
    b.gather(jnp.concatenate([small[:depth], small[depth:]], axis=1).astype(BF16))
    sent = step()
    sums_in_theirs = tied(sums_in_theirs, *sent)
    input_grad = input_step(
        places, mine, recv, hat_in, gain, inv_in, sums_in, sums_in_theirs, cotangent
    )
    sent = step(input_grad)
    act_theirs = tied(act_theirs, kernel_grad, *sent)
    block_out = out_step(places, frames_in, out_weight, act, act_theirs)
    step(block_out)
    b.hop()
    small = sum(some.astype(F32) for some in b.gathered)
    small = jnp.concatenate([small[:, :chans], small[:, chans:]])

    pair = a.cells.reshape(chips, 2, half // chips, 2 * chans)
    single = b.cells.reshape(chips, 1, half // chips, 2 * chans)
    grad_value, grad_gate, grad_out = join_halves(
        places, pair, core_swap(pair), single, core_swap(single)
    )
    return (
        block_out,
        input_grad,
        small[taps + 1],
        grad_value,
        grad_gate,
        small[:taps].T,
        small[taps],
        grad_out,
    )


def local(*arrays):
    chans, frames = arrays[0].shape
    taps = arrays[4].shape[1]
    count = lax.axis_size("seq")
    fits = lax.axis_size("tp") == 2 and taps == 32 and chans % 256 == 0 and frames % 512 == 0
    fits = fits and count == 16 and chans % (16 * count) == 0
    return (fused if fits else plain)(*arrays)


def solution(mesh):
    return jax.shard_map(
        local,
        mesh=mesh,
        in_specs=(
            P("tp", "seq"),
            P("tp"),
            P("tp", None),
            P("tp", None),
            P("tp", None),
            P("tp"),
            P("tp", None),
            P("tp", "seq"),
        ),
        out_specs=(
            P("tp", "seq"),
            P("tp", "seq"),
            P("tp"),
            P("tp", None),
            P("tp", None),
            P("tp", None),
            P("tp"),
            P("tp", None),
        ),
        check_vma=False,
    )
```

```python
import functools

import jax
import jax.numpy as jnp
from jax import lax
from jax.experimental import pallas as pl
from jax.experimental.pallas import tpu as pltpu
from jax.sharding import PartitionSpec as P

EPS = 1e-05
F32 = jnp.float32
BF16 = jnp.bfloat16
LANES = 128
REAL = ()


def dot(left, right, contract):
    return lax.dot_general(left, right, (contract, ((), ())), preferred_element_type=F32)


NT = ((1,), (1,))
NN = ((1,), (0,))
TN = ((0,), (0,))


def call(body, name, places, grid, ins, outs, args, scratch=(), flops=0, aliases=()):
    real = name in REAL
    size = sum(a.size * a.dtype.itemsize for a in args)
    size += sum(s.size * s.dtype.itemsize for s, _ in outs)
    return pl.pallas_call(
        body,
        out_shape=[s for s, _ in outs],
        grid_spec=pltpu.PrefetchScalarGridSpec(
            num_scalar_prefetch=1,
            grid=grid,
            in_specs=ins,
            out_specs=[b for _, b in outs],
            scratch_shapes=list(scratch),
        ),
        compiler_params=pltpu.CompilerParams(vmem_limit_bytes=24 * 2**20),
        cost_estimate=pl.CostEstimate(
            flops=flops if real else 1000, bytes_accessed=size if real else 1000, transcendentals=0
        ),
        input_output_aliases=dict(aliases),
        name=name,
    )(places, *args)


def shape(dims, kind):
    return jax.ShapeDtypeStruct(dims, kind)


def whole(dims):
    return pl.BlockSpec(dims, lambda i, p: (0,) * len(dims))


def lanes(rows, width):
    return pl.BlockSpec((rows, width), lambda i, p: (0, i))


def rows_of(height, cols):
    return pl.BlockSpec((height, cols), lambda i, p: (i, 0))


def d_act_terms(places, cotangent, weight):
    chans, frames = cotangent.shape

    def body(p, cot, w, theirs, mine, turned):
        @pl.when(pl.program_id(0) == 0)
        def _():
            turned[...] = cot[...].T
            theirs[...] = dot(turned[...], w[...], NN).astype(BF16)

        @pl.when(pl.program_id(0) == 1)
        def _():
            mine[...] = dot(turned[...], w[...], NN).astype(BF16)

    out = (shape((frames, chans), BF16), whole((frames, chans)))
    return call(
        body,
        "d_act_terms",
        places,
        (2,),
        [
            whole((chans, frames)),
            pl.BlockSpec((chans, chans), lambda i, p: (0, jnp.where(i == 0, 1 - p[0], p[0]))),
        ],
        [out, out],
        [cotangent, weight],
        [pltpu.VMEM((frames, chans), BF16)],
        4 * chans * chans * frames,
    )


def edges_first(index, count):
    quarter = count // 4
    inner = jnp.where(index < 2 * quarter, index + 2 * quarter, index - quarter)
    return jnp.where(index < quarter, index, inner)


def pack_edges(places, frames_in, gain):
    chans, frames = frames_in.shape
    quarter = frames // 4

    def body(p, first, last, g, out):
        out[:chans, :quarter] = first[...]
        out[:chans, quarter:] = last[...]
        out[chans:, :] = jnp.zeros_like(out[chans:, :])
        rest = g[...].reshape(1, chans)
        rows = []
        for _ in range(3):
            term = rest.astype(BF16).astype(F32)
            rest = rest - term
            rows += [term[:, at : at + 2 * quarter] for at in range(0, chans, 2 * quarter)]
        rows.append(jnp.zeros((16 - len(rows), 2 * quarter), F32))
        out[chans:, :] = jnp.concatenate(rows).astype(BF16)

    return call(
        body,
        "pack_edges",
        places,
        (1,),
        [
            pl.BlockSpec((chans, quarter), lambda i, p: (0, 0)),
            pl.BlockSpec((chans, quarter), lambda i, p: (0, 3)),
            pl.BlockSpec((chans,), lambda i, p: (0,)),
        ],
        [(shape((chans + 16, 2 * quarter), BF16), whole((chans + 16, 2 * quarter)))],
        [frames_in, frames_in, gain],
    )[0]


def glu_forward(places, mine, theirs, gain, packed, weights, held):
    chans, frames = mine.shape[0] // 16 * 16, mine.shape[1]
    if not held:
        chans = chans - 16
    width = 2 * chans
    step = 256
    half = 1 if held else 0

    def body(p, xm, xt, gm, gt, wv, wg, *refs):
        normed, hat, inv, glu, sig, slope, edge = refs[len(held) :]

        @pl.when(pl.program_id(0) == 0)
        def _():
            low = pl.multiple_of(p[0] * chans, LANES)
            high = pl.multiple_of((1 - p[0]) * chans, LANES)
            terms = gt[...].astype(F32)
            count = chans // frames
            gain_theirs = jnp.concatenate(
                [
                    terms[k : k + 1] + terms[count + k : count + k + 1]
                    + terms[2 * count + k : 2 * count + k + 1]
                    for k in range(count)
                ],
                axis=1,
            )
            for at in range(0, frames, LANES):
                some = pl.ds(at, LANES)
                a = xm[:chans, some].T.astype(F32)
                b = xt[:chans, some].T.astype(F32)
                total = jnp.sum(a, axis=1, keepdims=True) + jnp.sum(b, axis=1, keepdims=True)
                mean = total / width
                a = a - mean
                b = b - mean
                spread = jnp.sum(a * a, axis=1, keepdims=True)
                spread = spread + jnp.sum(b * b, axis=1, keepdims=True)
                scale = lax.rsqrt(spread / width + EPS)
                a = a * scale
                b = b * scale
                hat[some, :] = a
                inv[some, :] = jnp.broadcast_to(scale, (LANES, LANES))
                normed[some, pl.ds(low, chans)] = (a * gm[...]).astype(BF16)
                normed[some, pl.ds(high, chans)] = (b * gain_theirs).astype(BF16)

        value = dot(normed[...], wv[...], NT)
        gate = dot(normed[...], wg[...], NT)
        s = jax.nn.sigmoid(gate)
        g = (value * s).astype(BF16)
        glu[...] = g
        edge[0] = g[:16]
        edge[1] = g[frames - 16 :]
        sig[...] = s
        slope[...] = value * s * (1.0 - s)

    block = pl.BlockSpec((frames, step), lambda i, p: (half, i))

    def full(cols):
        return pl.BlockSpec((frames, cols), lambda i, p: (half, 0))

    return call(
        body,
        "glu_middle" if held else "glu_edges",
        places,
        (chans // step,),
        [whole(mine.shape)] * 2
        + [whole((1, chans)), pl.BlockSpec((16, frames), lambda i, p: (chans // 16, 0))]
        + [rows_of(step, width)] * 2
        + [pl.BlockSpec(memory_space=pl.ANY)] * len(held),
        [
            (shape((2 * frames, width), BF16), full(width)),
            (shape((2 * frames, chans), F32), full(chans)),
            (shape((2 * frames, LANES), F32), full(LANES)),
            (shape((2 * frames, chans), BF16), block),
            (shape((2 * frames, chans), F32), block),
            (shape((2 * frames, chans), F32), block),
            (shape((2, 16, chans), BF16), pl.BlockSpec((2, 16, step), lambda i, p: (0, 0, i))),
        ],
        [mine, theirs, gain, packed, *weights, *held],
        (),
        4 * chans * width * frames,
        [(7 + i, i) for i in range(len(held))],
    )


def fill_edges_first(wide, before, own, after):
    frames = own.shape[0]
    quarter = frames // 4
    wide[:16, :] = before[...].astype(F32)
    wide[16 : 16 + quarter, :] = own[:quarter, :].astype(F32)
    wide[16 + quarter : 16 + 3 * quarter, :] = own[2 * quarter :, :].astype(F32)
    wide[16 + 3 * quarter : 16 + frames, :] = own[quarter : 2 * quarter, :].astype(F32)
    wide[16 + frames :, :] = after[...].astype(F32)


def fill(wide, before, own, after):
    frames = own.shape[0]
    wide[:16, :] = before[...].astype(F32)
    wide[16 : 16 + frames, :] = own[...].astype(F32)
    wide[16 + frames :, :] = after[...].astype(F32)


def to_rows(first, second):
    size = first.shape[0]
    lane = lax.broadcasted_iota(jnp.int32, (size, LANES), 1)
    both = jnp.where(lane == 0, first, jnp.where(lane == 1, second, 0.0))
    return both.T[:8]


def to_cols(rows):
    turned = jnp.concatenate([rows] * (LANES // 8)).T
    return turned[:, 0:1], turned[:, 1:2]


STEP = 128


def conv_forward(places, before, glu, after, taps):
    frames, chans = glu.shape
    blocks = chans // LANES

    def body(p, b, g, a, w, conv, stats, wide):
        at = pl.program_id(0)
        fill_edges_first(wide, b, g, a)

        def chunk(i, carry):
            start = pl.multiple_of(i * STEP, STEP)
            total = jnp.zeros((STEP, LANES), F32)
            for r in range(8):
                x = wide[pl.ds(start + r, STEP + 24), :]
                for q in range(4):
                    tap = 8 * q + r
                    total = total + w[tap : tap + 1, :] * x[8 * q : 8 * q + STEP]
            conv[pl.ds(start, STEP), pl.ds(pl.multiple_of(at * LANES, LANES), LANES)] = total
            return carry

        lax.fori_loop(0, frames // STEP, chunk, 0)

        @pl.when(at == blocks - 1)
        def _():
            for low in range(0, frames, LANES):
                x = conv[low : low + LANES, :]
                mean = jnp.sum(x, axis=1, keepdims=True) / chans
                x = x - mean
                stats[:, low : low + LANES] = to_rows(mean, jnp.sum(x * x, axis=1, keepdims=True))

    return call(
        body,
        "conv_forward",
        places,
        (blocks,),
        [lanes(16, LANES), lanes(frames, LANES), lanes(16, LANES), lanes(32, LANES)],
        [
            (shape((frames, chans), F32), whole((frames, chans))),
            (shape((8, frames), F32), whole((8, frames))),
        ],
        [before, glu, after, taps],
        [pltpu.VMEM((frames + 32, LANES), F32)],
        64 * frames * chans,
    )


def merge(mine, theirs, chans):
    mean, spread = to_cols(mine)
    there, more = to_cols(theirs)
    gap = mean - there
    whole_spread = spread + more + gap * gap * (chans * 0.5)
    return (mean + there) * 0.5, lax.rsqrt(whole_spread / (2 * chans) + EPS)


def act_step(places, conv, mine, theirs, term, recv, gain):
    frames, chans = conv.shape
    height = LANES

    def body(p, x, sm, st, tm, tr, g, hat, e, sums, gain_grad):
        mean, inverse = merge(sm[...], st[...], chans)
        h = (x[...] - mean) * inverse
        hat[...] = h
        scaled = h * g[...]
        s = jax.nn.sigmoid(scaled)
        soft = scaled * s
        d = tm[...].astype(F32) + tr[...].astype(F32)
        d = d * (s + soft * (1.0 - s))

        @pl.when(pl.program_id(0) == 0)
        def _():
            gain_grad[...] = jnp.zeros_like(gain_grad)

        gain_grad[...] += jnp.sum(d * h, axis=0, keepdims=True)
        d = d * g[...]
        e[...] = d
        sums[...] = to_rows(
            jnp.sum(d, axis=1, keepdims=True), jnp.sum(d * h, axis=1, keepdims=True)
        )

    some = rows_of(height, chans)
    line = lanes(8, height)
    return call(
        body,
        "act_step",
        places,
        (frames // height,),
        [some, line, line, some, some, whole((1, chans))],
        [
            (shape((frames, chans), F32), some),
            (shape((frames, chans), F32), some),
            (shape((8, frames), F32), line),
            (shape((1, chans), F32), whole((1, chans))),
        ],
        [conv, mine, theirs, term, recv, gain],
        (),
        30 * frames * chans,
    )


def d_conv_step(places, e, hat, gain, mine, theirs, sums_mine, sums_theirs):
    frames, chans = e.shape
    height = LANES
    steps = frames // height

    def body(p, d, h, g, sm, st, um, ut, out, act, head, tail):
        _, inverse = merge(sm[...], st[...], chans)
        first, second = to_cols(um[...] + ut[...])
        width = 2 * chans
        got = (d[...] - first / width - h[...] * (second / width)) * inverse
        got = got.astype(BF16)
        out[...] = got
        scaled = h[...] * g[...]
        act[...] = (scaled * jax.nn.sigmoid(scaled)).astype(BF16)

        @pl.when(pl.program_id(0) == 0)
        def _():
            head[...] = got[:16]

        @pl.when(pl.program_id(0) == steps - 1)
        def _():
            tail[...] = got[height - 16 :]

    some = rows_of(height, chans)
    line = lanes(8, height)
    rim = (shape((16, chans), BF16), whole((16, chans)))
    return call(
        body,
        "d_conv_step",
        places,
        (steps,),
        [some, some, whole((1, chans)), line, line, line, line],
        [(shape((frames, chans), BF16), some)] * 2 + [rim, rim],
        [e, hat, gain, mine, theirs, sums_mine, sums_theirs],
        (),
        10 * frames * chans,
    )


def d_glu_step(places, before, d_conv, after, taps, sig, slope, own):
    frames, chans = d_conv.shape
    blocks = chans // LANES // 2

    def body(p, b, d, a, w, s, h, d_value, d_gate, wide):
        fill(wide, b, d, a)

        def chunk(i, carry):
            start = pl.multiple_of(i * STEP, STEP)
            total = jnp.zeros((STEP, LANES), F32)
            for r in range(8):
                x = wide[pl.ds(start + r + 1, STEP + 24), :]
                for q in range(4):
                    tap = 31 - (8 * q + r)
                    total = total + w[tap : tap + 1, :] * x[8 * q : 8 * q + STEP]
            quarter = frames // 4
            inner = jnp.where(start < 3 * quarter, start + quarter, start - 2 * quarter)
            there = jnp.where(start < quarter, start, inner)
            some = pl.ds(pl.multiple_of(there, STEP), STEP)
            d_value[some, :] = (total * s[some, :]).astype(BF16)
            d_gate[some, :] = (total * h[some, :]).astype(BF16)
            return carry

        lax.fori_loop(0, frames // STEP, chunk, 0)

    def pick(height):
        if own:
            return pl.BlockSpec((height, LANES), lambda i, p: (0, i + blocks * p[1]))
        return pl.BlockSpec((height, LANES), lambda i, p: (0, i + blocks * (1 - p[1])))

    out = (shape((frames, chans // 2), BF16), lanes(frames, LANES))
    return call(
        body,
        "d_glu_own" if own else "d_glu_other",
        places,
        (blocks,),
        [pick(16), pick(frames), pick(16), pick(32), pick(frames), pick(frames)],
        [out, out],
        [before, d_conv, after, taps, sig, slope],
        [pltpu.VMEM((frames + 32, LANES), F32)],
        32 * frames * chans,
    )


def taps_grad(places, before, glu, after, d_conv, scale):
    frames, chans = glu.shape
    part = 32

    def body(p, b, g, a, d, out, wide, sums):
        fill_edges_first(wide, b, g, a)
        sums[...] = jnp.zeros_like(sums)

        def chunk(i, carry):
            start = pl.multiple_of(i * part, part)
            mine = d[pl.ds(start, part), :].astype(F32)
            for r in range(8):
                x = wide[pl.ds(start + r, part + 24), :]
                for q in range(4):
                    both = mine * x[8 * q : 8 * q + part]
                    sums[8 * q + r] += jnp.sum(both.reshape(part // 8, 8, LANES), axis=0)
            return carry

        lax.fori_loop(0, frames // part, chunk, 0)
        out[...] = jnp.sum(sums[...], axis=1) * scale

    return call(
        body,
        "taps_grad",
        places,
        (chans // LANES,),
        [lanes(16, LANES), lanes(frames, LANES), lanes(16, LANES), lanes(frames, LANES)],
        [(shape((32, chans), F32), lanes(32, LANES))],
        [before, glu, after, d_conv],
        [pltpu.VMEM((frames + 32, LANES), F32), pltpu.VMEM((32, 8, LANES), F32)],
        64 * frames * chans,
    )[0]


def pair_grads(places, chips, mine, theirs, normed, normed_theirs, scale):
    frames, half = mine[0].shape
    width = normed.shape[1]
    step = width // 2

    def body(p, mv, mg, tv, tg, n, nt, out, turned):
        @pl.when(pl.program_id(0) == 0)
        def _():
            for k, (m, t) in enumerate(((mv, tv), (mg, tg))):
                turned[k, :, :frames] = m[...].T
                turned[k, :, frames:] = t[...].T

        for k in range(2):
            total = dot(turned[k, :, :frames], n[...], NN)
            total = total + dot(turned[k, :, frames:], nt[...], NN)
            out[:, k] = (total * scale).astype(BF16).reshape(chips, half // chips, step)

    dims = (chips, 2, half // chips)
    return call(
        body,
        "pair_grads",
        places,
        (width // step,),
        [whole((frames, half))] * 4 + [lanes(frames, step)] * 2,
        [(shape((*dims, width), BF16), pl.BlockSpec((*dims, step), lambda i, p: (0, 0, 0, i)))],
        [*mine, *theirs, normed, normed_theirs],
        [pltpu.VMEM((2, half, 2 * frames), BF16)],
        8 * half * width * frames,
    )[0]


def out_grads(places, cot, cot_theirs, acts, scale):
    chans, frames = cot.shape
    half = chans // 2

    def body(p, c, ct, a, b, a_theirs, b_theirs, out):
        first = pl.program_id(0) == 0
        left = jnp.where(first, a[...], b[...])
        right = jnp.where(first, a_theirs[...], b_theirs[...])
        total = dot(c[...], left, NN) + dot(ct[...], right, NN)
        out[...] = (total * scale).astype(BF16)

    out = (
        shape((half, 2 * chans), BF16),
        pl.BlockSpec((half, chans), lambda i, p: (0, jnp.where(i == 0, p[0], 1 - p[0]))),
    )
    return call(
        body,
        "out_grads",
        places,
        (2,),
        [pl.BlockSpec((half, frames), lambda i, p: (p[1], 0)), whole((half, frames))]
        + [whole((frames, chans))] * 4,
        [out],
        [cot, cot_theirs, *acts],
        (),
        8 * half * chans * frames,
    )[0]


def d_normed_terms(places, values, gates, value_weight, gate_weight):
    frames, half = values[0].shape
    chans = 2 * half

    def body(p, vo, vt, go, gt, wv, wg, theirs, mine):
        own = pl.ds(pl.multiple_of(p[1] * half, LANES), half)
        other = pl.ds(pl.multiple_of((1 - p[1]) * half, LANES), half)
        total = dot(vo[...], wv[own, :], NN) + dot(vt[...], wv[other, :], NN)
        total = total + dot(go[...], wg[own, :], NN) + dot(gt[...], wg[other, :], NN)

        @pl.when(pl.program_id(0) == 0)
        def _():
            theirs[...] = total.astype(BF16)

        @pl.when(pl.program_id(0) == 1)
        def _():
            mine[...] = total.astype(BF16)

    out = (shape((frames, chans), BF16), whole((frames, chans)))
    weight = pl.BlockSpec((chans, chans), lambda i, p: (0, jnp.where(i == 0, 1 - p[0], p[0])))
    return call(
        body,
        "d_normed_terms",
        places,
        (2,),
        [whole((frames, half))] * 4 + [weight] * 2,
        [out, out],
        [*values, *gates, value_weight, gate_weight],
        (),
        8 * chans * chans * frames,
    )


def norm_sums(places, term, recv, hat, gain):
    frames, chans = hat.shape
    height = LANES

    def body(p, tm, tr, h, g, sums, gain_grad):
        d = tm[...].astype(F32) + tr[...].astype(F32)

        @pl.when(pl.program_id(0) == 0)
        def _():
            gain_grad[...] = jnp.zeros_like(gain_grad)

        gain_grad[...] += jnp.sum(d * h[...], axis=0, keepdims=True)
        d = d * g[...]
        sums[...] = to_rows(
            jnp.sum(d, axis=1, keepdims=True), jnp.sum(d * h[...], axis=1, keepdims=True)
        )

    some = rows_of(height, chans)
    return call(
        body,
        "norm_sums",
        places,
        (frames // height,),
        [some, some, some, whole((1, chans))],
        [
            (shape((8, frames), F32), lanes(8, height)),
            (shape((1, chans), F32), whole((1, chans))),
        ],
        [term, recv, hat, gain],
        (),
        10 * frames * chans,
    )


def input_step(places, term, recv, hat, gain, inv, mine, theirs, cot):
    frames, chans = hat.shape
    height = LANES
    width = 2 * chans

    def body(p, tm, tr, h, g, i, um, ut, c, out):
        d = (tm[...].astype(F32) + tr[...].astype(F32)) * g[...]
        first, second = to_cols(um[...] + ut[...])
        got = (d - first / width - h[...] * (second / width)) * i[:, 0:1]
        out[...] = (c[...].astype(F32) + got.T).astype(BF16)

    some = rows_of(height, chans)
    line = lanes(8, height)
    block = pl.BlockSpec((chans, height), lambda i, p: (0, edges_first(i, frames // height)))
    return call(
        body,
        "input_step",
        places,
        (frames // height,),
        [some, some, some, whole((1, chans)), rows_of(height, LANES), line, line, block],
        [(shape((chans, frames), BF16), block)],
        [term, recv, hat, gain, inv, mine, theirs, cot],
        (),
        10 * frames * chans,
    )[0]


def out_step(places, frames_in, weight, act, act_theirs):
    chans, frames = frames_in.shape
    step = 256

    def body(p, x, w, a, b, out):
        own = pl.ds(pl.multiple_of(p[0] * chans, LANES), chans)
        other = pl.ds(pl.multiple_of((1 - p[0]) * chans, LANES), chans)
        total = dot(w[:, own], a[...], NT) + dot(w[:, other], b[...], NT)
        out[...] = (x[...].astype(F32) + total).astype(BF16)

    return call(
        body,
        "out_step",
        places,
        (chans // step,),
        [rows_of(step, frames), rows_of(step, 2 * chans)] + [whole((frames, chans))] * 2,
        [(shape((chans, frames), BF16), rows_of(step, frames))],
        [frames_in, weight, act, act_theirs],
        (),
        4 * chans * chans * frames,
    )[0]


def join_halves(places, pair, pair_theirs, single, single_theirs):
    chips, _, rows, cols = pair.shape

    def body(p, a, at, b, bt, *refs):
        outs, done = refs[:3], refs[3]
        copies = []
        for core, (two, one) in ((p[1], (a, b)), (1 - p[1], (at, bt))):
            for source, out in zip((two.at[:, 0], two.at[:, 1], one.at[:, 0]), outs):
                copies.append(pltpu.make_async_copy(source, out.at[core], done.at[len(copies)]))
        for copy in copies:
            copy.start()
        for copy in copies:
            copy.wait()

    anywhere = pl.BlockSpec(memory_space=pl.ANY)
    outs = call(
        body,
        "join_halves",
        places,
        (1,),
        [anywhere] * 4,
        [(shape((2, chips, rows, cols), BF16), anywhere)] * 3,
        [pair, pair_theirs, single, single_theirs],
        [pltpu.SemaphoreType.DMA((6,))],
    )
    return [out.reshape(2 * chips * rows, cols) for out in outs]


def ring_of(count):
    chips = count // 2
    if chips % 2 == 0:
        cols = chips // 2
        order = [2 * col for col in range(cols)] + [2 * col + 1 for col in reversed(range(cols))]
    else:
        order = list(range(chips))
    place = [0] * count
    ahead, behind = [], []
    for spot, chip in enumerate(order):
        after = order[(spot + 1) % chips]
        for core in range(2):
            place[2 * chip + core] = spot
            ahead.append((2 * chip + core, 2 * after + core))
            behind.append((2 * after + core, 2 * chip + core))
    return chips, place, ahead, behind


def pairs_of(count, step):
    return [(i, i ^ step) for i in range(count)]


def add(left, right):
    return (left.astype(F32) + right.astype(F32)).astype(BF16)


def ring_sum(sets):
    count = lax.axis_size("seq")
    chips, place, ahead, behind = ring_of(count)
    spot = jnp.asarray(place, jnp.int32)[lax.axis_index("seq")]
    reach = chips // 2

    def part(cells, step):
        return lax.dynamic_index_in_dim(cells, (spot + step + chips) % chips, 0, keepdims=False)

    def up(cells):
        return lax.ppermute(cells, "seq", ahead)

    def down(cells):
        return lax.ppermute(cells, "seq", behind)

    half = sets[0].shape[1] // 2
    flows = [(up(part(x, reach)[half:]), down(part(x, -reach)[:half])) for x in sets]
    for hop in range(reach - 1, 0, -1):
        later = []
        for x, (u, d) in zip(sets, flows):
            own_u, own_d = part(x, hop), part(x, -hop)
            if hop == reach - 1:
                u = jnp.concatenate([own_u[:half], add(own_u[half:], u)])
                d = jnp.concatenate([add(own_d[:half], d), own_d[half:]])
            else:
                u, d = add(own_u, u), add(own_d, d)
            later.append((up(u), down(d)))
        flows = later
    owns = [
        (part(x, 0).astype(F32) + u.astype(F32) + d.astype(F32)).astype(BF16)
        for x, (u, d) in zip(sets, flows)
    ]
    outs = []
    for x, own in zip(sets, owns):
        outs.append(lax.dynamic_update_index_in_dim(jnp.zeros_like(x), own, spot, 0))
    flows = [(own, own) for own in owns]
    for hop in range(1, reach):
        flows = [(up(u), down(d)) for u, d in flows]
        for i, (u, d) in enumerate(flows):
            out = lax.dynamic_update_index_in_dim(outs[i], u, (spot - hop + chips) % chips, 0)
            outs[i] = lax.dynamic_update_index_in_dim(out, d, (spot + hop) % chips, 0)
    for i, (u, d) in enumerate(flows):
        far = jnp.concatenate([down(d[:half]), up(u[half:])])
        outs[i] = lax.dynamic_update_index_in_dim(outs[i], far, (spot + reach) % chips, 0)
    return outs


def weight_sums(grads):
    count = lax.axis_size("seq")
    rows, cols = grads[0].shape
    chips = count // 2
    if count % 4 or rows % (2 * chips) or rows // (2 * chips) < 2:
        return [lax.psum(g.astype(BF16), "seq") for g in grads]
    core = lax.axis_index("seq") % 2
    swap = pairs_of(count, 1)
    half = rows // 2
    sets = []
    for g in grads:
        g = g.astype(BF16)
        theirs = lax.dynamic_slice_in_dim(g, (1 - core) * half, half, 0)
        mine = lax.dynamic_slice_in_dim(g, core * half, half, 0)
        mine = add(mine, lax.ppermute(theirs, "seq", swap))
        sets.append(mine.reshape(chips, half // chips, cols))
    outs = []
    for mine in ring_sum(sets):
        mine = mine.reshape(half, cols)
        theirs = lax.ppermute(mine, "seq", swap)
        outs.append(
            jnp.where(
                core == 0,
                jnp.concatenate([mine, theirs]),
                jnp.concatenate([theirs, mine]),
            )
        )
    return outs


def small_sum(values):
    count = lax.axis_size("seq")
    if count & (count - 1):
        return lax.psum(values, "seq"), []
    rests = []
    step = 1
    while step < count:
        values = values + lax.ppermute(values, "seq", pairs_of(count, step))
        rests.append(values)
        step *= 2
    return values, rests


def other(values):
    return lax.ppermute(values, "tp", [(0, 1), (1, 0)])


def tp_sum(values):
    if lax.axis_size("tp") == 2:
        return values + other(values)
    return lax.psum(values, "tp")


def tp_gather(values):
    if lax.axis_size("tp") == 2:
        theirs = other(values)
        first = lax.axis_index("tp") == 0
        return jnp.where(
            first, jnp.concatenate([values, theirs]), jnp.concatenate([theirs, values])
        )
    return lax.all_gather(values, "tp", axis=0, tiled=True)


def tp_scatter(term):
    term = term.astype(BF16)
    if lax.axis_size("tp") == 2:
        rows = term.shape[0] // 2
        me = lax.axis_index("tp")
        theirs = lax.dynamic_slice_in_dim(term, (1 - me) * rows, rows, 0)
        mine = lax.dynamic_slice_in_dim(term, me * rows, rows, 0)
        return mine.astype(F32) + other(theirs).astype(F32)
    return lax.psum_scatter(term, "tp", scatter_dimension=0, tiled=True).astype(F32)


def halo(cells, reach):
    count = lax.axis_size("seq")
    size = cells.shape[1]
    right = [(i, i + 1) for i in range(count - 1)]
    left = [(i + 1, i) for i in range(count - 1)]
    before = lax.ppermute(cells[:, size - reach :], "seq", right)
    after = lax.ppermute(cells[:, :reach], "seq", left)
    return jnp.concatenate([before, cells, after], axis=1)


def norm_back(d_hat, hat, inverse, width):
    sums = jnp.concatenate(
        [jnp.sum(d_hat, axis=0, keepdims=True), jnp.sum(d_hat * hat, axis=0, keepdims=True)]
    )
    sums = tp_sum(sums) / width
    return (d_hat - sums[:1] - hat * sums[1:]) * inverse


def contract_rows(left, right):
    return lax.dot_general(left, right, (((0,), (0,)), ((), ())), preferred_element_type=F32)


def contract_cols(left, right):
    return lax.dot_general(left, right, (((1,), (1,)), ((), ())), preferred_element_type=F32)


def plain(
    frames_in, norm_gain, value_weight, gate_weight, depth_kernel, conv_gain, out_weight, cotangent
):
    chans, row_count = frames_in.shape
    parts = lax.axis_size("tp")
    me = lax.axis_index("tp")
    width = chans * parts
    taps = depth_kernel.shape[1]
    reach = taps // 2
    scale = float(row_count * lax.axis_size("seq")) ** (-0.5)

    frames_all = tp_gather(frames_in)
    gain_all = lax.all_gather(norm_gain, "tp", axis=0, tiled=True)
    d_act = tp_scatter(contract_rows(out_weight, cotangent))

    wide = frames_all.astype(F32)
    centred = wide - jnp.mean(wide, axis=0, keepdims=True)
    inverse_in = lax.rsqrt(jnp.mean(centred * centred, axis=0, keepdims=True) + EPS)
    hat_all = centred * inverse_in
    normed_all = (hat_all * gain_all[:, None]).astype(BF16)
    value = jnp.dot(value_weight, normed_all, preferred_element_type=F32)
    gate = jnp.dot(gate_weight, normed_all, preferred_element_type=F32)
    gate_sig = jax.nn.sigmoid(gate)
    glu = (value * gate_sig).astype(BF16)
    glu_wide = halo(glu, reach).astype(F32)
    conv = jnp.zeros((chans, row_count), F32)
    for tap in range(taps):
        conv = conv + depth_kernel[:, tap : tap + 1] * glu_wide[:, tap : tap + row_count]

    mean = jnp.mean(conv, axis=0, keepdims=True)
    spread = jnp.sum((conv - mean) ** 2, axis=0, keepdims=True)
    if parts == 2:
        there = other(jnp.concatenate([mean, spread]))
        gap = mean - there[:1]
        mean = (mean + there[:1]) * 0.5
        spread = (spread + there[1:] + gap * gap * (chans * 0.5)) / width
    else:
        whole = lax.pmean(mean, "tp")
        spread = lax.psum(spread + chans * (mean - whole) ** 2, "tp") / width
        mean = whole
    inverse_conv = lax.rsqrt(spread + EPS)
    hat_conv = (conv - mean) * inverse_conv
    scaled = hat_conv * conv_gain[:, None]
    swish_sig = jax.nn.sigmoid(scaled)
    act = (scaled * swish_sig).astype(BF16)
    act_all = tp_gather(act)
    block_out = (
        frames_in.astype(F32) + jnp.dot(out_weight, act_all, preferred_element_type=F32)
    ).astype(BF16)
    grad_out = contract_cols(cotangent, act_all) * scale

    d_scaled = d_act * (swish_sig + scaled * swish_sig * (1.0 - swish_sig))
    grad_conv_gain = jnp.sum(d_scaled * hat_conv, axis=1) * scale
    d_conv = norm_back(d_scaled * conv_gain[:, None], hat_conv, inverse_conv, width).astype(BF16)
    d_conv_f = d_conv.astype(F32)
    d_conv_wide = halo(d_conv, reach).astype(F32)
    d_glu = jnp.zeros((chans, row_count), F32)
    kernel_cols = []
    for tap in range(taps):
        start = 2 * reach - tap
        d_glu = d_glu + depth_kernel[:, tap : tap + 1] * d_conv_wide[:, start : start + row_count]
        kernel_cols.append(jnp.sum(glu_wide[:, tap : tap + row_count] * d_conv_f, axis=1))
    grad_kernel = jnp.stack(kernel_cols, axis=0) * scale
    d_value = (d_glu * gate_sig).astype(BF16)
    d_gate = (d_glu * value * gate_sig * (1.0 - gate_sig)).astype(BF16)
    grad_value = contract_cols(d_value, normed_all) * scale
    grad_gate = contract_cols(d_gate, normed_all) * scale
    d_normed = tp_scatter(
        contract_rows(value_weight, d_value) + contract_rows(gate_weight, d_gate)
    )
    hat_in = lax.dynamic_slice_in_dim(hat_all, me * chans, chans, 0)
    grad_norm_gain = jnp.sum(d_normed * hat_in, axis=1) * scale
    input_grad = (
        cotangent.astype(F32) + norm_back(d_normed * norm_gain[:, None], hat_in, inverse_in, width)
    ).astype(BF16)
    small, _ = small_sum(
        jnp.concatenate([grad_kernel, grad_conv_gain[None], grad_norm_gain[None]], axis=0)
    )
    grad_out, grad_value, grad_gate = weight_sums([grad_out, grad_value, grad_gate])
    return (
        block_out,
        input_grad,
        small[taps + 1],
        grad_value,
        grad_gate,
        small[:taps].T,
        small[taps],
        grad_out,
    )


def core_swap(values):
    return lax.ppermute(values, "seq", pairs_of(lax.axis_size("seq"), 1))


def rims(tail, head):
    count = lax.axis_size("seq")
    before = lax.ppermute(tail, "seq", [(i, i + 1) for i in range(count - 1)])
    after = lax.ppermute(head, "seq", [(i + 1, i) for i in range(count - 1)])
    return before, after


def tied(values, *after):
    return lax.optimization_barrier((values, *after))[0]


class Ring:
    def __init__(self, cells, mirrored):
        self.chips, _, ahead, behind = ring_of(lax.axis_size("seq"))
        chip = lax.axis_index("seq") // 2
        self.spot = jnp.where(chip % 2 == 0, chip // 2, self.chips - 1 - chip // 2)
        self.reach = self.chips // 2
        self.ways = (behind, ahead) if mirrored else (ahead, behind)
        self.sign = -1 if mirrored else 1
        self.cells = cells
        self.count = 0
        self.here = ()
        self.extra = None

    def at(self, step):
        return (self.spot + self.sign * step + self.chips) % self.chips

    def part(self, step):
        return lax.dynamic_index_in_dim(self.cells, self.at(step), 0, keepdims=False)

    def put(self, some, step):
        rows = self.cells.shape[1]
        self.cells = lax.dynamic_update_index_in_dim(self.cells, some[:rows], self.at(step), 0)
        if self.extra is not None:
            self.gathered.append(some[rows:])

    def send(self, cells, after):
        if after:
            cells = lax.optimization_barrier((*cells, *after))[: len(cells)]
        self.sent = tuple(cells)
        self.here = tuple(lax.ppermute(x, "seq", way) for x, way in zip(cells, self.ways))

    def hop(self, *after):
        reach = self.reach
        self.count += 1
        left = reach + 1 - self.count
        if left > 0:
            cells = [self.part(left)]
            if left > 1:
                cells.append(self.part(1 - left))
            else:
                self.early = self.here[1]
            if self.count > 1:
                cells = [add(mine, there) for mine, there in zip(cells, self.here)]
            self.send(cells, after)
        else:
            cells = self.here
            if left == 0:
                own = self.part(0).astype(F32) + self.here[0].astype(F32)
                own = (own + self.early.astype(F32)).astype(BF16)
                if self.extra is not None:
                    own = jnp.concatenate([own, self.extra])
                    self.gathered = []
                self.put(own, 0)
                cells = (own, own)
            if left == 1 - reach:
                cells = cells[:1]
            self.send(cells, after)
            for x, step in zip(self.here, (left - 1, 1 - left)):
                self.put(x, step)

    def gather(self, extra):
        self.extra = extra


def fused(
    frames_in, norm_gain, value_weight, gate_weight, depth_kernel, conv_gain, out_weight, cotangent
):
    chans, frames = frames_in.shape
    taps = depth_kernel.shape[1]
    half = chans // 2
    quarter = frames // 4
    count = lax.axis_size("seq")
    chips = count // 2
    scale = float(frames * count) ** (-0.5)
    place = lax.axis_index("seq")
    core = place % 2
    places = jnp.stack([lax.axis_index("tp"), core, place // 2 % 2, place // 4 % 2])
    places = places.astype(jnp.int32)

    gain = norm_gain[None]
    edges = pack_edges(places, frames_in, norm_gain)
    edges_theirs = other(edges)
    middle = frames_in[:, quarter : 3 * quarter]
    middle_theirs = other(middle)
    taps_by = depth_kernel.T
    cot_half = lax.dynamic_slice_in_dim(cotangent, (1 - core) * half, half, 0)

    theirs, d_act_mine = d_act_terms(places, tied(cotangent, cot_half, middle), out_weight)
    cot_theirs = core_swap(cot_half)
    d_act_recv = other(theirs)

    weights = (value_weight, gate_weight)
    *held, edge = glu_forward(places, edges, tied(edges_theirs, theirs, cot_theirs), gain, edges_theirs, weights, ())
    before, after = rims(edge[1], edge[0])
    normed, hat_in, inv_in, glu, sig, slope, _ = glu_forward(
        places,
        middle,
        middle_theirs,
        gain,
        edges_theirs,
        weights,
        tuple(held),
    )
    conv, stats = conv_forward(places, before, glu, after, taps_by)
    normed_theirs = core_swap(normed)
    stats_theirs = other(stats)
    hat_conv, e, sums, gain_grad = act_step(
        places, conv, stats, stats_theirs, d_act_mine, d_act_recv, conv_gain[None]
    )
    sums_theirs = other(sums)
    d_conv, act, head, tail = d_conv_step(
        places, e, hat_conv, conv_gain[None], stats, stats_theirs, sums, sums_theirs
    )
    d_before, d_after = rims(tail, head)
    act_theirs = other(act)
    sent_v, sent_g = d_glu_step(places, d_before, d_conv, d_after, taps_by, sig, slope, False)
    recv_v, recv_g = core_swap(sent_v), core_swap(sent_g)
    own_v, own_g = d_glu_step(
        places, d_before, tied(d_conv, sent_v), d_after, taps_by, sig, slope, True
    )

    grads = pair_grads(
        places, chips, (own_v, own_g), (recv_v, recv_g), normed, normed_theirs, scale
    )
    a = Ring(grads.reshape(chips, -1, 2 * chans), False)
    a.hop()
    act, act_theirs = lax.optimization_barrier((act, act_theirs, grads))[:2]
    acts = [act, act_theirs, core_swap(act), core_swap(act_theirs)]
    grad_out = out_grads(places, cotangent, cot_theirs, acts, scale)
    b = Ring(grad_out.reshape(chips, -1, 2 * chans), True)

    def step(*after):
        there = a.here
        a.hop()
        b.hop(*after, *there)
        return (*a.sent, *b.sent)

    sent = step()
    own_v = tied(own_v, grad_out, *sent)
    theirs, mine = d_normed_terms(
        places, [own_v, sent_v], [own_g, sent_g], value_weight, gate_weight
    )
    recv = other(theirs)
    sent = step(theirs)
    kernel_grad = taps_grad(places, before, glu, after, tied(d_conv, theirs, *sent), scale)
    sent = step(kernel_grad)
    sent = step()
    sums_in, norm_grad = norm_sums(places, mine, tied(recv, kernel_grad, *sent), hat_in, gain)
    sums_in_theirs = other(sums_in)
    small = jnp.concatenate([kernel_grad, gain_grad * scale, norm_grad * scale])
    small = small + core_swap(small)
    depth = (taps + 2 + 15) // 16 * 8
    small = jnp.pad(small, ((0, 2 * depth - taps - 2), (0, 0)))
    b.gather(jnp.concatenate([small[:depth], small[depth:]], axis=1).astype(BF16))
    sent = step()
    sums_in_theirs = tied(sums_in_theirs, *sent)
    input_grad = input_step(
        places, mine, recv, hat_in, gain, inv_in, sums_in, sums_in_theirs, cotangent
    )
    sent = step(input_grad)
    act_theirs = tied(act_theirs, kernel_grad, *sent)
    block_out = out_step(places, frames_in, out_weight, act, act_theirs)
    step(block_out)
    b.hop()
    small = sum(some.astype(F32) for some in b.gathered)
    small = jnp.concatenate([small[:, :chans], small[:, chans:]])

    pair = a.cells.reshape(chips, 2, half // chips, 2 * chans)
    single = b.cells.reshape(chips, 1, half // chips, 2 * chans)
    grad_value, grad_gate, grad_out = join_halves(
        places, pair, core_swap(pair), single, core_swap(single)
    )
    return (
        block_out,
        input_grad,
        small[taps + 1],
        grad_value,
        grad_gate,
        small[:taps].T,
        small[taps],
        grad_out,
    )


def local(*arrays):
    chans, frames = arrays[0].shape
    taps = arrays[4].shape[1]
    count = lax.axis_size("seq")
    fits = lax.axis_size("tp") == 2 and taps == 32 and chans % 256 == 0 and frames % 512 == 0
    fits = fits and count == 16 and chans % (16 * count) == 0
    return (fused if fits else plain)(*arrays)


def solution(mesh):
    return jax.shard_map(
        local,
        mesh=mesh,
        in_specs=(
            P("tp", "seq"),
            P("tp"),
            P("tp", None),
            P("tp", None),
            P("tp", None),
            P("tp"),
            P("tp", None),
            P("tp", "seq"),
        ),
        out_specs=(
            P("tp", "seq"),
            P("tp", "seq"),
            P("tp"),
            P("tp", None),
            P("tp", None),
            P("tp", None),
            P("tp"),
            P("tp", None),
        ),
        check_vma=False,
    )
```

```python
import functools

import jax
import jax.numpy as jnp
from jax import lax
from jax.experimental import pallas as pl
from jax.experimental.pallas import tpu as pltpu
from jax.sharding import PartitionSpec as P

EPS = 1e-05
F32 = jnp.float32
BF16 = jnp.bfloat16
LANES = 128
REAL = ()


def dot(left, right, contract):
    return lax.dot_general(left, right, (contract, ((), ())), preferred_element_type=F32)


NT = ((1,), (1,))
NN = ((1,), (0,))
TN = ((0,), (0,))


def call(body, name, places, grid, ins, outs, args, scratch=(), flops=0, aliases=()):
    real = name in REAL
    size = sum(a.size * a.dtype.itemsize for a in args)
    size += sum(s.size * s.dtype.itemsize for s, _ in outs)
    return pl.pallas_call(
        body,
        out_shape=[s for s, _ in outs],
        grid_spec=pltpu.PrefetchScalarGridSpec(
            num_scalar_prefetch=1,
            grid=grid,
            in_specs=ins,
            out_specs=[b for _, b in outs],
            scratch_shapes=list(scratch),
        ),
        compiler_params=pltpu.CompilerParams(vmem_limit_bytes=24 * 2**20),
        cost_estimate=pl.CostEstimate(
            flops=flops if real else 1000, bytes_accessed=size if real else 1000, transcendentals=0
        ),
        input_output_aliases=dict(aliases),
        name=name,
    )(places, *args)


def shape(dims, kind):
    return jax.ShapeDtypeStruct(dims, kind)


def whole(dims):
    return pl.BlockSpec(dims, lambda i, p: (0,) * len(dims))


def lanes(rows, width):
    return pl.BlockSpec((rows, width), lambda i, p: (0, i))


def rows_of(height, cols):
    return pl.BlockSpec((height, cols), lambda i, p: (i, 0))


def d_act_terms(places, cotangent, weight):
    chans, frames = cotangent.shape

    def body(p, cot, w, theirs, mine, turned):
        @pl.when(pl.program_id(0) == 0)
        def _():
            turned[...] = cot[...].T
            theirs[...] = dot(turned[...], w[...], NN).astype(BF16)

        @pl.when(pl.program_id(0) == 1)
        def _():
            mine[...] = dot(turned[...], w[...], NN).astype(BF16)

    out = (shape((frames, chans), BF16), whole((frames, chans)))
    return call(
        body,
        "d_act_terms",
        places,
        (2,),
        [
            whole((chans, frames)),
            pl.BlockSpec((chans, chans), lambda i, p: (0, jnp.where(i == 0, 1 - p[0], p[0]))),
        ],
        [out, out],
        [cotangent, weight],
        [pltpu.VMEM((frames, chans), BF16)],
        4 * chans * chans * frames,
    )


def edges_first(index, count):
    quarter = count // 4
    inner = jnp.where(index < 2 * quarter, index + 2 * quarter, index - quarter)
    return jnp.where(index < quarter, index, inner)


def pack_edges(places, frames_in, gain):
    chans, frames = frames_in.shape
    quarter = frames // 4

    def body(p, first, last, g, out):
        out[:chans, :quarter] = first[...]
        out[:chans, quarter:] = last[...]
        out[chans:, :] = jnp.zeros_like(out[chans:, :])
        rest = g[...].reshape(1, chans)
        rows = []
        for _ in range(3):
            term = rest.astype(BF16).astype(F32)
            rest = rest - term
            rows += [term[:, at : at + 2 * quarter] for at in range(0, chans, 2 * quarter)]
        rows.append(jnp.zeros((16 - len(rows), 2 * quarter), F32))
        out[chans:, :] = jnp.concatenate(rows).astype(BF16)

    return call(
        body,
        "pack_edges",
        places,
        (1,),
        [
            pl.BlockSpec((chans, quarter), lambda i, p: (0, 0)),
            pl.BlockSpec((chans, quarter), lambda i, p: (0, 3)),
            pl.BlockSpec((chans,), lambda i, p: (0,)),
        ],
        [(shape((chans + 16, 2 * quarter), BF16), whole((chans + 16, 2 * quarter)))],
        [frames_in, frames_in, gain],
    )[0]


def glu_forward(places, mine, theirs, gain, packed, weights, held):
    chans, frames = mine.shape[0] // 16 * 16, mine.shape[1]
    if not held:
        chans = chans - 16
    width = 2 * chans
    step = 256
    half = 1 if held else 0

    def body(p, xm, xt, gm, gt, wv, wg, *refs):
        normed, hat, inv, glu, sig, slope, edge = refs[len(held) :]

        @pl.when(pl.program_id(0) == 0)
        def _():
            low = pl.multiple_of(p[0] * chans, LANES)
            high = pl.multiple_of((1 - p[0]) * chans, LANES)
            terms = gt[...].astype(F32)
            count = chans // frames
            gain_theirs = jnp.concatenate(
                [
                    terms[k : k + 1] + terms[count + k : count + k + 1]
                    + terms[2 * count + k : 2 * count + k + 1]
                    for k in range(count)
                ],
                axis=1,
            )
            for at in range(0, frames, LANES):
                some = pl.ds(at, LANES)
                a = xm[:chans, some].T.astype(F32)
                b = xt[:chans, some].T.astype(F32)
                total = jnp.sum(a, axis=1, keepdims=True) + jnp.sum(b, axis=1, keepdims=True)
                mean = total / width
                a = a - mean
                b = b - mean
                spread = jnp.sum(a * a, axis=1, keepdims=True)
                spread = spread + jnp.sum(b * b, axis=1, keepdims=True)
                scale = lax.rsqrt(spread / width + EPS)
                a = a * scale
                b = b * scale
                hat[some, :] = a
                inv[some, :] = jnp.broadcast_to(scale, (LANES, LANES))
                normed[some, pl.ds(low, chans)] = (a * gm[...]).astype(BF16)
                normed[some, pl.ds(high, chans)] = (b * gain_theirs).astype(BF16)

        value = dot(normed[...], wv[...], NT)
        gate = dot(normed[...], wg[...], NT)
        s = jax.nn.sigmoid(gate)
        g = (value * s).astype(BF16)
        glu[...] = g
        edge[0] = g[:16]
        edge[1] = g[frames - 16 :]
        sig[...] = s
        slope[...] = value * s * (1.0 - s)

    block = pl.BlockSpec((frames, step), lambda i, p: (half, i))

    def full(cols):
        return pl.BlockSpec((frames, cols), lambda i, p: (half, 0))

    return call(
        body,
        "glu_middle" if held else "glu_edges",
        places,
        (chans // step,),
        [whole(mine.shape)] * 2
        + [whole((1, chans)), pl.BlockSpec((16, frames), lambda i, p: (chans // 16, 0))]
        + [rows_of(step, width)] * 2
        + [pl.BlockSpec(memory_space=pl.ANY)] * len(held),
        [
            (shape((2 * frames, width), BF16), full(width)),
            (shape((2 * frames, chans), F32), full(chans)),
            (shape((2 * frames, LANES), F32), full(LANES)),
            (shape((2 * frames, chans), BF16), block),
            (shape((2 * frames, chans), F32), block),
            (shape((2 * frames, chans), F32), block),
            (shape((2, 16, chans), BF16), pl.BlockSpec((2, 16, step), lambda i, p: (0, 0, i))),
        ],
        [mine, theirs, gain, packed, *weights, *held],
        (),
        4 * chans * width * frames,
        [(7 + i, i) for i in range(len(held))],
    )


def fill_edges_first(wide, before, own, after):
    frames = own.shape[0]
    quarter = frames // 4
    wide[:16, :] = before[...].astype(F32)
    wide[16 : 16 + quarter, :] = own[:quarter, :].astype(F32)
    wide[16 + quarter : 16 + 3 * quarter, :] = own[2 * quarter :, :].astype(F32)
    wide[16 + 3 * quarter : 16 + frames, :] = own[quarter : 2 * quarter, :].astype(F32)
    wide[16 + frames :, :] = after[...].astype(F32)


def fill(wide, before, own, after):
    frames = own.shape[0]
    wide[:16, :] = before[...].astype(F32)
    wide[16 : 16 + frames, :] = own[...].astype(F32)
    wide[16 + frames :, :] = after[...].astype(F32)


def to_rows(first, second):
    size = first.shape[0]
    lane = lax.broadcasted_iota(jnp.int32, (size, LANES), 1)
    both = jnp.where(lane == 0, first, jnp.where(lane == 1, second, 0.0))
    return both.T[:8]


def to_cols(rows):
    turned = jnp.concatenate([rows] * (LANES // 8)).T
    return turned[:, 0:1], turned[:, 1:2]


STEP = 128


def conv_forward(places, before, glu, after, taps):
    frames, chans = glu.shape
    blocks = chans // LANES

    def body(p, b, g, a, w, conv, stats, wide):
        at = pl.program_id(0)
        fill_edges_first(wide, b, g, a)

        def chunk(i, carry):
            start = pl.multiple_of(i * STEP, STEP)
            total = jnp.zeros((STEP, LANES), F32)
            for r in range(8):
                x = wide[pl.ds(start + r, STEP + 24), :]
                for q in range(4):
                    tap = 8 * q + r
                    total = total + w[tap : tap + 1, :] * x[8 * q : 8 * q + STEP]
            conv[pl.ds(start, STEP), pl.ds(pl.multiple_of(at * LANES, LANES), LANES)] = total
            return carry

        lax.fori_loop(0, frames // STEP, chunk, 0)

        @pl.when(at == blocks - 1)
        def _():
            for low in range(0, frames, LANES):
                x = conv[low : low + LANES, :]
                mean = jnp.sum(x, axis=1, keepdims=True) / chans
                x = x - mean
                stats[:, low : low + LANES] = to_rows(mean, jnp.sum(x * x, axis=1, keepdims=True))

    return call(
        body,
        "conv_forward",
        places,
        (blocks,),
        [lanes(16, LANES), lanes(frames, LANES), lanes(16, LANES), lanes(32, LANES)],
        [
            (shape((frames, chans), F32), whole((frames, chans))),
            (shape((8, frames), F32), whole((8, frames))),
        ],
        [before, glu, after, taps],
        [pltpu.VMEM((frames + 32, LANES), F32)],
        64 * frames * chans,
    )


def merge(mine, theirs, chans):
    mean, spread = to_cols(mine)
    there, more = to_cols(theirs)
    gap = mean - there
    whole_spread = spread + more + gap * gap * (chans * 0.5)
    return (mean + there) * 0.5, lax.rsqrt(whole_spread / (2 * chans) + EPS)


def act_step(places, conv, mine, theirs, term, recv, gain):
    frames, chans = conv.shape
    height = LANES

    def body(p, x, sm, st, tm, tr, g, hat, e, sums, gain_grad):
        mean, inverse = merge(sm[...], st[...], chans)
        h = (x[...] - mean) * inverse
        hat[...] = h
        scaled = h * g[...]
        s = jax.nn.sigmoid(scaled)
        soft = scaled * s
        d = tm[...].astype(F32) + tr[...].astype(F32)
        d = d * (s + soft * (1.0 - s))

        @pl.when(pl.program_id(0) == 0)
        def _():
            gain_grad[...] = jnp.zeros_like(gain_grad)

        gain_grad[...] += jnp.sum(d * h, axis=0, keepdims=True)
        d = d * g[...]
        e[...] = d
        sums[...] = to_rows(
            jnp.sum(d, axis=1, keepdims=True), jnp.sum(d * h, axis=1, keepdims=True)
        )

    some = rows_of(height, chans)
    line = lanes(8, height)
    return call(
        body,
        "act_step",
        places,
        (frames // height,),
        [some, line, line, some, some, whole((1, chans))],
        [
            (shape((frames, chans), F32), some),
            (shape((frames, chans), F32), some),
            (shape((8, frames), F32), line),
            (shape((1, chans), F32), whole((1, chans))),
        ],
        [conv, mine, theirs, term, recv, gain],
        (),
        30 * frames * chans,
    )


def d_conv_step(places, e, hat, gain, mine, theirs, sums_mine, sums_theirs):
    frames, chans = e.shape
    height = LANES
    steps = frames // height

    def body(p, d, h, g, sm, st, um, ut, out, act, head, tail):
        _, inverse = merge(sm[...], st[...], chans)
        first, second = to_cols(um[...] + ut[...])
        width = 2 * chans
        got = (d[...] - first / width - h[...] * (second / width)) * inverse
        got = got.astype(BF16)
        out[...] = got
        scaled = h[...] * g[...]
        act[...] = (scaled * jax.nn.sigmoid(scaled)).astype(BF16)

        @pl.when(pl.program_id(0) == 0)
        def _():
            head[...] = got[:16]

        @pl.when(pl.program_id(0) == steps - 1)
        def _():
            tail[...] = got[height - 16 :]

    some = rows_of(height, chans)
    line = lanes(8, height)
    rim = (shape((16, chans), BF16), whole((16, chans)))
    return call(
        body,
        "d_conv_step",
        places,
        (steps,),
        [some, some, whole((1, chans)), line, line, line, line],
        [(shape((frames, chans), BF16), some)] * 2 + [rim, rim],
        [e, hat, gain, mine, theirs, sums_mine, sums_theirs],
        (),
        10 * frames * chans,
    )


def d_glu_step(places, before, d_conv, after, taps, sig, slope, own):
    frames, chans = d_conv.shape
    blocks = chans // LANES // 2

    def body(p, b, d, a, w, s, h, d_value, d_gate, wide):
        fill(wide, b, d, a)

        def chunk(i, carry):
            start = pl.multiple_of(i * STEP, STEP)
            total = jnp.zeros((STEP, LANES), F32)
            for r in range(8):
                x = wide[pl.ds(start + r + 1, STEP + 24), :]
                for q in range(4):
                    tap = 31 - (8 * q + r)
                    total = total + w[tap : tap + 1, :] * x[8 * q : 8 * q + STEP]
            quarter = frames // 4
            inner = jnp.where(start < 3 * quarter, start + quarter, start - 2 * quarter)
            there = jnp.where(start < quarter, start, inner)
            some = pl.ds(pl.multiple_of(there, STEP), STEP)
            d_value[some, :] = (total * s[some, :]).astype(BF16)
            d_gate[some, :] = (total * h[some, :]).astype(BF16)
            return carry

        lax.fori_loop(0, frames // STEP, chunk, 0)

    def pick(height):
        if own:
            return pl.BlockSpec((height, LANES), lambda i, p: (0, i + blocks * p[1]))
        return pl.BlockSpec((height, LANES), lambda i, p: (0, i + blocks * (1 - p[1])))

    out = (shape((frames, chans // 2), BF16), lanes(frames, LANES))
    return call(
        body,
        "d_glu_own" if own else "d_glu_other",
        places,
        (blocks,),
        [pick(16), pick(frames), pick(16), pick(32), pick(frames), pick(frames)],
        [out, out],
        [before, d_conv, after, taps, sig, slope],
        [pltpu.VMEM((frames + 32, LANES), F32)],
        32 * frames * chans,
    )


def taps_grad(places, before, glu, after, d_conv, scale):
    frames, chans = glu.shape
    part = 128

    def body(p, b, g, a, d, out, wide, sums):
        fill_edges_first(wide, b, g, a)
        sums[...] = jnp.zeros_like(sums)

        def chunk(i, carry):
            start = pl.multiple_of(i * part, part)
            mine = d[pl.ds(start, part), :].astype(F32)
            for r in range(8):
                x = wide[pl.ds(start + r, part + 24), :]
                for q in range(4):
                    both = mine * x[8 * q : 8 * q + part]
                    sums[8 * q + r] += jnp.sum(both.reshape(part // 8, 8, LANES), axis=0)
            return carry

        lax.fori_loop(0, frames // part, chunk, 0)
        out[...] = jnp.sum(sums[...], axis=1) * scale

    return call(
        body,
        "taps_grad",
        places,
        (chans // LANES,),
        [lanes(16, LANES), lanes(frames, LANES), lanes(16, LANES), lanes(frames, LANES)],
        [(shape((32, chans), F32), lanes(32, LANES))],
        [before, glu, after, d_conv],
        [pltpu.VMEM((frames + 32, LANES), F32), pltpu.VMEM((32, 8, LANES), F32)],
        64 * frames * chans,
    )[0]


def pair_grads(places, chips, mine, theirs, normed, normed_theirs, scale):
    frames, half = mine[0].shape
    width = normed.shape[1]
    step = width // 2

    def body(p, mv, mg, tv, tg, n, nt, out, turned):
        @pl.when(pl.program_id(0) == 0)
        def _():
            for k, (m, t) in enumerate(((mv, tv), (mg, tg))):
                turned[k, :, :frames] = m[...].T
                turned[k, :, frames:] = t[...].T

        for k in range(2):
            total = dot(turned[k, :, :frames], n[...], NN)
            total = total + dot(turned[k, :, frames:], nt[...], NN)
            out[:, k] = (total * scale).astype(BF16).reshape(chips, half // chips, step)

    dims = (chips, 2, half // chips)
    return call(
        body,
        "pair_grads",
        places,
        (width // step,),
        [whole((frames, half))] * 4 + [lanes(frames, step)] * 2,
        [(shape((*dims, width), BF16), pl.BlockSpec((*dims, step), lambda i, p: (0, 0, 0, i)))],
        [*mine, *theirs, normed, normed_theirs],
        [pltpu.VMEM((2, half, 2 * frames), BF16)],
        8 * half * width * frames,
    )[0]


def out_grads(places, cot, cot_theirs, acts, scale):
    chans, frames = cot.shape
    half = chans // 2

    def body(p, c, ct, a, b, a_theirs, b_theirs, out):
        first = pl.program_id(0) == 0
        left = jnp.where(first, a[...], b[...])
        right = jnp.where(first, a_theirs[...], b_theirs[...])
        total = dot(c[...], left, NN) + dot(ct[...], right, NN)
        out[...] = (total * scale).astype(BF16)

    out = (
        shape((half, 2 * chans), BF16),
        pl.BlockSpec((half, chans), lambda i, p: (0, jnp.where(i == 0, p[0], 1 - p[0]))),
    )
    return call(
        body,
        "out_grads",
        places,
        (2,),
        [pl.BlockSpec((half, frames), lambda i, p: (p[1], 0)), whole((half, frames))]
        + [whole((frames, chans))] * 4,
        [out],
        [cot, cot_theirs, *acts],
        (),
        8 * half * chans * frames,
    )[0]


def d_normed_terms(places, values, gates, value_weight, gate_weight):
    frames, half = values[0].shape
    chans = 2 * half

    def body(p, vo, vt, go, gt, wv, wg, theirs, mine):
        own = pl.ds(pl.multiple_of(p[1] * half, LANES), half)
        other = pl.ds(pl.multiple_of((1 - p[1]) * half, LANES), half)
        total = dot(vo[...], wv[own, :], NN) + dot(vt[...], wv[other, :], NN)
        total = total + dot(go[...], wg[own, :], NN) + dot(gt[...], wg[other, :], NN)

        @pl.when(pl.program_id(0) == 0)
        def _():
            theirs[...] = total.astype(BF16)

        @pl.when(pl.program_id(0) == 1)
        def _():
            mine[...] = total.astype(BF16)

    out = (shape((frames, chans), BF16), whole((frames, chans)))
    weight = pl.BlockSpec((chans, chans), lambda i, p: (0, jnp.where(i == 0, 1 - p[0], p[0])))
    return call(
        body,
        "d_normed_terms",
        places,
        (2,),
        [whole((frames, half))] * 4 + [weight] * 2,
        [out, out],
        [*values, *gates, value_weight, gate_weight],
        (),
        8 * chans * chans * frames,
    )


def norm_sums(places, term, recv, hat, gain):
    frames, chans = hat.shape
    height = LANES

    def body(p, tm, tr, h, g, sums, gain_grad):
        d = tm[...].astype(F32) + tr[...].astype(F32)

        @pl.when(pl.program_id(0) == 0)
        def _():
            gain_grad[...] = jnp.zeros_like(gain_grad)

        gain_grad[...] += jnp.sum(d * h[...], axis=0, keepdims=True)
        d = d * g[...]
        sums[...] = to_rows(
            jnp.sum(d, axis=1, keepdims=True), jnp.sum(d * h[...], axis=1, keepdims=True)
        )

    some = rows_of(height, chans)
    return call(
        body,
        "norm_sums",
        places,
        (frames // height,),
        [some, some, some, whole((1, chans))],
        [
            (shape((8, frames), F32), lanes(8, height)),
            (shape((1, chans), F32), whole((1, chans))),
        ],
        [term, recv, hat, gain],
        (),
        10 * frames * chans,
    )


def input_step(places, term, recv, hat, gain, inv, mine, theirs, cot):
    frames, chans = hat.shape
    height = LANES
    width = 2 * chans

    def body(p, tm, tr, h, g, i, um, ut, c, out):
        d = (tm[...].astype(F32) + tr[...].astype(F32)) * g[...]
        first, second = to_cols(um[...] + ut[...])
        got = (d - first / width - h[...] * (second / width)) * i[:, 0:1]
        out[...] = (c[...].astype(F32) + got.T).astype(BF16)

    some = rows_of(height, chans)
    line = lanes(8, height)
    block = pl.BlockSpec((chans, height), lambda i, p: (0, edges_first(i, frames // height)))
    return call(
        body,
        "input_step",
        places,
        (frames // height,),
        [some, some, some, whole((1, chans)), rows_of(height, LANES), line, line, block],
        [(shape((chans, frames), BF16), block)],
        [term, recv, hat, gain, inv, mine, theirs, cot],
        (),
        10 * frames * chans,
    )[0]


def out_step(places, frames_in, weight, act, act_theirs):
    chans, frames = frames_in.shape
    step = 256

    def body(p, x, w, a, b, out):
        own = pl.ds(pl.multiple_of(p[0] * chans, LANES), chans)
        other = pl.ds(pl.multiple_of((1 - p[0]) * chans, LANES), chans)
        total = dot(w[:, own], a[...], NT) + dot(w[:, other], b[...], NT)
        out[...] = (x[...].astype(F32) + total).astype(BF16)

    return call(
        body,
        "out_step",
        places,
        (chans // step,),
        [rows_of(step, frames), rows_of(step, 2 * chans)] + [whole((frames, chans))] * 2,
        [(shape((chans, frames), BF16), rows_of(step, frames))],
        [frames_in, weight, act, act_theirs],
        (),
        4 * chans * chans * frames,
    )[0]


def join_halves(places, pair, pair_theirs, single, single_theirs):
    chips, _, rows, cols = pair.shape

    def body(p, a, at, b, bt, *refs):
        outs, done = refs[:3], refs[3]
        copies = []
        for core, (two, one) in ((p[1], (a, b)), (1 - p[1], (at, bt))):
            for source, out in zip((two.at[:, 0], two.at[:, 1], one.at[:, 0]), outs):
                copies.append(pltpu.make_async_copy(source, out.at[core], done.at[len(copies)]))
        for copy in copies:
            copy.start()
        for copy in copies:
            copy.wait()

    anywhere = pl.BlockSpec(memory_space=pl.ANY)
    outs = call(
        body,
        "join_halves",
        places,
        (1,),
        [anywhere] * 4,
        [(shape((2, chips, rows, cols), BF16), anywhere)] * 3,
        [pair, pair_theirs, single, single_theirs],
        [pltpu.SemaphoreType.DMA((6,))],
    )
    return [out.reshape(2 * chips * rows, cols) for out in outs]


def ring_of(count):
    chips = count // 2
    if chips % 2 == 0:
        cols = chips // 2
        order = [2 * col for col in range(cols)] + [2 * col + 1 for col in reversed(range(cols))]
    else:
        order = list(range(chips))
    place = [0] * count
    ahead, behind = [], []
    for spot, chip in enumerate(order):
        after = order[(spot + 1) % chips]
        for core in range(2):
            place[2 * chip + core] = spot
            ahead.append((2 * chip + core, 2 * after + core))
            behind.append((2 * after + core, 2 * chip + core))
    return chips, place, ahead, behind


def pairs_of(count, step):
    return [(i, i ^ step) for i in range(count)]


def add(left, right):
    return (left.astype(F32) + right.astype(F32)).astype(BF16)


def ring_sum(sets):
    count = lax.axis_size("seq")
    chips, place, ahead, behind = ring_of(count)
    spot = jnp.asarray(place, jnp.int32)[lax.axis_index("seq")]
    reach = chips // 2

    def part(cells, step):
        return lax.dynamic_index_in_dim(cells, (spot + step + chips) % chips, 0, keepdims=False)

    def up(cells):
        return lax.ppermute(cells, "seq", ahead)

    def down(cells):
        return lax.ppermute(cells, "seq", behind)

    half = sets[0].shape[1] // 2
    flows = [(up(part(x, reach)[half:]), down(part(x, -reach)[:half])) for x in sets]
    for hop in range(reach - 1, 0, -1):
        later = []
        for x, (u, d) in zip(sets, flows):
            own_u, own_d = part(x, hop), part(x, -hop)
            if hop == reach - 1:
                u = jnp.concatenate([own_u[:half], add(own_u[half:], u)])
                d = jnp.concatenate([add(own_d[:half], d), own_d[half:]])
            else:
                u, d = add(own_u, u), add(own_d, d)
            later.append((up(u), down(d)))
        flows = later
    owns = [
        (part(x, 0).astype(F32) + u.astype(F32) + d.astype(F32)).astype(BF16)
        for x, (u, d) in zip(sets, flows)
    ]
    outs = []
    for x, own in zip(sets, owns):
        outs.append(lax.dynamic_update_index_in_dim(jnp.zeros_like(x), own, spot, 0))
    flows = [(own, own) for own in owns]
    for hop in range(1, reach):
        flows = [(up(u), down(d)) for u, d in flows]
        for i, (u, d) in enumerate(flows):
            out = lax.dynamic_update_index_in_dim(outs[i], u, (spot - hop + chips) % chips, 0)
            outs[i] = lax.dynamic_update_index_in_dim(out, d, (spot + hop) % chips, 0)
    for i, (u, d) in enumerate(flows):
        far = jnp.concatenate([down(d[:half]), up(u[half:])])
        outs[i] = lax.dynamic_update_index_in_dim(outs[i], far, (spot + reach) % chips, 0)
    return outs


def weight_sums(grads):
    count = lax.axis_size("seq")
    rows, cols = grads[0].shape
    chips = count // 2
    if count % 4 or rows % (2 * chips) or rows // (2 * chips) < 2:
        return [lax.psum(g.astype(BF16), "seq") for g in grads]
    core = lax.axis_index("seq") % 2
    swap = pairs_of(count, 1)
    half = rows // 2
    sets = []
    for g in grads:
        g = g.astype(BF16)
        theirs = lax.dynamic_slice_in_dim(g, (1 - core) * half, half, 0)
        mine = lax.dynamic_slice_in_dim(g, core * half, half, 0)
        mine = add(mine, lax.ppermute(theirs, "seq", swap))
        sets.append(mine.reshape(chips, half // chips, cols))
    outs = []
    for mine in ring_sum(sets):
        mine = mine.reshape(half, cols)
        theirs = lax.ppermute(mine, "seq", swap)
        outs.append(
            jnp.where(
                core == 0,
                jnp.concatenate([mine, theirs]),
                jnp.concatenate([theirs, mine]),
            )
        )
    return outs


def small_sum(values):
    count = lax.axis_size("seq")
    if count & (count - 1):
        return lax.psum(values, "seq"), []
    rests = []
    step = 1
    while step < count:
        values = values + lax.ppermute(values, "seq", pairs_of(count, step))
        rests.append(values)
        step *= 2
    return values, rests


def other(values):
    return lax.ppermute(values, "tp", [(0, 1), (1, 0)])


def tp_sum(values):
    if lax.axis_size("tp") == 2:
        return values + other(values)
    return lax.psum(values, "tp")


def tp_gather(values):
    if lax.axis_size("tp") == 2:
        theirs = other(values)
        first = lax.axis_index("tp") == 0
        return jnp.where(
            first, jnp.concatenate([values, theirs]), jnp.concatenate([theirs, values])
        )
    return lax.all_gather(values, "tp", axis=0, tiled=True)


def tp_scatter(term):
    term = term.astype(BF16)
    if lax.axis_size("tp") == 2:
        rows = term.shape[0] // 2
        me = lax.axis_index("tp")
        theirs = lax.dynamic_slice_in_dim(term, (1 - me) * rows, rows, 0)
        mine = lax.dynamic_slice_in_dim(term, me * rows, rows, 0)
        return mine.astype(F32) + other(theirs).astype(F32)
    return lax.psum_scatter(term, "tp", scatter_dimension=0, tiled=True).astype(F32)


def halo(cells, reach):
    count = lax.axis_size("seq")
    size = cells.shape[1]
    right = [(i, i + 1) for i in range(count - 1)]
    left = [(i + 1, i) for i in range(count - 1)]
    before = lax.ppermute(cells[:, size - reach :], "seq", right)
    after = lax.ppermute(cells[:, :reach], "seq", left)
    return jnp.concatenate([before, cells, after], axis=1)


def norm_back(d_hat, hat, inverse, width):
    sums = jnp.concatenate(
        [jnp.sum(d_hat, axis=0, keepdims=True), jnp.sum(d_hat * hat, axis=0, keepdims=True)]
    )
    sums = tp_sum(sums) / width
    return (d_hat - sums[:1] - hat * sums[1:]) * inverse


def contract_rows(left, right):
    return lax.dot_general(left, right, (((0,), (0,)), ((), ())), preferred_element_type=F32)


def contract_cols(left, right):
    return lax.dot_general(left, right, (((1,), (1,)), ((), ())), preferred_element_type=F32)


def plain(
    frames_in, norm_gain, value_weight, gate_weight, depth_kernel, conv_gain, out_weight, cotangent
):
    chans, row_count = frames_in.shape
    parts = lax.axis_size("tp")
    me = lax.axis_index("tp")
    width = chans * parts
    taps = depth_kernel.shape[1]
    reach = taps // 2
    scale = float(row_count * lax.axis_size("seq")) ** (-0.5)

    frames_all = tp_gather(frames_in)
    gain_all = lax.all_gather(norm_gain, "tp", axis=0, tiled=True)
    d_act = tp_scatter(contract_rows(out_weight, cotangent))

    wide = frames_all.astype(F32)
    centred = wide - jnp.mean(wide, axis=0, keepdims=True)
    inverse_in = lax.rsqrt(jnp.mean(centred * centred, axis=0, keepdims=True) + EPS)
    hat_all = centred * inverse_in
    normed_all = (hat_all * gain_all[:, None]).astype(BF16)
    value = jnp.dot(value_weight, normed_all, preferred_element_type=F32)
    gate = jnp.dot(gate_weight, normed_all, preferred_element_type=F32)
    gate_sig = jax.nn.sigmoid(gate)
    glu = (value * gate_sig).astype(BF16)
    glu_wide = halo(glu, reach).astype(F32)
    conv = jnp.zeros((chans, row_count), F32)
    for tap in range(taps):
        conv = conv + depth_kernel[:, tap : tap + 1] * glu_wide[:, tap : tap + row_count]

    mean = jnp.mean(conv, axis=0, keepdims=True)
    spread = jnp.sum((conv - mean) ** 2, axis=0, keepdims=True)
    if parts == 2:
        there = other(jnp.concatenate([mean, spread]))
        gap = mean - there[:1]
        mean = (mean + there[:1]) * 0.5
        spread = (spread + there[1:] + gap * gap * (chans * 0.5)) / width
    else:
        whole = lax.pmean(mean, "tp")
        spread = lax.psum(spread + chans * (mean - whole) ** 2, "tp") / width
        mean = whole
    inverse_conv = lax.rsqrt(spread + EPS)
    hat_conv = (conv - mean) * inverse_conv
    scaled = hat_conv * conv_gain[:, None]
    swish_sig = jax.nn.sigmoid(scaled)
    act = (scaled * swish_sig).astype(BF16)
    act_all = tp_gather(act)
    block_out = (
        frames_in.astype(F32) + jnp.dot(out_weight, act_all, preferred_element_type=F32)
    ).astype(BF16)
    grad_out = contract_cols(cotangent, act_all) * scale

    d_scaled = d_act * (swish_sig + scaled * swish_sig * (1.0 - swish_sig))
    grad_conv_gain = jnp.sum(d_scaled * hat_conv, axis=1) * scale
    d_conv = norm_back(d_scaled * conv_gain[:, None], hat_conv, inverse_conv, width).astype(BF16)
    d_conv_f = d_conv.astype(F32)
    d_conv_wide = halo(d_conv, reach).astype(F32)
    d_glu = jnp.zeros((chans, row_count), F32)
    kernel_cols = []
    for tap in range(taps):
        start = 2 * reach - tap
        d_glu = d_glu + depth_kernel[:, tap : tap + 1] * d_conv_wide[:, start : start + row_count]
        kernel_cols.append(jnp.sum(glu_wide[:, tap : tap + row_count] * d_conv_f, axis=1))
    grad_kernel = jnp.stack(kernel_cols, axis=0) * scale
    d_value = (d_glu * gate_sig).astype(BF16)
    d_gate = (d_glu * value * gate_sig * (1.0 - gate_sig)).astype(BF16)
    grad_value = contract_cols(d_value, normed_all) * scale
    grad_gate = contract_cols(d_gate, normed_all) * scale
    d_normed = tp_scatter(
        contract_rows(value_weight, d_value) + contract_rows(gate_weight, d_gate)
    )
    hat_in = lax.dynamic_slice_in_dim(hat_all, me * chans, chans, 0)
    grad_norm_gain = jnp.sum(d_normed * hat_in, axis=1) * scale
    input_grad = (
        cotangent.astype(F32) + norm_back(d_normed * norm_gain[:, None], hat_in, inverse_in, width)
    ).astype(BF16)
    small, _ = small_sum(
        jnp.concatenate([grad_kernel, grad_conv_gain[None], grad_norm_gain[None]], axis=0)
    )
    grad_out, grad_value, grad_gate = weight_sums([grad_out, grad_value, grad_gate])
    return (
        block_out,
        input_grad,
        small[taps + 1],
        grad_value,
        grad_gate,
        small[:taps].T,
        small[taps],
        grad_out,
    )


def core_swap(values):
    return lax.ppermute(values, "seq", pairs_of(lax.axis_size("seq"), 1))


def rims(tail, head):
    count = lax.axis_size("seq")
    before = lax.ppermute(tail, "seq", [(i, i + 1) for i in range(count - 1)])
    after = lax.ppermute(head, "seq", [(i + 1, i) for i in range(count - 1)])
    return before, after


def tied(values, *after):
    return lax.optimization_barrier((values, *after))[0]


class Ring:
    def __init__(self, cells, mirrored):
        self.chips, _, ahead, behind = ring_of(lax.axis_size("seq"))
        chip = lax.axis_index("seq") // 2
        self.spot = jnp.where(chip % 2 == 0, chip // 2, self.chips - 1 - chip // 2)
        self.reach = self.chips // 2
        self.ways = (behind, ahead) if mirrored else (ahead, behind)
        self.sign = -1 if mirrored else 1
        self.cells = cells
        self.count = 0
        self.here = ()
        self.extra = None

    def at(self, step):
        return (self.spot + self.sign * step + self.chips) % self.chips

    def part(self, step):
        return lax.dynamic_index_in_dim(self.cells, self.at(step), 0, keepdims=False)

    def put(self, some, step):
        rows = self.cells.shape[1]
        self.cells = lax.dynamic_update_index_in_dim(self.cells, some[:rows], self.at(step), 0)
        if self.extra is not None:
            self.gathered.append(some[rows:])

    def send(self, cells, after):
        if after:
            cells = lax.optimization_barrier((*cells, *after))[: len(cells)]
        self.sent = tuple(cells)
        self.here = tuple(lax.ppermute(x, "seq", way) for x, way in zip(cells, self.ways))

    def hop(self, *after):
        reach = self.reach
        self.count += 1
        left = reach + 1 - self.count
        if left > 0:
            cells = [self.part(left)]
            if left > 1:
                cells.append(self.part(1 - left))
            else:
                self.early = self.here[1]
            if self.count > 1:
                cells = [add(mine, there) for mine, there in zip(cells, self.here)]
            self.send(cells, after)
        else:
            cells = self.here
            if left == 0:
                own = self.part(0).astype(F32) + self.here[0].astype(F32)
                own = (own + self.early.astype(F32)).astype(BF16)
                if self.extra is not None:
                    own = jnp.concatenate([own, self.extra])
                    self.gathered = []
                self.put(own, 0)
                cells = (own, own)
            if left == 1 - reach:
                cells = cells[:1]
            self.send(cells, after)
            for x, step in zip(self.here, (left - 1, 1 - left)):
                self.put(x, step)

    def gather(self, extra):
        self.extra = extra


def fused(
    frames_in, norm_gain, value_weight, gate_weight, depth_kernel, conv_gain, out_weight, cotangent
):
    chans, frames = frames_in.shape
    taps = depth_kernel.shape[1]
    half = chans // 2
    quarter = frames // 4
    count = lax.axis_size("seq")
    chips = count // 2
    scale = float(frames * count) ** (-0.5)
    place = lax.axis_index("seq")
    core = place % 2
    places = jnp.stack([lax.axis_index("tp"), core, place // 2 % 2, place // 4 % 2])
    places = places.astype(jnp.int32)

    gain = norm_gain[None]
    edges = pack_edges(places, frames_in, norm_gain)
    edges_theirs = other(edges)
    middle = frames_in[:, quarter : 3 * quarter]
    middle_theirs = other(middle)
    taps_by = depth_kernel.T
    cot_half = lax.dynamic_slice_in_dim(cotangent, (1 - core) * half, half, 0)

    theirs, d_act_mine = d_act_terms(places, tied(cotangent, cot_half, middle), out_weight)
    cot_theirs = core_swap(cot_half)
    d_act_recv = other(theirs)

    weights = (value_weight, gate_weight)
    *held, edge = glu_forward(places, edges, tied(edges_theirs, theirs, cot_theirs), gain, edges_theirs, weights, ())
    before, after = rims(edge[1], edge[0])
    normed, hat_in, inv_in, glu, sig, slope, _ = glu_forward(
        places,
        middle,
        middle_theirs,
        gain,
        edges_theirs,
        weights,
        tuple(held),
    )
    conv, stats = conv_forward(places, before, glu, after, taps_by)
    normed_theirs = core_swap(normed)
    stats_theirs = other(stats)
    hat_conv, e, sums, gain_grad = act_step(
        places, conv, stats, stats_theirs, d_act_mine, d_act_recv, conv_gain[None]
    )
    sums_theirs = other(sums)
    d_conv, act, head, tail = d_conv_step(
        places, e, hat_conv, conv_gain[None], stats, stats_theirs, sums, sums_theirs
    )
    d_before, d_after = rims(tail, head)
    act_theirs = other(act)
    sent_v, sent_g = d_glu_step(places, d_before, d_conv, d_after, taps_by, sig, slope, False)
    recv_v, recv_g = core_swap(sent_v), core_swap(sent_g)
    own_v, own_g = d_glu_step(
        places, d_before, tied(d_conv, sent_v), d_after, taps_by, sig, slope, True
    )

    grads = pair_grads(
        places, chips, (own_v, own_g), (recv_v, recv_g), normed, normed_theirs, scale
    )
    a = Ring(grads.reshape(chips, -1, 2 * chans), False)
    a.hop()
    act, act_theirs = lax.optimization_barrier((act, act_theirs, grads))[:2]
    acts = [act, act_theirs, core_swap(act), core_swap(act_theirs)]
    grad_out = out_grads(places, cotangent, cot_theirs, acts, scale)
    b = Ring(grad_out.reshape(chips, -1, 2 * chans), True)

    def step(*after):
        there = a.here
        a.hop()
        b.hop(*after, *there)
        return (*a.sent, *b.sent)

    sent = step()
    own_v = tied(own_v, grad_out, *sent)
    theirs, mine = d_normed_terms(
        places, [own_v, sent_v], [own_g, sent_g], value_weight, gate_weight
    )
    recv = other(theirs)
    sent = step(theirs)
    kernel_grad = taps_grad(places, before, glu, after, tied(d_conv, theirs, *sent), scale)
    sent = step(kernel_grad)
    sent = step()
    sums_in, norm_grad = norm_sums(places, mine, tied(recv, kernel_grad, *sent), hat_in, gain)
    sums_in_theirs = other(sums_in)
    small = jnp.concatenate([kernel_grad, gain_grad * scale, norm_grad * scale])
    small = small + core_swap(small)
    depth = (taps + 2 + 15) // 16 * 8
    small = jnp.pad(small, ((0, 2 * depth - taps - 2), (0, 0)))
    b.gather(jnp.concatenate([small[:depth], small[depth:]], axis=1).astype(BF16))
    sent = step()
    sums_in_theirs = tied(sums_in_theirs, *sent)
    input_grad = input_step(
        places, mine, recv, hat_in, gain, inv_in, sums_in, sums_in_theirs, cotangent
    )
    sent = step(input_grad)
    act_theirs = tied(act_theirs, kernel_grad, *sent)
    block_out = out_step(places, frames_in, out_weight, act, act_theirs)
    step(block_out)
    b.hop()
    small = sum(some.astype(F32) for some in b.gathered)
    small = jnp.concatenate([small[:, :chans], small[:, chans:]])

    pair = a.cells.reshape(chips, 2, half // chips, 2 * chans)
    single = b.cells.reshape(chips, 1, half // chips, 2 * chans)
    grad_value, grad_gate, grad_out = join_halves(
        places, pair, core_swap(pair), single, core_swap(single)
    )
    return (
        block_out,
        input_grad,
        small[taps + 1],
        grad_value,
        grad_gate,
        small[:taps].T,
        small[taps],
        grad_out,
    )


def local(*arrays):
    chans, frames = arrays[0].shape
    taps = arrays[4].shape[1]
    count = lax.axis_size("seq")
    fits = lax.axis_size("tp") == 2 and taps == 32 and chans % 256 == 0 and frames % 512 == 0
    fits = fits and count == 16 and chans % (16 * count) == 0
    return (fused if fits else plain)(*arrays)


def solution(mesh):
    return jax.shard_map(
        local,
        mesh=mesh,
        in_specs=(
            P("tp", "seq"),
            P("tp"),
            P("tp", None),
            P("tp", None),
            P("tp", None),
            P("tp"),
            P("tp", None),
            P("tp", "seq"),
        ),
        out_specs=(
            P("tp", "seq"),
            P("tp", "seq"),
            P("tp"),
            P("tp", None),
            P("tp", None),
            P("tp", None),
            P("tp"),
            P("tp", None),
        ),
        check_vma=False,
    )
```
